32 devices in a mesh: dp: 8 (over z, y), fsdp: 4 (over x, core).
Axes of the slice: x: 2, y: 2, z: 4, core: 2. Of those that a mesh axis runs over, the one named last changes fastest.
Arguments:
- tokens: bfloat16 [16384, 1024], P(('dp', 'fsdp')), may hold values from -6 to 6
- cotangent: bfloat16 [16384, 1024], P(('dp', 'fsdp')), may hold values from -6 to 6
- group: int32 [8], P('dp'), may hold values from 0 to 1, as said below
- images: int32 [8, 4], P('dp', 'fsdp'), may hold values from 1 to 10, as said below
- counts: int32 [2], replicated, may hold values from 100 to 999
- ln_gain: bfloat16 [2, 1024], P(None, 'fsdp'), may hold values from 0.19921875 to 1.796875
- ln_bias: bfloat16 [2, 1024], P(None, 'fsdp'), may hold values from -3 to 3
- w_qkv: bfloat16 [1024, 3072], P(None, 'fsdp'), may hold values from -0.25 to 0.25
- qv_bias: bfloat16 [2, 1024], P(None, 'fsdp'), may hold values from -3 to 3
- w_out: bfloat16 [1024, 1024], P(None, 'fsdp'), may hold values from -0.75 to 0.75
- out_bias: bfloat16 [2, 1024], P(None, 'fsdp'), may hold values from -3 to 3
- w_up: bfloat16 [1024, 4096], P(None, 'fsdp'), may hold values from -0.1875 to 0.1875
- up_bias: bfloat16 [4096], P('fsdp'), may hold values from -3 to 3
- w_down: bfloat16 [4096, 1024], P('fsdp'), may hold values from -0.125 to 0.125
Outputs:
- output: bfloat16 [16384, 1024], P(('dp', 'fsdp'))
- grad_tokens: bfloat16 [16384, 1024], P(('dp', 'fsdp'))
- g_ln_gain: float32 [2, 1024], P(None, 'fsdp')
- g_ln_bias: float32 [2, 1024], P(None, 'fsdp')
- g_w_qkv: float32 [1024, 3072], P(None, 'fsdp')
- g_qv_bias: float32 [2, 1024], P(None, 'fsdp')
- g_w_out: float32 [1024, 1024], P(None, 'fsdp')
- g_out_bias: float32 [2, 1024], P(None, 'fsdp')
- g_w_up: float32 [1024, 4096], P(None, 'fsdp')
- g_up_bias: float32 [4096], P('fsdp')
- g_w_down: float32 [4096, 1024], P('fsdp')
The draws below stay inside these ranges and needn't reach their ends.
Inputs may be any that keep to these rules, and one draw needn't show every extreme that they name: `group`: exactly half of the 8 entries are 1. A device of group 0 holds at most 10 images of 50 tokens, one of group 1 at most 3 images of 145 tokens; the devices of fsdp index 0 hold exactly that most.
All inputs are finite; a program needn't handle non-finite values.
Results may differ from the reference program's by a relative error of at most 0.015.
Values may be sent and summed in bfloat16 or wider, within the bound.
A program may use at most 256 MiB of HBM per device.

```python
import jax
import jax.numpy as jnp
from jax import lax

D = 1024
HEADS = 16
HDIM = 64
FF = 4096
LEN0 = 50
LEN1 = 145
TOK_DEV = 512
TOKENS = 16384
N_DP = 8
N_FSDP = 4


def group_pattern(key):
    ordering = jax.random.permutation(key, N_DP)
    return (ordering % 2).astype(jnp.int32)


def draw_group(key, part):
    return group_pattern(key)


def draw_images(key, part):
    pattern = group_pattern(key)
    key = jax.random.fold_in(key, 11)
    fewer_images = jax.random.randint(key, (N_DP, N_FSDP), 0, 3)
    column = jnp.arange(N_FSDP)[None, :]
    fewer_images = jnp.where(column == 0, 0, fewer_images)
    most_images = jnp.where(pattern == 0, TOK_DEV // LEN0, TOK_DEV // LEN1)[:, None]
    return jnp.maximum(most_images - fewer_images, 1).astype(jnp.int32)


def shard_levels(key, extent, cuts, low, top_value):
    loudness, own = 1.0, jax.random.fold_in(key, 6)
    for dim, shards_of in cuts:
        heights = jnp.exp(jax.random.uniform(jax.random.fold_in(own, dim), (shards_of,), jnp.float32, low / len(cuts), top_value / len(cuts)))
        loudness = loudness * jnp.repeat(heights, extent[dim] // shards_of).reshape([-1 if axis == dim else 1 for axis in range(len(extent))])
    return loudness


def bell_draw(stream_key, extent, width, reach, pieces=(), held_as=jnp.bfloat16):
    values = jax.random.normal(stream_key, extent, jnp.float32) * width
    if len(pieces) > 0:
        values = shard_levels(stream_key, extent, pieces, -0.22, 0.18) * values
    return jnp.clip(values, min=-reach, max=reach).astype(held_as)


def setup_inputs(seed: int = 0) -> dict:
    splits = jax.random.split(jax.random.key(seed), 15)
    tokens = bell_draw(splits[0], (TOKENS, D), 1.0, 6.0, ((0, 32),))
    cotangent = bell_draw(splits[1], (TOKENS, D), 1.0, 6.0, ((0, 32),))
    group = draw_group(jax.random.fold_in(splits[14], 71), 0)
    images = draw_images(jax.random.fold_in(splits[14], 71), 0)
    counts = jax.random.randint(splits[4], (2,), 100, 1000).astype(jnp.int32)
    ln_gain = jnp.clip(1.0 + 0.16 * jax.random.normal(splits[5], (2, D), jnp.float32), 0.19921875, 1.796875).astype(jnp.bfloat16)
    ln_bias = bell_draw(splits[6], (2, D), 0.3, 3.0, ((1, 4),))
    w_qkv = bell_draw(splits[7], (D, 3 * D), (D // 2) ** -0.5, 0.25, ((1, 4),))
    qv_bias = bell_draw(splits[8], (2, D), 0.3, 3.0, ((1, 4),))
    w_out = bell_draw(splits[9], (D, D), (D // 16) ** -0.5, 0.75, ((1, 4),))
    out_bias = bell_draw(splits[10], (2, D), 0.3, 3.0, ((1, 4),))
    w_up = bell_draw(splits[11], (D, FF), D ** -0.5, 0.1875, ((1, 4),))
    up_bias = bell_draw(splits[12], (FF,), 0.3, 3.0, ((0, 4),))
    w_down = bell_draw(splits[13], (FF, D), (FF // 2) ** -0.5, 0.125, ((0, 4),))
    return dict(tokens=tokens, cotangent=cotangent, group=group, images=images, counts=counts, ln_gain=ln_gain, ln_bias=ln_bias, w_qkv=w_qkv, qv_bias=qv_bias, w_out=w_out, out_bias=out_bias, w_up=w_up, up_bias=up_bias, w_down=w_down)


@jax.custom_vjp
def low(v):
    return lax.optimization_barrier(v.astype(jnp.bfloat16)).astype(jnp.float32)

@jax.custom_vjp
def low_back(v):
    return v

def low_keep(v):
    return (low(v), None)

def low_pass(kept, grad):
    return (grad,)

def back_keep(v):
    return (v, None)

def back_low(kept, grad):
    return (low(grad),)
low.defvjp(low_keep, low_pass)
low_back.defvjp(back_keep, back_low)
EPSILON = 1e-06
PRECISE = lax.Precision.HIGHEST

def layer_norm(inputs, gain_row, shift_row):
    center = inputs - lax.optimization_barrier(jnp.mean(inputs, axis=-1, keepdims=True))
    spread = lax.optimization_barrier(jnp.mean(center * center, axis=-1, keepdims=True))
    return center * lax.rsqrt(spread + EPSILON) * gain_row + shift_row

def product(first_op, second_op):
    return jnp.dot(first_op, second_op, precision=PRECISE)

def rounded_both(inputs):
    return low(low_back(inputs))

def segment_ids(group_id, image_count):
    length = jnp.where(group_id == 0, LEN0, LEN1).astype(jnp.int32)
    position = jnp.arange(TOK_DEV, dtype=jnp.int32)
    image_index = position // length
    in_image = image_index < image_count
    return (jnp.where(in_image, image_index, TOK_DEV).astype(jnp.int32), in_image)

def forward(params, tokens, segment):
    ln_gain, ln_bias, w_qkv, qv_bias, w_out, out_bias, w_up, up_bias, w_down = params
    row_count = tokens.shape[0]
    normed = low(layer_norm(tokens, ln_gain[0], ln_bias[0]))
    projected = product(normed, w_qkv)
    queries = rounded_both(projected[:, :D] + qv_bias[0]).reshape(row_count, HEADS, HDIM)
    key_rows = rounded_both(projected[:, D:2 * D]).reshape(row_count, HEADS, HDIM)
    values = rounded_both(projected[:, 2 * D:] + qv_bias[1]).reshape(row_count, HEADS, HDIM)
    scores = low_back(jnp.einsum('qhd,khd->hqk', queries, key_rows, precision=PRECISE) * HDIM ** (-0.5))
    allowed = segment[:, None] == segment[None, :]
    scores = jnp.where(allowed[None], scores, -1e+30)
    highest = lax.optimization_barrier(jnp.max(scores, axis=-1, keepdims=True))
    weights = jnp.exp(scores - highest)
    weights = low(weights / lax.optimization_barrier(jnp.sum(weights, axis=-1, keepdims=True)))
    attended = rounded_both(jnp.einsum('hqk,khd->qhd', weights, values, precision=PRECISE).reshape(row_count, D))
    branch = low_back(product(attended, w_out) + out_bias[0])
    middle = tokens + branch
    normed_mlp = low(layer_norm(middle, ln_gain[1], ln_bias[1]))
    hidden_pre = low_back(product(normed_mlp, w_up) + up_bias)
    hidden = low(jax.nn.gelu(hidden_pre, approximate=False))
    result = low_back(product(hidden, w_down) + out_bias[1])
    return middle + result

def reference(tokens, cotangent, group, images, counts, ln_gain, ln_bias, w_qkv, qv_bias, w_out, out_bias, w_up, up_bias, w_down):
    blocks = N_DP * N_FSDP
    params = (ln_gain.astype(jnp.float32), ln_bias.astype(jnp.float32), w_qkv.astype(jnp.float32), qv_bias.astype(jnp.float32), w_out.astype(jnp.float32), out_bias.astype(jnp.float32), w_up.astype(jnp.float32), up_bias.astype(jnp.float32), w_down.astype(jnp.float32))
    inputs = tokens.astype(jnp.float32).reshape(blocks, TOK_DEV, D)
    cot_blocks = cotangent.astype(jnp.float32).reshape(blocks, TOK_DEV, D)
    groups = jnp.repeat(group, N_FSDP).astype(jnp.int32)
    image_counts = images.reshape(blocks).astype(jnp.int32)
    weights_raw = counts.astype(jnp.float32)
    shares = weights_raw / (weights_raw[0] + weights_raw[1]) / (blocks // 2)

    def visit(running, record):
        block_in, block_cot, group_id, image_count = record
        segment, in_image = segment_ids(group_id, image_count)
        result_rows, pullback = jax.vjp(lambda param_set, block_rows: forward(param_set, block_rows, segment), params, block_in)
        grad_params, grad_in = pullback(block_cot * in_image[:, None].astype(jnp.float32))
        factor = jnp.where(group_id == 0, shares[0], shares[1])
        running = jax.tree.map(lambda summed, fresh: summed + factor * fresh, running, grad_params)
        return (running, (result_rows.astype(jnp.bfloat16), grad_in.astype(jnp.bfloat16)))
    empty_sum = jax.tree.map(jnp.zeros_like, params)
    totals, (result_all, grad_all) = lax.scan(visit, empty_sum, (inputs, cot_blocks, groups, image_counts))
    return (result_all.reshape(TOKENS, D), grad_all.reshape(TOKENS, D), totals[0], totals[1], totals[2], totals[3], totals[4], totals[5], totals[6], totals[7], totals[8])
```

```python
import functools

import jax
import jax.numpy as jnp
from jax import lax
from jax.experimental import pallas as pl
from jax.experimental.pallas import tpu as pltpu
from jax.sharding import PartitionSpec as P

D = 1024
HEADS = 16
HDIM = 64
LEN0 = 50
LEN1 = 145
EPSILON = 1e-06
WIDE = 1024
F32 = jnp.float32
BF16 = jnp.bfloat16
MESH = pl.DeviceIdType.MESH


def layer_norm(inputs, gain_row, shift_row):
    center = inputs - jnp.mean(inputs, axis=-1, keepdims=True)
    spread = jnp.mean(center * center, axis=-1, keepdims=True)
    return center * lax.rsqrt(spread + EPSILON) * gain_row + shift_row


def dot_plain(first_op, second_op):
    return jnp.dot(first_op, second_op, preferred_element_type=jnp.float32)


def segment_ids(group_id, image_count, row_count):
    length = jnp.where(group_id == 0, LEN0, LEN1).astype(jnp.int32)
    position = jnp.arange(row_count, dtype=jnp.int32)
    image_index = position // length
    in_image = image_index < image_count
    return (jnp.where(in_image, image_index, row_count), in_image)


def block_scores(query_part, key_rows, segment_part, segment):
    scores = jnp.einsum(
        "qhd,khd->hqk", query_part, key_rows, preferred_element_type=jnp.float32
    ) * HDIM ** (-0.5)
    allowed = segment_part[:, None] == segment[None, :]
    return jnp.where(allowed[None], scores, -1e30)


def split_plan(chunk_rows, bit_count):
    rows, cols, plan = chunk_rows, WIDE, []
    for _ in range(bit_count):
        if rows >= 32:
            rows //= 2
            plan.append(("rows", rows, cols))
        else:
            cols //= 2
            plan.append(("cols", rows, cols))
    return plan


def reduce_scratch(chunk_rows, bit_count):
    plan = split_plan(chunk_rows, bit_count)
    return [
        pltpu.VMEM((2, 2, chunk_rows, WIDE), BF16),
        pltpu.VMEM((2, 2, chunk_rows, WIDE), BF16),
        pltpu.VMEM((4, chunk_rows, WIDE), BF16),
        pltpu.VMEM((4, chunk_rows, WIDE), BF16),
        pltpu.VMEM((16, chunk_rows, WIDE), BF16),
        [pltpu.VMEM((4, r, c), BF16) for _, r, c in plan],
        pltpu.SemaphoreType.DMA((2, 2)),
        pltpu.SemaphoreType.DMA((2, 2)),
        pltpu.SemaphoreType.DMA((2, 4)),
        pltpu.SemaphoreType.DMA((bit_count, 2, 4)),
        pltpu.SemaphoreType.DMA((bit_count, 2, 4)),
    ]


def greet(peers):
    barrier = pltpu.get_barrier_semaphore()
    for peer in peers:
        pl.semaphore_signal(barrier, inc=1, device_id=peer, device_id_type=MESH)
    pl.semaphore_wait(barrier, len(peers))


def reduction(chunk_rows, chunk_count, bit_count, g_ref, out_ref, load, core_in, x_out, x_in, acc, bit_in,
              local_sem, core_sem, x_sem, bit_sem, ag_sem):
    dp, f = lax.axis_index("dp"), lax.axis_index("fsdp")
    core, across = lax.rem(f, 2), f // 2
    plan = split_plan(chunk_rows, bit_count)
    bits = [lax.rem(dp // (1 << b), 2) for b in range(bit_count)]
    flips = [dp + (1 - 2 * bits[b]) * (1 << b) for b in range(bit_count)]
    core_peer = (dp, f + 1 - 2 * core)
    x_peer = (dp, f + 2 - 4 * across)
    peers = [core_peer, x_peer] + [(p, f) for p in flips]

    def region(level, other):
        row, col, rows, cols = 0, 0, chunk_rows, WIDE
        for b in range(level):
            kind, rows, cols = plan[b]
            bit = 1 - bits[b] if other and b == level - 1 else bits[b]
            if kind == "rows":
                row = row + bit * rows
            else:
                col = col + bit * cols
        return row, rows, col, cols

    def cut(ref, lead, base, level, other):
        row, rows, col, cols = region(level, other)
        row_slice = pl.ds(pl.multiple_of(base + row, 16), rows)
        col_slice = slice(None) if cols == WIDE else pl.ds(pl.multiple_of(col, 128), cols)
        return ref.at[lead + (row_slice, col_slice)]

    def rows_of(j):
        return pl.ds(pl.multiple_of(j * chunk_rows, chunk_rows), chunk_rows)

    def remote(src, dst, sems, slot, peer):
        return pltpu.make_async_remote_copy(src, dst, sems.at[0, slot], sems.at[1, slot], device_id=peer,
                                            device_id_type=MESH)

    def load_copy(j):
        return pltpu.make_async_copy(g_ref.at[core, :, rows_of(j), :], load.at[lax.rem(j, 2)],
                                     local_sem.at[0, lax.rem(j, 2)])

    def core_copy(j):
        s = lax.rem(j, 2)
        return remote(g_ref.at[1 - core, :, rows_of(j), :], core_in.at[s], core_sem, s, core_peer)

    def x_copy(j):
        s = lax.rem(j, 4)
        return remote(x_out.at[s], x_in.at[s], x_sem, s, x_peer)

    def bit_copy(b, j):
        s = lax.rem(j, 4)
        return remote(cut(acc, (lax.rem(j, 16),), 0, b + 1, True), bit_in[b].at[s], bit_sem.at[b], s, (flips[b], f))

    def own_copy(j):
        return pltpu.make_async_copy(cut(acc, (lax.rem(j, 16),), 0, bit_count, False),
                                     cut(out_ref, (), j * chunk_rows, bit_count, False),
                                     local_sem.at[1, lax.rem(j, 2)])

    def ag_copy(b, j):
        mine = cut(out_ref, (), j * chunk_rows, b + 1, False)
        src = cut(acc, (lax.rem(j, 16),), 0, bit_count, False) if b == bit_count - 1 else mine
        return remote(src, mine, ag_sem.at[b], lax.rem(j, 4), (flips[b], f))

    skews = [2 if b < 1 else 1 for b in range(bit_count)]
    when_core, when_x = 1, 3
    when_bits, now = [], when_x
    for b in range(bit_count):
        now += skews[b]
        when_bits.append(now)
    when_ag = [0] * bit_count
    for b in reversed(range(bit_count)):
        now += skews[b]
        when_ag[b] = now

    def guarded(t, delay, action):
        j = t - delay

        @pl.when(jnp.logical_and(j >= 0, j < chunk_count))
        def _():
            action(j)

    def on_ag(b):
        def action(j):
            if b == bit_count - 1:
                own_copy(j).wait()
            ag_copy(b, j).wait()
            if b > 0:
                ag_copy(b - 1, j).start()
        return action

    def on_bit(b):
        def action(j):
            bit_copy(b, j).wait()
            mine = cut(acc, (lax.rem(j, 16),), 0, b + 1, False)
            mine[...] = (mine[...].astype(F32) + bit_in[b][lax.rem(j, 4)].astype(F32)).astype(BF16)
            if b + 1 < bit_count:
                bit_copy(b + 1, j).start()
            else:
                ag_copy(b, j).start()
                own_copy(j).start()
        return action

    def on_x(j):
        x_copy(j).wait()
        s = lax.rem(j, 16)
        acc[s] = (acc[s].astype(F32) + x_in[lax.rem(j, 4)].astype(F32)).astype(BF16)
        bit_copy(0, j).start()

    def on_core(j):
        load_copy(j).wait()
        core_copy(j).wait()
        s = lax.rem(j, 2)
        for piece, target in ((1 - across, x_out.at[lax.rem(j, 4)]), (across, acc.at[lax.rem(j, 16)])):
            target[...] = (load[s, piece].astype(F32) + core_in[s, piece].astype(F32)).astype(BF16)
        x_copy(j).start()

    def on_start(j):
        load_copy(j).start()
        core_copy(j).start()

    def tick(t):
        for b in range(bit_count):
            guarded(t, when_ag[b], on_ag(b))
        for b in reversed(range(bit_count)):
            guarded(t, when_bits[b], on_bit(b))
        guarded(t, when_x, on_x)
        guarded(t, when_core, on_core)
        guarded(t, 0, on_start)

    return tick, chunk_count + now, peers


def dot_nn(a, b):
    return lax.dot_general(a, b, (((1,), (0,)), ((), ())), preferred_element_type=F32)


def dot_nt(a, b):
    return lax.dot_general(a, b, (((1,), (1,)), ((), ())), preferred_element_type=F32)


def dot_tn(a, b):
    return lax.dot_general(a, b, (((0,), (0,)), ((), ())), preferred_element_type=F32)


def lanes(index, width):
    return pl.ds(pl.multiple_of(index * width, width), width)


def half_mask(shape, dim, half):
    spot = lax.broadcasted_iota(jnp.int32, shape, dim)
    return spot < HDIM if half == 0 else spot >= HDIM


def backward_kernel(rows, chunk_rows, chunk_count, bit_count, factor_ref, cot_hbm, live_hbm, bias_hbm, z_hbm, slope_hbm, h2_hbm,
                    x1_hbm, o_hbm, qkv_hbm, lse_hbm, h1_hbm, x_hbm, gains_hbm, wd_hbm, wu_hbm, wqkv_hbm, wo_hbm,
                    out_ref, gtok_ref, g_ref,
                    dy, live, bias, h2, x1, o, qkv, lse, h1, x, gains, wqkv, wo,
                    z_tile, slope_tile, wd_tile, wu_tile, stage, du_low,
                    dh, dx1, da, do, dp_all, vecs, upb, tail, load_sem, tile_sem, stage_sem, gtok_sem, comm):
    tick, tick_count, peers = reduction(chunk_rows, chunk_count, bit_count, g_ref, out_ref, *comm)
    proj_tick = min(29, 2048 // chunk_rows - 1)

    def tile_copies(n):
        s, q, f = lax.rem(n, 2), n // 4, lax.rem(n, 4)
        return [
            pltpu.make_async_copy(z_hbm.at[n], z_tile.at[s], tile_sem.at[0, s]),
            pltpu.make_async_copy(slope_hbm.at[n], slope_tile.at[s], tile_sem.at[1, s]),
            pltpu.make_async_copy(wd_hbm.at[f, lanes(q, 256), :], wd_tile.at[s], tile_sem.at[2, s]),
            pltpu.make_async_copy(wu_hbm.at[f, :, lanes(q, 256)], wu_tile.at[s], tile_sem.at[3, s]),
        ]

    whole = [(cot_hbm, dy), (live_hbm, live), (h2_hbm, h2), (x1_hbm, x1), (gains_hbm, gains), (wo_hbm, wo), (bias_hbm, bias),
             (o_hbm, o), (qkv_hbm, qkv), (lse_hbm, lse), (h1_hbm, h1), (wqkv_hbm, wqkv), (x_hbm, x)]

    def whole_copy(i):
        return pltpu.make_async_copy(whole[i][0], whole[i][1], load_sem.at[i])

    for i in range(3):
        whole_copy(i).start()
    for copy in tile_copies(0):
        copy.start()
    for i in range(3, len(whole)):
        whole_copy(i).start()
    greet(peers)
    factor = factor_ref[0]
    for i in range(3):
        whole_copy(i).wait()
    dy[...] = (dy[...].astype(F32) * live[...]).astype(BF16)
    dh[...] = jnp.zeros_like(dh)

    def stage_copy(which, n):
        s, q, f = lax.rem(n, 2), n // 4, lax.rem(n, 4)
        if which == 2:
            row = pl.ds(pl.multiple_of(2048 + q * 256, 256), 256)
        else:
            row = pl.ds(pl.multiple_of(q * 512 + which * 256, 256), 256)
        return pltpu.make_async_copy(stage.at[which, s], g_ref.at[lax.rem(f, 2), f // 2, row, :], stage_sem.at[which, s])

    def ffn(n, carry):
        s = lax.rem(n, 2)

        @pl.when(n + 1 < 16)
        def _():
            for copy in tile_copies(n + 1):
                copy.start()

        for copy in tile_copies(n):
            copy.wait()

        @pl.when(n >= 2)
        def _():
            for which in (0, 1):
                stage_copy(which, n - 2).wait()

        @pl.when(n >= 6)
        def _():
            tick(n - 6)

        stage[0, s] = (dot_tn(z_tile[s], dy[...]) * factor).astype(BF16)
        stage_copy(0, n).start()
        du = dot_nt(dy[...], wd_tile[s]) * slope_tile[s].astype(F32)
        low = du.astype(BF16)
        du_low[...] = low
        upb[n] = jnp.sum(low.astype(F32), axis=0, keepdims=True)
        stage[1, s] = (dot_tn(low, h2[...]) * factor).astype(BF16)
        stage_copy(1, n).start()
        dh[...] += dot_nt(du_low[...], wu_tile[s])
        return carry

    lax.fori_loop(0, 16, ffn, 0)
    for n in (14, 15):
        for which in (0, 1):
            stage_copy(which, n).wait()
    tick(10)

    for i in (3, 4):
        whole_copy(i).wait()
    vecs[...] = jnp.zeros_like(vecs)
    step = 64

    def norm_back(base_ref, which, finish):
        def body(i, carry):
            part = pl.ds(pl.multiple_of(i * step, step), step)
            v = base_ref[part, :].astype(F32)
            center = v - jnp.mean(v, axis=-1, keepdims=True)
            rstd = lax.rsqrt(jnp.mean(center * center, axis=-1, keepdims=True) + EPSILON)
            hat = center * rstd
            grad = dh[part, :]
            vecs[which] += jnp.sum(grad * hat, axis=0, keepdims=True)
            vecs[2 + which] += jnp.sum(grad, axis=0, keepdims=True)
            scaled = grad * gains[which]
            finish(part, rstd * (scaled - jnp.mean(scaled, axis=-1, keepdims=True)
                                 - hat * jnp.mean(scaled * hat, axis=-1, keepdims=True)))
            return carry

        lax.fori_loop(0, rows // step, body, 0)

    def finish_mlp(part, dx):
        dy_part = dy[part, :].astype(F32)
        full = dy_part + dx
        low = full.astype(BF16)
        dx1[part, :] = full
        da[part, :] = low
        vecs[6] += jnp.sum(low.astype(F32), axis=0, keepdims=True)
        vecs[7] += jnp.sum(dy_part, axis=0, keepdims=True)

    norm_back(x1, 1, finish_mlp)
    tick(11)

    whole_copy(5).wait()
    for c in range(4):
        total = jnp.zeros((rows, 256), F32)
        for f in range(4):
            total += dot_nt(da[:, 256 * f : 256 * f + 256], wo[f, 256 * c : 256 * c + 256, :])
        low = total.astype(BF16)
        do[2 * c] = low[:, :128]
        do[2 * c + 1] = low[:, 128:]
    tick(12)
    for i in range(6, 10):
        whole_copy(i).wait()

    def heads(p, carry):
        q_pair, k_pair, v_pair, do_pair = qkv[p], qkv[8 + p], qkv[16 + p], do[p]
        k_turned = k_pair.T
        dk = jnp.zeros((rows, 128), F32)
        dv = jnp.zeros((rows, 128), F32)
        dq = jnp.zeros((128, rows), F32)
        for half in range(2):
            @pl.when(13 + 2 * p + half < proj_tick)
            def _():
                tick(13 + 2 * p + half)

            mask = half_mask((rows, 128), 1, half)
            q_half = jnp.where(mask, q_pair, jnp.zeros_like(q_pair))
            do_half = jnp.where(mask, do_pair, jnp.zeros_like(do_pair))
            k_half = jnp.where(half_mask((128, rows), 0, half), k_turned, jnp.zeros_like(k_turned))
            scores = dot_nt(k_pair, q_half) + bias[...]
            weights = jnp.exp(scores - lse[p, half])
            grad = dot_nt(v_pair, do_half)
            inner = jnp.sum(weights * grad, axis=0, keepdims=True)
            low = weights.astype(BF16)
            ds = (weights * (grad - inner)).astype(BF16)
            dv += dot_nn(low, do_half)
            dk += dot_nn(ds, q_half)
            dq += dot_nn(k_half, ds)
        for i, value in ((0, dq.T * HDIM ** (-0.5)), (1, dk), (2, dv)):
            low = value.astype(BF16)
            dp_all[:, lanes(8 * i + p, 128)] = low
            if i != 1:
                vecs[4 + i // 2, :, lanes(p, 128)] = jnp.sum(low.astype(F32), axis=0, keepdims=True)
        return carry

    lax.fori_loop(0, 8, heads, 0)

    whole_copy(10).wait()

    def proj(n, carry):
        s, q, f = lax.rem(n, 2), n // 4, lax.rem(n, 4)

        @pl.when(n >= 2)
        def _():
            stage_copy(2, n - 2).wait()

        stage[2, s, :, 0:768] = (dot_tn(h1[:, lanes(q, 256)], dp_all[:, lanes(f, 768)]) * factor).astype(BF16)
        stage[2, s, :, 768:1024] = (dot_tn(o[:, lanes(q, 256)], da[:, lanes(f, 256)]) * factor).astype(BF16)
        stage_copy(2, n).start()

        @pl.when(lax.rem(n, 4) == 3)
        def _():
            tick(proj_tick + n // 4)

        return carry

    lax.fori_loop(0, 16, proj, 0)
    for n in (14, 15):
        stage_copy(2, n).wait()

    whole_copy(11).wait()
    whole_copy(12).wait()
    for c in range(4):
        total = jnp.zeros((rows, 256), F32)
        for f in range(4):
            total += dot_nt(dp_all[:, 768 * f : 768 * f + 768], wqkv[f, 256 * c : 256 * c + 256, :])
        dh[:, 256 * c : 256 * c + 256] = total
        tick(proj_tick + 4 + c)

    def finish_attn(part, dx):
        x[part, :] = (dx1[part, :] + dx).astype(BF16)

    norm_back(x, 0, finish_attn)
    gtok_copy = pltpu.make_async_copy(x, gtok_ref, gtok_sem.at[0])
    gtok_copy.start()
    for f in range(4):
        tail[f] = jnp.zeros((chunk_rows, WIDE), BF16)
        for i in range(8):
            tail[f, 2 * i : 2 * i + 1, 0:256] = (vecs[i, :, 256 * f : 256 * f + 256] * factor).astype(BF16)
        for q in range(4):
            tail[f, 16:17, 256 * q : 256 * q + 256] = (upb[4 * q + f] * factor).astype(BF16)
    tail_copies = [pltpu.make_async_copy(tail.at[f], g_ref.at[f % 2, f // 2, pl.ds(3072, chunk_rows), :], gtok_sem.at[1 + f])
                   for f in range(4)]
    for copy in tail_copies:
        copy.start()
    for copy in tail_copies:
        copy.wait()

    def rest(t, carry):
        tick(t)
        return carry

    lax.fori_loop(proj_tick + 8, tick_count, rest, 0)
    gtok_copy.wait()


def backward(factor, cot, live, bias, z, slope, h2, x1, o, qkv, lse, h1, x, gains, wd, wu, wqkv, wo, dp_size):
    rows = cot.shape[0]
    chunk_rows = 64 if dp_size <= 32 else 128
    chunk_count = 3072 // chunk_rows + 1
    bit_count = dp_size.bit_length() - 1
    any_space = pl.BlockSpec(memory_space=pl.ANY)
    like = lambda a: pltpu.VMEM(a.shape, a.dtype)
    scratch = [like(a) for a in (cot, live, bias, h2, x1, o, qkv, lse, h1, x, gains, wqkv, wo)] + [
        pltpu.VMEM((2, rows, 256), BF16),
        pltpu.VMEM((2, rows, 256), BF16),
        pltpu.VMEM((2, 256, D), BF16),
        pltpu.VMEM((2, D, 256), BF16),
        pltpu.VMEM((3, 2, 256, WIDE), BF16),
        pltpu.VMEM((rows, 256), BF16),
        pltpu.VMEM((rows, D), F32),
        pltpu.VMEM((rows, D), F32),
        pltpu.VMEM((rows, D), BF16),
        pltpu.VMEM((8, rows, 128), BF16),
        pltpu.VMEM((rows, 3 * D), BF16),
        pltpu.VMEM((8, 1, D), F32),
        pltpu.VMEM((16, 1, 256), F32),
        pltpu.VMEM((4, chunk_rows, WIDE), BF16),
        pltpu.SemaphoreType.DMA((13,)),
        pltpu.SemaphoreType.DMA((4, 2)),
        pltpu.SemaphoreType.DMA((3, 2)),
        pltpu.SemaphoreType.DMA((5,)),
        reduce_scratch(chunk_rows, bit_count),
    ]
    g_rows = 3072 + chunk_rows
    return pl.pallas_call(
        functools.partial(backward_kernel, rows, chunk_rows, chunk_count, bit_count),
        out_shape=(
            jax.ShapeDtypeStruct((g_rows, WIDE), BF16),
            jax.ShapeDtypeStruct((rows, D), BF16),
            jax.ShapeDtypeStruct((2, 2, g_rows, WIDE), BF16),
        ),
        in_specs=[pl.BlockSpec(memory_space=pltpu.SMEM)] + [any_space] * 17,
        out_specs=(any_space, any_space, any_space),
        scratch_shapes=scratch,
        compiler_params=pltpu.CompilerParams(collective_id=1, has_side_effects=True, vmem_limit_bytes=60 * 2**20),
        name="backward",
    )(factor, cot, live, bias, z, slope, h2, x1, o, qkv, lse, h1, x, gains, wd, wu, wqkv, wo)


def local(
    tokens,
    cotangent,
    group,
    images,
    counts,
    ln_gain,
    ln_bias,
    w_qkv,
    qv_bias,
    w_out,
    out_bias,
    w_up,
    up_bias,
    w_down,
):
    rows = tokens.shape[0]
    group_id = group[0]
    segment, in_image = segment_ids(group_id, images[0, 0], rows)
    gather = lambda a: lax.all_gather(a, "fsdp", axis=0)
    vec = gather(jnp.concatenate([ln_gain, ln_bias, qv_bias, out_bias, up_bias.reshape(4, 256)], axis=0)).astype(F32)
    pick = lambda i: vec[:, i].reshape(D)
    wqkv, wo, wu, wd = gather(w_qkv), gather(w_out), gather(w_up), gather(w_down)
    flat = lambda w: w.transpose(1, 0, 2).reshape(D, -1)
    x = tokens.astype(F32)
    h1 = layer_norm(x, pick(0), pick(2)).astype(BF16)
    projected = dot_plain(h1, flat(wqkv))
    q = (projected[:, :D] + pick(4)).astype(BF16)
    k = projected[:, D : 2 * D].astype(BF16)
    v = (projected[:, 2 * D :] + pick(5)).astype(BF16)
    split = lambda a: a.reshape(rows, HEADS, HDIM)
    scores = block_scores(split(q), split(k), segment, segment)
    highest = jnp.max(scores, axis=-1, keepdims=True)
    weights = jnp.exp(scores - highest)
    totals = jnp.sum(weights, axis=-1, keepdims=True)
    o = jnp.einsum("hqk,khd->qhd", (weights / totals).astype(BF16), split(v), preferred_element_type=F32)
    o = o.reshape(rows, D).astype(BF16)
    lse = (highest + jnp.log(totals))[..., 0]
    x1 = x + dot_plain(o, flat(wo)) + pick(6)
    h2 = layer_norm(x1, pick(1), pick(3)).astype(BF16)
    u = dot_plain(h2, flat(wu)) + vec[:, 8:].reshape(-1)
    gelu, pull = jax.vjp(functools.partial(jax.nn.gelu, approximate=False), u)
    z = gelu.astype(BF16)
    slope = pull(jnp.ones_like(u))[0].astype(BF16)
    output = (x1 + dot_plain(z, wd.reshape(-1, D)) + pick(7)).astype(BF16)
    tile = lambda a: a.reshape(rows, 4, 4, 256).transpose(2, 1, 0, 3).reshape(16, rows, 256)
    qkv = jnp.concatenate([q * HDIM ** (-0.5), k, v], axis=1).astype(BF16).reshape(rows, 24, 128).transpose(1, 0, 2)
    bias = jnp.where(segment[:, None] == segment[None, :], 0.0, -1e30).astype(F32)
    weights_raw = counts.astype(F32)
    shares = weights_raw / (weights_raw[0] + weights_raw[1]) / (lax.axis_size("dp") * lax.axis_size("fsdp") // 2)
    factor = jnp.where(group_id == 0, shares[0], shares[1])
    total, grad_tokens, _ = backward(
        factor.reshape(1), cotangent, in_image[:, None].astype(F32), bias, tile(z), tile(slope), h2, x1, o, qkv,
        lse.reshape(8, 2, 1, rows), h1, tokens, jnp.stack([pick(0), pick(1)])[:, None, :], wd, wu, wqkv, wo,
        lax.axis_size("dp"))
    total = total.astype(F32)
    blocks = total[:2048].reshape(4, 2, 256, D)
    small = total[3072:3089]
    return (
        output, grad_tokens, small[0:4:2, :256], small[4:8:2, :256], total[2048:3072, :768], small[8:12:2, :256],
        total[2048:3072, 768:], small[12:16:2, :256], blocks[:, 1].reshape(D, D).T, small[16], blocks[:, 0].reshape(D, D),
    )


def solution(mesh):
    return jax.shard_map(
        local,
        mesh=mesh,
        in_specs=(
            P(("dp", "fsdp"), None),
            P(("dp", "fsdp"), None),
            P("dp"),
            P("dp", "fsdp"),
            P(),
            P(None, "fsdp"),
            P(None, "fsdp"),
            P(None, "fsdp"),
            P(None, "fsdp"),
            P(None, "fsdp"),
            P(None, "fsdp"),
            P(None, "fsdp"),
            P("fsdp"),
            P("fsdp", None),
        ),
        out_specs=(
            P(("dp", "fsdp"), None),
            P(("dp", "fsdp"), None),
            P(None, "fsdp"),
            P(None, "fsdp"),
            P(None, "fsdp"),
            P(None, "fsdp"),
            P(None, "fsdp"),
            P(None, "fsdp"),
            P(None, "fsdp"),
            P("fsdp"),
            P("fsdp", None),
        ),
        check_vma=False,
    )
```

```python
import functools

import jax
import jax.numpy as jnp
from jax import lax
from jax.experimental import pallas as pl
from jax.experimental.pallas import tpu as pltpu
from jax.sharding import PartitionSpec as P

D = 1024
HEADS = 16
HDIM = 64
LEN0 = 50
LEN1 = 145
EPSILON = 1e-06
WIDE = 1024
F32 = jnp.float32
BF16 = jnp.bfloat16
MESH = pl.DeviceIdType.MESH


def split_plan(chunk_rows, bit_count):
    rows, cols, plan = chunk_rows, WIDE, []
    for _ in range(bit_count):
        if rows >= 32:
            rows //= 2
            plan.append(("rows", rows, cols))
        else:
            cols //= 2
            plan.append(("cols", rows, cols))
    return plan


def reduce_scratch(chunk_rows, bit_count):
    plan = split_plan(chunk_rows, bit_count)
    return [
        pltpu.VMEM((2, 2, chunk_rows, WIDE), BF16),
        pltpu.VMEM((2, 2, chunk_rows, WIDE), BF16),
        pltpu.VMEM((4, chunk_rows, WIDE), BF16),
        pltpu.VMEM((4, chunk_rows, WIDE), BF16),
        pltpu.VMEM((16, chunk_rows, WIDE), BF16),
        [pltpu.VMEM((4, r, c), BF16) for _, r, c in plan],
        pltpu.SemaphoreType.DMA((2, 2)),
        pltpu.SemaphoreType.DMA((2, 2)),
        pltpu.SemaphoreType.DMA((2, 4)),
        pltpu.SemaphoreType.DMA((bit_count, 2, 4)),
        pltpu.SemaphoreType.DMA((bit_count, 2, 4)),
    ]


def greet(peers):
    barrier = pltpu.get_barrier_semaphore()
    for peer in peers:
        pl.semaphore_signal(barrier, inc=1, device_id=peer, device_id_type=MESH)
    pl.semaphore_wait(barrier, len(peers))


def reduction(chunk_rows, chunk_count, bit_count, g_ref, out_ref, load, core_in, x_out, x_in, acc, bit_in,
              local_sem, core_sem, x_sem, bit_sem, ag_sem):
    dp, f = lax.axis_index("dp"), lax.axis_index("fsdp")
    core, across = lax.rem(f, 2), f // 2
    plan = split_plan(chunk_rows, bit_count)
    bits = [lax.rem(dp // (1 << b), 2) for b in range(bit_count)]
    flips = [dp + (1 - 2 * bits[b]) * (1 << b) for b in range(bit_count)]
    core_peer = (dp, f + 1 - 2 * core)
    x_peer = (dp, f + 2 - 4 * across)
    peers = [core_peer, x_peer] + [(p, f) for p in flips]

    def region(level, other):
        row, col, rows, cols = 0, 0, chunk_rows, WIDE
        for b in range(level):
            kind, rows, cols = plan[b]
            bit = 1 - bits[b] if other and b == level - 1 else bits[b]
            if kind == "rows":
                row = row + bit * rows
            else:
                col = col + bit * cols
        return row, rows, col, cols

    def cut(ref, lead, base, level, other):
        row, rows, col, cols = region(level, other)
        row_slice = pl.ds(pl.multiple_of(base + row, 16), rows)
        col_slice = slice(None) if cols == WIDE else pl.ds(pl.multiple_of(col, 128), cols)
        return ref.at[lead + (row_slice, col_slice)]

    def rows_of(j):
        return pl.ds(pl.multiple_of(j * chunk_rows, chunk_rows), chunk_rows)

    def remote(src, dst, sems, slot, peer):
        return pltpu.make_async_remote_copy(src, dst, sems.at[0, slot], sems.at[1, slot], device_id=peer,
                                            device_id_type=MESH)

    def load_copy(j):
        return pltpu.make_async_copy(g_ref.at[core, :, rows_of(j), :], load.at[lax.rem(j, 2)],
                                     local_sem.at[0, lax.rem(j, 2)])

    def core_copy(j):
        s = lax.rem(j, 2)
        return remote(g_ref.at[1 - core, :, rows_of(j), :], core_in.at[s], core_sem, s, core_peer)

    def x_copy(j):
        s = lax.rem(j, 4)
        return remote(x_out.at[s], x_in.at[s], x_sem, s, x_peer)

    def bit_copy(b, j):
        s = lax.rem(j, 4)
        return remote(cut(acc, (lax.rem(j, 16),), 0, b + 1, True), bit_in[b].at[s], bit_sem.at[b], s, (flips[b], f))

    def own_copy(j):
        return pltpu.make_async_copy(cut(acc, (lax.rem(j, 16),), 0, bit_count, False),
                                     cut(out_ref, (), j * chunk_rows, bit_count, False),
                                     local_sem.at[1, lax.rem(j, 2)])

    def ag_copy(b, j):
        mine = cut(out_ref, (), j * chunk_rows, b + 1, False)
        src = cut(acc, (lax.rem(j, 16),), 0, bit_count, False) if b == bit_count - 1 else mine
        return remote(src, mine, ag_sem.at[b], lax.rem(j, 4), (flips[b], f))

    skews = [2 if b < 1 else 1 for b in range(bit_count)]
    when_core, when_x = 1, 3
    when_bits, now = [], when_x
    for b in range(bit_count):
        now += skews[b]
        when_bits.append(now)
    when_ag = [0] * bit_count
    for b in reversed(range(bit_count)):
        now += skews[b]
        when_ag[b] = now

    def guarded(t, delay, action):
        j = t - delay

        @pl.when(jnp.logical_and(j >= 0, j < chunk_count))
        def _():
            action(j)

    def on_ag(b):
        def action(j):
            if b == bit_count - 1:
                own_copy(j).wait()
            ag_copy(b, j).wait()
            if b > 0:
                ag_copy(b - 1, j).start()
        return action

    def on_bit(b):
        def action(j):
            bit_copy(b, j).wait()
            mine = cut(acc, (lax.rem(j, 16),), 0, b + 1, False)
            mine[...] = (mine[...].astype(F32) + bit_in[b][lax.rem(j, 4)].astype(F32)).astype(BF16)
            if b + 1 < bit_count:
                bit_copy(b + 1, j).start()
            else:
                ag_copy(b, j).start()
                own_copy(j).start()
        return action

    def on_x(j):
        x_copy(j).wait()
        s = lax.rem(j, 16)
        acc[s] = (acc[s].astype(F32) + x_in[lax.rem(j, 4)].astype(F32)).astype(BF16)
        bit_copy(0, j).start()

    def on_core(j):
        load_copy(j).wait()
        core_copy(j).wait()
        s = lax.rem(j, 2)
        for piece, target in ((1 - across, x_out.at[lax.rem(j, 4)]), (across, acc.at[lax.rem(j, 16)])):
            target[...] = (load[s, piece].astype(F32) + core_in[s, piece].astype(F32)).astype(BF16)
        x_copy(j).start()

    def on_start(j):
        load_copy(j).start()
        core_copy(j).start()

    def tick(t):
        for b in range(bit_count):
            guarded(t, when_ag[b], on_ag(b))
        for b in reversed(range(bit_count)):
            guarded(t, when_bits[b], on_bit(b))
        guarded(t, when_x, on_x)
        guarded(t, when_core, on_core)
        guarded(t, 0, on_start)

    return tick, chunk_count + now, peers


def dot_nn(a, b):
    return lax.dot_general(a, b, (((1,), (0,)), ((), ())), preferred_element_type=F32)


def dot_nt(a, b):
    return lax.dot_general(a, b, (((1,), (1,)), ((), ())), preferred_element_type=F32)


def dot_tn(a, b):
    return lax.dot_general(a, b, (((0,), (0,)), ((), ())), preferred_element_type=F32)


def lanes(index, width):
    return pl.ds(pl.multiple_of(index * width, width), width)


def half_mask(shape, dim, half):
    spot = lax.broadcasted_iota(jnp.int32, shape, dim)
    return spot < HDIM if half == 0 else spot >= HDIM


def backward_kernel(rows, chunk_rows, chunk_count, bit_count, info_ref, cot_hbm, z_hbm, slope_hbm, h2_hbm,
                    x1_hbm, o_hbm, qkv_hbm, lse_hbm, h1_hbm, x_hbm, vecs_hbm, wd_hbm, wu_hbm, wqkv_hbm, wo_hbm,
                    out_ref, gtok_ref, g_ref,
                    dy, h2, x1, o, qkv, lse, h1, x, gains, wqkv, wo, bias,
                    z_tile, slope_tile, wd_tile, wu_tile, stage, du_low,
                    dh, dx1, da, do, dp_all, vecs, upb, tail, load_sem, tile_sem, stage_sem, gtok_sem, comm):
    tick, tick_count, peers = reduction(chunk_rows, chunk_count, bit_count, g_ref, out_ref, *comm)
    proj_tick = min(29, 2048 // chunk_rows - 1)

    def tile_copies(n):
        s, q, f = lax.rem(n, 2), n // 4, lax.rem(n, 4)
        return [
            pltpu.make_async_copy(z_hbm.at[n], z_tile.at[s], tile_sem.at[0, s]),
            pltpu.make_async_copy(slope_hbm.at[n], slope_tile.at[s], tile_sem.at[1, s]),
            pltpu.make_async_copy(wd_hbm.at[f, lanes(q, 256), :], wd_tile.at[s], tile_sem.at[2, s]),
            pltpu.make_async_copy(wu_hbm.at[f, :, lanes(q, 256)], wu_tile.at[s], tile_sem.at[3, s]),
        ]

    whole = [(cot_hbm, dy), (h2_hbm, h2), (x1_hbm, x1), (vecs_hbm, gains), (wo_hbm, wo), (o_hbm, o), (qkv_hbm, qkv),
             (lse_hbm, lse), (h1_hbm, h1), (wqkv_hbm, wqkv), (x_hbm, x)]

    def whole_copy(i):
        return pltpu.make_async_copy(whole[i][0], whole[i][1], load_sem.at[i])

    for i in range(2):
        whole_copy(i).start()
    for copy in tile_copies(0):
        copy.start()
    for i in range(2, len(whole)):
        whole_copy(i).start()
    greet(peers)
    factor = info_ref[0]
    for i in range(2):
        whole_copy(i).wait()
    live = lax.broadcasted_iota(jnp.int32, (rows, D), 0).astype(F32) < info_ref[2]
    dy[...] = jnp.where(live, dy[...].astype(F32), 0.0).astype(BF16)
    dh[...] = jnp.zeros_like(dh)

    def stage_copy(which, n):
        s, q, f = lax.rem(n, 2), n // 4, lax.rem(n, 4)
        if which == 2:
            row = pl.ds(pl.multiple_of(2048 + q * 256, 256), 256)
        else:
            row = pl.ds(pl.multiple_of(q * 512 + which * 256, 256), 256)
        return pltpu.make_async_copy(stage.at[which, s], g_ref.at[lax.rem(f, 2), f // 2, row, :], stage_sem.at[which, s])

    def ffn(n, carry):
        s = lax.rem(n, 2)

        @pl.when(n + 1 < 16)
        def _():
            for copy in tile_copies(n + 1):
                copy.start()

        for copy in tile_copies(n):
            copy.wait()

        @pl.when(n >= 2)
        def _():
            for which in (0, 1):
                stage_copy(which, n - 2).wait()

        @pl.when(n >= 6)
        def _():
            tick(n - 6)

        stage[0, s] = (dot_tn(z_tile[s], dy[...]) * factor).astype(BF16)
        stage_copy(0, n).start()
        du = dot_nt(dy[...], wd_tile[s]) * slope_tile[s].astype(F32)
        low = du.astype(BF16)
        du_low[...] = low
        upb[n] = jnp.sum(low.astype(F32), axis=0, keepdims=True)
        stage[1, s] = (dot_tn(low, h2[...]) * factor).astype(BF16)
        stage_copy(1, n).start()
        dh[...] += dot_nt(du_low[...], wu_tile[s])
        return carry

    lax.fori_loop(0, 16, ffn, 0)
    for n in (14, 15):
        for which in (0, 1):
            stage_copy(which, n).wait()
    tick(10)

    for i in (2, 3):
        whole_copy(i).wait()
    vecs[...] = jnp.zeros_like(vecs)
    step = 64

    def norm_back(base_ref, which, finish):
        def body(i, carry):
            part = pl.ds(pl.multiple_of(i * step, step), step)
            v = base_ref[part, :].astype(F32)
            center = v - jnp.mean(v, axis=-1, keepdims=True)
            rstd = lax.rsqrt(jnp.mean(center * center, axis=-1, keepdims=True) + EPSILON)
            hat = center * rstd
            grad = dh[part, :]
            vecs[which] += jnp.sum(grad * hat, axis=0, keepdims=True)
            vecs[2 + which] += jnp.sum(grad, axis=0, keepdims=True)
            scaled = grad * gains[which]
            finish(part, rstd * (scaled - jnp.mean(scaled, axis=-1, keepdims=True)
                                 - hat * jnp.mean(scaled * hat, axis=-1, keepdims=True)))
            return carry

        lax.fori_loop(0, rows // step, body, 0)

    def finish_mlp(part, dx):
        dy_part = dy[part, :].astype(F32)
        full = dy_part + dx
        low = full.astype(BF16)
        dx1[part, :] = full
        da[part, :] = low
        vecs[6] += jnp.sum(low.astype(F32), axis=0, keepdims=True)
        vecs[7] += jnp.sum(dy_part, axis=0, keepdims=True)

    norm_back(x1, 1, finish_mlp)
    tick(11)

    whole_copy(4).wait()
    for c in range(4):
        total = jnp.zeros((rows, 256), F32)
        for f in range(4):
            total += dot_nt(da[:, 256 * f : 256 * f + 256], wo[f, 256 * c : 256 * c + 256, :])
        low = total.astype(BF16)
        do[2 * c] = low[:, :128]
        do[2 * c + 1] = low[:, 128:]
    tick(12)
    for i in range(5, 8):
        whole_copy(i).wait()
    fill_bias(bias, info_ref, rows)

    def heads(p, carry):
        q_pair, k_pair, v_pair, do_pair = qkv[p], qkv[8 + p], qkv[16 + p], do[p]
        k_turned = k_pair.T
        dk = jnp.zeros((rows, 128), F32)
        dv = jnp.zeros((rows, 128), F32)
        dq = jnp.zeros((128, rows), F32)
        for half in range(2):
            @pl.when(13 + 2 * p + half < proj_tick)
            def _():
                tick(13 + 2 * p + half)

            mask = half_mask((rows, 128), 1, half)
            q_half = jnp.where(mask, q_pair, jnp.zeros_like(q_pair))
            do_half = jnp.where(mask, do_pair, jnp.zeros_like(do_pair))
            k_half = jnp.where(half_mask((128, rows), 0, half), k_turned, jnp.zeros_like(k_turned))
            scores = dot_nt(k_pair, q_half) + bias[...]
            weights = jnp.exp(scores - lse[p, half])
            grad = dot_nt(v_pair, do_half)
            inner = jnp.sum(weights * grad, axis=0, keepdims=True)
            low = weights.astype(BF16)
            ds = (weights * (grad - inner)).astype(BF16)
            dv += dot_nn(low, do_half)
            dk += dot_nn(ds, q_half)
            dq += dot_nn(k_half, ds)
        for i, value in ((0, dq.T * HDIM ** (-0.5)), (1, dk), (2, dv)):
            low = value.astype(BF16)
            dp_all[:, lanes(8 * i + p, 128)] = low
            if i != 1:
                vecs[4 + i // 2, :, lanes(p, 128)] = jnp.sum(low.astype(F32), axis=0, keepdims=True)
        return carry

    lax.fori_loop(0, 8, heads, 0)

    whole_copy(8).wait()

    def proj(n, carry):
        s, q, f = lax.rem(n, 2), n // 4, lax.rem(n, 4)

        @pl.when(n >= 2)
        def _():
            stage_copy(2, n - 2).wait()

        stage[2, s, :, 0:768] = (dot_tn(h1[:, lanes(q, 256)], dp_all[:, lanes(f, 768)]) * factor).astype(BF16)
        stage[2, s, :, 768:1024] = (dot_tn(o[:, lanes(q, 256)], da[:, lanes(f, 256)]) * factor).astype(BF16)
        stage_copy(2, n).start()

        @pl.when(lax.rem(n, 4) == 3)
        def _():
            tick(proj_tick + n // 4)

        return carry

    lax.fori_loop(0, 16, proj, 0)
    for n in (14, 15):
        stage_copy(2, n).wait()

    whole_copy(9).wait()
    whole_copy(10).wait()
    for c in range(4):
        total = jnp.zeros((rows, 256), F32)
        for f in range(4):
            total += dot_nt(dp_all[:, 768 * f : 768 * f + 768], wqkv[f, 256 * c : 256 * c + 256, :])
        dh[:, 256 * c : 256 * c + 256] = total
        tick(proj_tick + 4 + c)

    def finish_attn(part, dx):
        x[part, :] = (dx1[part, :] + dx).astype(BF16)

    norm_back(x, 0, finish_attn)
    gtok_copy = pltpu.make_async_copy(x, gtok_ref, gtok_sem.at[0])
    gtok_copy.start()
    for f in range(4):
        tail[f] = jnp.zeros((chunk_rows, WIDE), BF16)
        for i in range(8):
            tail[f, 2 * i : 2 * i + 1, 0:256] = (vecs[i, :, 256 * f : 256 * f + 256] * factor).astype(BF16)
        for q in range(4):
            tail[f, 16:17, 256 * q : 256 * q + 256] = (upb[4 * q + f] * factor).astype(BF16)
    tail_copies = [pltpu.make_async_copy(tail.at[f], g_ref.at[f % 2, f // 2, pl.ds(3072, chunk_rows), :], gtok_sem.at[1 + f])
                   for f in range(4)]
    for copy in tail_copies:
        copy.start()
    for copy in tail_copies:
        copy.wait()

    def rest(t, carry):
        tick(t)
        return carry

    lax.fori_loop(proj_tick + 8, tick_count, rest, 0)
    gtok_copy.wait()


def backward(info, cot, z, slope, h2, x1, o, qkv, lse, h1, x, vecs, wd, wu, wqkv, wo, dp_size):
    rows = cot.shape[0]
    chunk_rows = 64 if dp_size <= 32 else 128
    chunk_count = 3072 // chunk_rows + 1
    bit_count = dp_size.bit_length() - 1
    any_space = pl.BlockSpec(memory_space=pl.ANY)
    like = lambda a: pltpu.VMEM(a.shape, a.dtype)
    scratch = [like(a) for a in (cot, h2, x1, o, qkv, lse, h1, x, vecs, wqkv, wo)] + [
        pltpu.VMEM((rows, rows), F32),
        pltpu.VMEM((2, rows, 256), BF16),
        pltpu.VMEM((2, rows, 256), BF16),
        pltpu.VMEM((2, 256, D), BF16),
        pltpu.VMEM((2, D, 256), BF16),
        pltpu.VMEM((3, 2, 256, WIDE), BF16),
        pltpu.VMEM((rows, 256), BF16),
        pltpu.VMEM((rows, D), F32),
        pltpu.VMEM((rows, D), F32),
        pltpu.VMEM((rows, D), BF16),
        pltpu.VMEM((8, rows, 128), BF16),
        pltpu.VMEM((rows, 3 * D), BF16),
        pltpu.VMEM((8, 1, D), F32),
        pltpu.VMEM((16, 1, 256), F32),
        pltpu.VMEM((4, chunk_rows, WIDE), BF16),
        pltpu.SemaphoreType.DMA((11,)),
        pltpu.SemaphoreType.DMA((4, 2)),
        pltpu.SemaphoreType.DMA((3, 2)),
        pltpu.SemaphoreType.DMA((5,)),
        reduce_scratch(chunk_rows, bit_count),
    ]
    g_rows = 3072 + chunk_rows
    return pl.pallas_call(
        functools.partial(backward_kernel, rows, chunk_rows, chunk_count, bit_count),
        out_shape=(
            jax.ShapeDtypeStruct((g_rows, WIDE), BF16),
            jax.ShapeDtypeStruct((rows, D), BF16),
            jax.ShapeDtypeStruct((2, 2, g_rows, WIDE), BF16),
        ),
        in_specs=[pl.BlockSpec(memory_space=pltpu.SMEM)] + [any_space] * 15,
        out_specs=(any_space, any_space, any_space),
        scratch_shapes=scratch,
        compiler_params=pltpu.CompilerParams(collective_id=1, has_side_effects=True, vmem_limit_bytes=60 * 2**20),
        name="backward",
    )(info, cot, z, slope, h2, x1, o, qkv, lse, h1, x, vecs, wd, wu, wqkv, wo)


def fill_bias(bias, info_ref, rows):
    step = 128

    def segments(dim, shape, start):
        place = (lax.broadcasted_iota(jnp.int32, shape, dim) + start).astype(F32)
        return jnp.where(place < info_ref[2], jnp.floor((place + 0.5) * info_ref[1]), float(rows))

    for i in range(rows // step):
        same = segments(0, (step, rows), i * step) == segments(1, (step, rows), 0)
        bias[i * step : (i + 1) * step, :] = jnp.where(same, 0.0, -1e30)


ERF_TOP = (-2.72614225801306e-10, 2.77068142495902e-08, -2.10102402082508e-06, -5.69250639462346e-05,
           -7.34990630326855e-04, -2.95459980854025e-03, -1.60960333262415e-02)
ERF_BOTTOM = (-1.45660718464996e-05, -2.13374055278905e-04, -1.68282697438203e-03, -7.37332916720468e-03,
              -1.42647390514189e-02)


def erf(v):
    v = jnp.clip(v, -4.0, 4.0)
    square = v * v
    top, bottom = ERF_TOP[0], ERF_BOTTOM[0]
    for c in ERF_TOP[1:]:
        top = top * square + c
    for c in ERF_BOTTOM[1:]:
        bottom = bottom * square + c
    return v * top / bottom


PARTS = 3
PART_ROWS = 336
PIECE_ROWS = 112
PIECES = PART_ROWS // PIECE_ROWS
REST = PARTS * PART_ROWS


def forward_kernel(rows, info_ref, tok_hbm, vec_hbm, sqkv, so, su, sd,
                   wqkv, wo, wu, wd, out_hbm, qkv_hbm, lse_hbm, o_hbm, x1_hbm, h1_hbm, h2_hbm, z_hbm, slope_hbm, vecs_hbm,
                   x, h1, qkv, o, x1, h2, y, bias, lse, vec, vecs, qv, upb, wqkv_v, wo_v, wu_t, wd_t, z_t, slope_t, own,
                   own_sem, vec_sem, rest_sem, x_sem, y_sem, z_sem, fx_sem, fy_sem, fz_sem, frest_sem, core_sem,
                   load_sem, tile_sem, save_sem, ztile_sem):
    dp, f = lax.axis_index("dp"), lax.axis_index("fsdp")
    core, across = lax.rem(f, 2), f // 2
    yb, zb = lax.rem(dp, 2), lax.rem(dp // 2, 2)
    core_f, x_f = f + 1 - 2 * core, f + 2 - 4 * across
    diag_f = 3 - f
    core_peer, x_peer, diag_peer = (dp, core_f), (dp, x_f), (dp, diag_f)
    y_peer, z_peer = (dp + 1 - 2 * yb, f), (dp + 2 - 4 * zb, f)
    part_x = yb + (1 - yb) * 2 * zb
    part_y = (1 - yb) + yb * 2 * zb
    part_z = 2 - 2 * zb
    shards, full = (sqkv, so, su, sd), (wqkv, wo, wu, wd)

    def order(i):
        return 2 * lax.rem(across + i // 2, 2) + lax.rem(core + i, 2)

    def remote(src, dst, sems, slot, peer):
        return pltpu.make_async_remote_copy(src, dst, sems.at[0, slot], sems.at[1, slot], device_id=peer,
                                            device_id_type=MESH)

    def part(k, index):
        return pl.ds(pl.multiple_of(index * PART_ROWS + (k % PIECES) * PIECE_ROWS, 16), PIECE_ROWS)

    rest = pl.ds(REST, D - REST)

    def x_copy(k):
        w, at = k // PIECES, part(k, part_x)
        return remote(shards[w].at[at, :], full[w].at[f, at, :], x_sem, k, x_peer)

    def hop(k, index, sems, peer):
        w, at = k // PIECES, part(k, index)
        return remote(full[w].at[x_f, at, :], full[w].at[x_f, at, :], sems, k, peer)

    y_copy = lambda k: hop(k, part_x, y_sem, y_peer)
    z_copy = lambda k: hop(k, 2 * zb, z_sem, z_peer)
    fx_copy = lambda k: hop(k, part_x, fx_sem, core_peer)
    fy_copy = lambda k: hop(k, part_y, fy_sem, core_peer)
    fz_copy = lambda k: hop(k, part_z, fz_sem, core_peer)

    def rest_copy(w):
        return remote(shards[w].at[rest, :], full[w].at[f, rest, :], rest_sem, w, x_peer)

    def frest_copy(w):
        return remote(full[w].at[x_f, rest, :], full[w].at[x_f, rest, :], frest_sem, w, core_peer)

    def core_copy(w):
        return remote(shards[w], full[w].at[f], core_sem, w, core_peer)

    def own_load(w):
        return pltpu.make_async_copy(shards[w], own[w], own_sem.at[0, w])

    def own_copy(w):
        return pltpu.make_async_copy(own[w], full[w].at[f], own_sem.at[1, w])

    count = 4 * PIECES

    def service(k):
        if 0 <= k - 2 < count:
            z_copy(k - 2).wait_recv()
            fz_copy(k - 2).start()
        if 0 <= k - 1 < count:
            y_copy(k - 1).wait_recv()
            fy_copy(k - 1).start()

            @pl.when(yb == 1)
            def _():
                z_copy(k - 1).start()
        if 0 <= k < count:
            x_copy(k).wait_recv()
            y_copy(k).start()

            @pl.when(yb == 0)
            def _():
                z_copy(k).start()

            fx_copy(k).start()
            if k + 3 < count:
                x_copy(k + 3).start()
            if k % PIECES == 0:
                w = k // PIECES
                rest_copy(w).wait_recv()
                frest_copy(w).start()

    def arrived(w):
        frest_copy(w).wait_recv()
        for k in range(w * PIECES, (w + 1) * PIECES):
            fx_copy(k).wait_recv()
            fy_copy(k).wait_recv()
            fz_copy(k).wait_recv()

    load_x = pltpu.make_async_copy(tok_hbm, x, load_sem.at[0])
    load_x.start()
    load_vec = pltpu.make_async_copy(vec_hbm, vec.at[f], load_sem.at[1])
    load_vec.start()
    for w in range(4):
        own_load(w).start()
    greet([core_peer, x_peer, diag_peer, y_peer, z_peer])
    load_vec.wait()
    vec_copies = [remote(vec.at[f], vec.at[f], vec_sem, i, peer)
                  for i, peer in enumerate((core_peer, x_peer, diag_peer))]
    for copy in vec_copies:
        copy.start()
    for k in range(3):
        x_copy(k).start()
    core_copy(0).start()
    for w in range(4):
        rest_copy(w).start()
    for w in range(1, 4):
        core_copy(w).start()
    for w in range(4):
        own_load(w).wait()
        own_copy(w).start()
    fill_bias(bias, info_ref, rows)
    for copy in vec_copies:
        copy.wait()
    qv[...] = jnp.zeros_like(qv)
    for g in range(4):
        wide = vec[g].astype(F32)
        for i in range(8):
            vecs[i, :, 256 * g : 256 * g + 256] = wide[i : i + 1, :]
        for i in range(4):
            upb[4 * g + i] = wide[8 + i : 9 + i, :]
        for i in range(2):
            qv[2 * g + i] = wide[4:5, 128 * i : 128 * i + 128]
            qv[16 + 2 * g + i] = wide[5:6, 128 * i : 128 * i + 128]

    step = 64

    def normalize(value, which):
        center = value - jnp.mean(value, axis=-1, keepdims=True)
        spread = jnp.mean(center * center, axis=-1, keepdims=True)
        return (center * lax.rsqrt(spread + EPSILON) * vecs[which] + vecs[2 + which]).astype(BF16)

    load_x.wait()

    def norm_in(i, carry):
        at = pl.ds(pl.multiple_of(i * step, step), step)
        h1[at, :] = normalize(x[at, :].astype(F32), 0)
        return carry

    lax.fori_loop(0, rows // step, norm_in, 0)
    saves = []

    def save(src, dst):
        copy = pltpu.make_async_copy(src, dst, save_sem.at[len(saves)])
        copy.start()
        saves.append(copy)

    save(h1, h1_hbm)
    save(vecs, vecs_hbm)

    def qkv_load(i):
        return pltpu.make_async_copy(wqkv.at[order(i)], wqkv_v.at[i % 2], load_sem.at[2 + i % 2])

    def project(i):
        qkv_load(i).wait()
        product = dot_nn(h1[...], wqkv_v[i % 2])
        for b in range(6):
            block = 6 * order(i) + b
            scale = jnp.where(block < 8, HDIM ** (-0.5), 1.0).astype(F32)
            qkv[block] = ((product[:, 128 * b : 128 * b + 128] + qv[block]) * scale).astype(BF16)

    own_copy(0).wait()
    qkv_load(0).start()
    core_copy(0).wait_recv()
    qkv_load(1).start()
    project(0)
    service(0)
    project(1)
    for k in range(1, 5):
        service(k)
    qkv_load(2).start()
    arrived(0)
    qkv_load(3).start()
    project(2)
    project(3)
    service(5)
    save(qkv, qkv_hbm)

    def heads(p, carry):
        for i, k in ((0, 6), (2, 7), (4, 8), (7, 9)):
            @pl.when(p == i)
            def _(k=k):
                service(k)

        q_pair, k_pair, v_turned = qkv[p], qkv[8 + p], qkv[16 + p].T
        total = jnp.zeros((128, rows), F32)
        for half in range(2):
            q_half = jnp.where(half_mask((rows, 128), 1, half), q_pair, jnp.zeros_like(q_pair))
            v_half = jnp.where(half_mask((128, rows), 0, half), v_turned, jnp.zeros_like(v_turned))
            scores = dot_nt(k_pair, q_half) + bias[...]
            highest = jnp.max(scores, axis=0, keepdims=True)
            weights = jnp.exp(scores - highest)
            sums = jnp.sum(weights, axis=0, keepdims=True)
            total += dot_nn(v_half, (weights * (1.0 / sums)).astype(BF16))
            lse[p, half] = highest + jnp.log(sums)
        o[:, lanes(p, 128)] = total.T.astype(BF16)
        return carry

    lax.fori_loop(0, 8, heads, 0)
    save(o, o_hbm)
    save(lse, lse_hbm)

    own_copy(1).wait()
    core_copy(1).wait_recv()
    arrived(1)
    wo_load = pltpu.make_async_copy(wo, wo_v, load_sem.at[4])
    wo_load.start()
    own_copy(2).wait()
    own_copy(3).wait()
    for w in (2, 3):
        core_copy(w).wait_recv()

    def tile_of(n):
        return 4 * lax.rem(n, 4) + order(n // 4)

    def tile_loads(n):
        s, q, g = lax.rem(n, 2), lax.rem(n, 4), order(n // 4)
        return [pltpu.make_async_copy(wu.at[g, :, lanes(q, 256)], wu_t.at[s], tile_sem.at[0, s]),
                pltpu.make_async_copy(wd.at[g, lanes(q, 256), :], wd_t.at[s], tile_sem.at[1, s])]

    for copy in tile_loads(0):
        copy.start()
    wo_load.wait()
    for g in range(4):
        at = slice(256 * g, 256 * g + 256)
        x1[:, at] = x[:, at].astype(F32) + dot_nn(o[...], wo_v[g]) + vecs[6, :, at]
    save(x1, x1_hbm)

    def norm_mid(i, carry):
        at = pl.ds(pl.multiple_of(i * step, step), step)
        value = x1[at, :]
        h2[at, :] = normalize(value, 1)
        y[at, :] = value + vecs[7]
        return carry

    lax.fori_loop(0, rows // step, norm_mid, 0)
    save(h2, h2_hbm)

    def tile_saves(n):
        s = lax.rem(n, 2)
        return [pltpu.make_async_copy(z_t.at[s], z_hbm.at[tile_of(n)], ztile_sem.at[0, s]),
                pltpu.make_async_copy(slope_t.at[s], slope_hbm.at[tile_of(n)], ztile_sem.at[1, s])]

    def ffn(n, carry):
        s = lax.rem(n, 2)
        for i, k in ((1, 10), (4, 11), (6, 12), (7, 13)):
            @pl.when(n == i)
            def _(k=k):
                service(k)
                if k == 13:
                    arrived(2)
                    arrived(3)

        @pl.when(n + 1 < 16)
        def _():
            for copy in tile_loads(n + 1):
                copy.start()

        for copy in tile_loads(n):
            copy.wait()

        @pl.when(n >= 2)
        def _():
            for copy in tile_saves(n - 2):
                copy.wait()

        u = dot_nn(h2[...], wu_t[s]) + upb[4 * order(n // 4) + lax.rem(n, 4)]
        bell = 0.5 + 0.5 * erf(u * (0.5 ** 0.5))
        z = (u * bell).astype(BF16)
        z_t[s] = z
        slope_t[s] = (bell + u * (jnp.exp(-0.5 * u * u) * 0.3989422804014327)).astype(BF16)
        for copy in tile_saves(n):
            copy.start()
        y[...] += dot_nn(z, wd_t[s])
        return carry

    lax.fori_loop(0, 16, ffn, 0)
    x[...] = y[...].astype(BF16)
    save(x, out_hbm)
    for n in (14, 15):
        for copy in tile_saves(n):
            copy.wait()
    for copy in saves:
        copy.wait()
    for k in range(count):
        for copy in (x_copy(k), y_copy(k), z_copy(k), fx_copy(k), fy_copy(k), fz_copy(k)):
            copy.wait_send()
    for w in range(4):
        for copy in (rest_copy(w), frest_copy(w), core_copy(w)):
            copy.wait_send()


def forward(info, tokens, vec, w_qkv, w_out, w_up, w_down):
    rows = tokens.shape[0]
    any_space = pl.BlockSpec(memory_space=pl.ANY)
    full = lambda a: jax.ShapeDtypeStruct((4,) + a.shape, a.dtype)
    shape = jax.ShapeDtypeStruct
    count = 4 * PIECES
    sems = lambda *dims: pltpu.SemaphoreType.DMA(dims)
    return pl.pallas_call(
        functools.partial(forward_kernel, rows),
        out_shape=(
            full(w_qkv), full(w_out), full(w_up), full(w_down),
            shape((rows, D), BF16), shape((24, rows, 128), BF16), shape((8, 2, 1, rows), F32), shape((rows, D), BF16),
            shape((rows, D), F32), shape((rows, D), BF16), shape((rows, D), BF16), shape((16, rows, 256), BF16),
            shape((16, rows, 256), BF16), shape((8, 1, D), F32),
        ),
        in_specs=[pl.BlockSpec(memory_space=pltpu.SMEM)] + [any_space] * 6,
        out_specs=(any_space,) * 14,
        scratch_shapes=[
            pltpu.VMEM((rows, D), BF16),
            pltpu.VMEM((rows, D), BF16),
            pltpu.VMEM((24, rows, 128), BF16),
            pltpu.VMEM((rows, D), BF16),
            pltpu.VMEM((rows, D), F32),
            pltpu.VMEM((rows, D), BF16),
            pltpu.VMEM((rows, D), F32),
            pltpu.VMEM((rows, rows), F32),
            pltpu.VMEM((8, 2, 1, rows), F32),
            pltpu.VMEM((4, 16, 256), BF16),
            pltpu.VMEM((8, 1, D), F32),
            pltpu.VMEM((24, 1, 128), F32),
            pltpu.VMEM((16, 1, 256), F32),
            pltpu.VMEM((2,) + w_qkv.shape, BF16),
            pltpu.VMEM((4,) + w_out.shape, BF16),
            pltpu.VMEM((2, D, 256), BF16),
            pltpu.VMEM((2, 256, D), BF16),
            pltpu.VMEM((2, rows, 256), BF16),
            pltpu.VMEM((2, rows, 256), BF16),
            [pltpu.VMEM(a.shape, BF16) for a in (w_qkv, w_out, w_up, w_down)],
            sems(2, 4), sems(2, 3), sems(2, 4),
            sems(2, count), sems(2, count), sems(2, count), sems(2, count), sems(2, count), sems(2, count),
            sems(2, 4), sems(2, 4), sems(5), sems(2, 2), sems(8), sems(2, 2),
        ],
        compiler_params=pltpu.CompilerParams(collective_id=2, has_side_effects=True, vmem_limit_bytes=60 * 2**20),
        name="forward",
    )(info, tokens, vec, w_qkv, w_out, w_up, w_down)


def local(
    tokens,
    cotangent,
    group,
    images,
    counts,
    ln_gain,
    ln_bias,
    w_qkv,
    qv_bias,
    w_out,
    out_bias,
    w_up,
    up_bias,
    w_down,
):
    rows = tokens.shape[0]
    group_id = group[0]
    weights_raw = counts.astype(F32)
    shares = weights_raw / (weights_raw[0] + weights_raw[1]) / (lax.axis_size("dp") * lax.axis_size("fsdp") // 2)
    factor = jnp.where(group_id == 0, shares[0], shares[1])
    length = jnp.where(group_id == 0, LEN0, LEN1)
    info = jnp.stack([factor, 1.0 / length.astype(F32), (images[0, 0] * length).astype(F32)])
    vec = jnp.concatenate(
        [ln_gain, ln_bias, qv_bias, out_bias, up_bias.reshape(4, 256), jnp.zeros((4, 256), BF16)], axis=0)
    wqkv, wo, wu, wd, output, qkv, lse, o, x1, h1, h2, z, slope, vecs = forward(
        info, tokens, vec, w_qkv, w_out, w_up, w_down)
    total, grad_tokens, _ = backward(
        info, cotangent, z, slope, h2, x1, o, qkv, lse, h1, tokens, vecs, wd, wu, wqkv, wo, lax.axis_size("dp"))
    blocks = total[:2048].reshape(4, 2, 256, D)
    small = total[3072:3089].astype(F32)
    return (
        output, grad_tokens, small[0:4:2, :256], small[4:8:2, :256], total[2048:3072, :768].astype(F32), small[8:12:2, :256],
        total[2048:3072, 768:].astype(F32), small[12:16:2, :256], blocks[:, 1].reshape(D, D).T.astype(F32), small[16],
        blocks[:, 0].reshape(D, D).astype(F32),
    )


def solution(mesh):
    return jax.shard_map(
        local,
        mesh=mesh,
        in_specs=(
            P(("dp", "fsdp"), None),
            P(("dp", "fsdp"), None),
            P("dp"),
            P("dp", "fsdp"),
            P(),
            P(None, "fsdp"),
            P(None, "fsdp"),
            P(None, "fsdp"),
            P(None, "fsdp"),
            P(None, "fsdp"),
            P(None, "fsdp"),
            P(None, "fsdp"),
            P("fsdp"),
            P("fsdp", None),
        ),
        out_specs=(
            P(("dp", "fsdp"), None),
            P(("dp", "fsdp"), None),
            P(None, "fsdp"),
            P(None, "fsdp"),
            P(None, "fsdp"),
            P(None, "fsdp"),
            P(None, "fsdp"),
            P(None, "fsdp"),
            P(None, "fsdp"),
            P("fsdp"),
            P("fsdp", None),
        ),
        check_vma=False,
    )
```

```python
import functools

import jax
import jax.numpy as jnp
from jax import lax
from jax.experimental import pallas as pl
from jax.experimental.pallas import tpu as pltpu
from jax.sharding import PartitionSpec as P

D = 1024
HDIM = 64
LEN0 = 50
LEN1 = 145
EPSILON = 1e-06
WIDE = 1024
F32 = jnp.float32
BF16 = jnp.bfloat16
MESH = pl.DeviceIdType.MESH
VMEM_BYTES = 62 * 2**20


def split_plan(chunk_rows, bit_count):
    rows, cols, plan = chunk_rows, WIDE, []
    for _ in range(bit_count):
        if rows >= 32:
            rows //= 2
            plan.append(("rows", rows, cols))
        else:
            cols //= 2
            plan.append(("cols", rows, cols))
    return plan


def pipeline_plan(bit_count):
    lag = 2 if bit_count <= 3 else 1
    order = ["core", "x"] + [("bit", b) for b in range(bit_count)] + [("ag", b) for b in reversed(range(bit_count))]
    skews = {stage: 1 if stage == "core" else lag for stage in order}
    when, now = {}, 0
    for stage in order:
        now += skews[stage]
        when[stage] = now
    return skews, when, now


def reduce_scratch(chunk_rows, bit_count):
    plan = split_plan(chunk_rows, bit_count)
    skews, when, _ = pipeline_plan(bit_count)
    slots = {stage: 2 * skew for stage, skew in skews.items()}
    held = when["ag", bit_count - 1] - when["core"] + 1
    return [
        pltpu.VMEM((slots["core"], 2, chunk_rows, WIDE), BF16),
        pltpu.VMEM((slots["core"], 2, chunk_rows, WIDE), BF16),
        pltpu.VMEM((slots["x"], chunk_rows, WIDE), BF16),
        pltpu.VMEM((slots["x"], chunk_rows, WIDE), BF16),
        pltpu.VMEM((held, chunk_rows, WIDE), BF16),
        [pltpu.VMEM((slots["bit", b], r, c), BF16) for b, (_, r, c) in enumerate(plan)],
        pltpu.SemaphoreType.DMA((2, slots["core"])),
        pltpu.SemaphoreType.DMA((2, slots["core"])),
        pltpu.SemaphoreType.DMA((2, slots["x"])),
        [pltpu.SemaphoreType.DMA((2, slots["bit", b])) for b in range(bit_count)],
        [pltpu.SemaphoreType.DMA((2, slots["ag", b])) for b in range(bit_count)],
    ]


def greet(peers):
    barrier = pltpu.get_barrier_semaphore()
    for peer in peers:
        pl.semaphore_signal(barrier, inc=1, device_id=peer, device_id_type=MESH)
    pl.semaphore_wait(barrier, len(peers))


def reduction(chunk_rows, chunk_count, bit_count, g_ref, out_ref, load, core_in, x_out, x_in, acc, bit_in,
              local_sem, core_sem, x_sem, bit_sem, ag_sem):
    dp, f = lax.axis_index("dp"), lax.axis_index("fsdp")
    core, across = lax.rem(f, 2), f // 2
    plan = split_plan(chunk_rows, bit_count)
    skews, when, depth = pipeline_plan(bit_count)
    slot = lambda stage, j: lax.rem(j, 2 * skews[stage])
    held = lambda j: lax.rem(j, acc.shape[0])
    bits = [lax.rem(dp // (1 << b), 2) for b in range(bit_count)]
    flips = [dp + (1 - 2 * bits[b]) * (1 << b) for b in range(bit_count)]
    core_peer = (dp, f + 1 - 2 * core)
    x_peer = (dp, f + 2 - 4 * across)
    peers = [core_peer, x_peer] + [(p, f) for p in flips]

    def region(level, other):
        row, col, rows, cols = 0, 0, chunk_rows, WIDE
        for b in range(level):
            kind, rows, cols = plan[b]
            bit = 1 - bits[b] if other and b == level - 1 else bits[b]
            if kind == "rows":
                row = row + bit * rows
            else:
                col = col + bit * cols
        return row, rows, col, cols

    def cut(ref, lead, base, level, other):
        row, rows, col, cols = region(level, other)
        row_slice = pl.ds(pl.multiple_of(base + row, 16), rows)
        col_slice = slice(None) if cols == WIDE else pl.ds(pl.multiple_of(col, 128), cols)
        return ref.at[lead + (row_slice, col_slice)]

    def rows_of(j):
        return pl.ds(pl.multiple_of(j * chunk_rows, chunk_rows), chunk_rows)

    def remote(src, dst, sems, slot, peer):
        return pltpu.make_async_remote_copy(src, dst, sems.at[0, slot], sems.at[1, slot], device_id=peer,
                                            device_id_type=MESH)

    def load_copy(j):
        s = slot("core", j)
        return pltpu.make_async_copy(g_ref.at[core, :, rows_of(j), :], load.at[s], local_sem.at[0, s])

    def core_copy(j):
        s = slot("core", j)
        return remote(g_ref.at[1 - core, :, rows_of(j), :], core_in.at[s], core_sem, s, core_peer)

    def x_copy(j):
        s = slot("x", j)
        return remote(x_out.at[s], x_in.at[s], x_sem, s, x_peer)

    def bit_copy(b, j):
        s = slot(("bit", b), j)
        return remote(cut(acc, (held(j),), 0, b + 1, True), bit_in[b].at[s], bit_sem[b], s, (flips[b], f))

    def own_copy(j):
        return pltpu.make_async_copy(cut(acc, (held(j),), 0, bit_count, False),
                                     cut(out_ref, (), j * chunk_rows, bit_count, False),
                                     local_sem.at[1, slot("core", j)])

    def ag_copy(b, j):
        mine = cut(out_ref, (), j * chunk_rows, b + 1, False)
        src = cut(acc, (held(j),), 0, bit_count, False) if b == bit_count - 1 else mine
        return remote(src, mine, ag_sem[b], slot(("ag", b), j), (flips[b], f))

    def guarded(t, delay, action):
        j = t - delay

        @pl.when(jnp.logical_and(j >= 0, j < chunk_count))
        def _():
            action(j)

    def on_ag(b):
        def action(j):
            if b == bit_count - 1:
                own_copy(j).wait()
            ag_copy(b, j).wait()
            if b > 0:
                ag_copy(b - 1, j).start()
        return action

    def on_bit(b):
        def action(j):
            bit_copy(b, j).wait()
            mine = cut(acc, (held(j),), 0, b + 1, False)
            mine[...] = (mine[...].astype(F32) + bit_in[b][slot(("bit", b), j)].astype(F32)).astype(BF16)
            if b + 1 < bit_count:
                bit_copy(b + 1, j).start()
            else:
                ag_copy(b, j).start()
                own_copy(j).start()
        return action

    def on_x(j):
        x_copy(j).wait()
        s = held(j)
        acc[s] = (acc[s].astype(F32) + x_in[slot("x", j)].astype(F32)).astype(BF16)
        bit_copy(0, j).start()

    def on_core(j):
        load_copy(j).wait()
        core_copy(j).wait()
        s = slot("core", j)
        for piece, target in ((1 - across, x_out.at[slot("x", j)]), (across, acc.at[held(j)])):
            target[...] = (load[s, piece].astype(F32) + core_in[s, piece].astype(F32)).astype(BF16)
        x_copy(j).start()

    def on_start(j):
        load_copy(j).start()
        core_copy(j).start()

    def tick(t):
        for b in range(bit_count):
            guarded(t, when["ag", b], on_ag(b))
        for b in reversed(range(bit_count)):
            guarded(t, when["bit", b], on_bit(b))
        guarded(t, when["x"], on_x)
        guarded(t, when["core"], on_core)
        guarded(t, 0, on_start)

    return tick, chunk_count + depth, peers


def dot_nn(a, b):
    return lax.dot_general(a, b, (((1,), (0,)), ((), ())), preferred_element_type=F32)


def dot_nt(a, b):
    return lax.dot_general(a, b, (((1,), (1,)), ((), ())), preferred_element_type=F32)


def lanes(index, width):
    return pl.ds(pl.multiple_of(index * width, width), width)


def half_mask(shape, dim, half):
    spot = lax.broadcasted_iota(jnp.int32, shape, dim)
    return spot < HDIM if half == 0 else spot >= HDIM


def fill_bias(bias, inverse, limit, rows):
    step = 128

    def segments(dim, shape, start):
        place = (lax.broadcasted_iota(jnp.int32, shape, dim) + start).astype(F32)
        return jnp.where(place < limit, jnp.floor((place + 0.5) * inverse), float(rows))

    for i in range(rows // step):
        same = segments(0, (step, rows), i * step) == segments(1, (step, rows), 0)
        bias[i * step : (i + 1) * step, :] = jnp.where(same, 0.0, -1e30)


ERF_TOP = (-2.72614225801306e-10, 2.77068142495902e-08, -2.10102402082508e-06, -5.69250639462346e-05,
           -7.34990630326855e-04, -2.95459980854025e-03, -1.60960333262415e-02)
ERF_BOTTOM = (-1.45660718464996e-05, -2.13374055278905e-04, -1.68282697438203e-03, -7.37332916720468e-03,
              -1.42647390514189e-02)


def erf(v):
    v = jnp.clip(v, -4.0, 4.0)
    square = v * v
    top, bottom = ERF_TOP[0], ERF_BOTTOM[0]
    for c in ERF_TOP[1:]:
        top = top * square + c
    for c in ERF_BOTTOM[1:]:
        bottom = bottom * square + c
    return v * top / bottom


PARTS = 3
PART_ROWS = 336
PIECE_ROWS = 48
PIECES = PART_ROWS // PIECE_ROWS
COUNT = 4 * PIECES
REST = PARTS * PART_ROWS
WINDOW = 4
Y_LAG = Z_LAG = 2


def layer_kernel(rows, chunk_rows, chunk_count, bit_count, share, group_ref, images_ref, counts_ref, tok_hbm, cot_hbm,
                 gain_hbm, shift_hbm, qvb_hbm, outb_hbm, upb_hbm, sqkv, so, su, sd,
                 out_hbm, gtok_hbm, sum_hbm, g_hbm,
                 wqkv, wo, wu, wd, x, h1, qkv, o, x1, h2, z, slope, y, bias, lse, dy, dh, da, stage,
                 smalls, pack, vec, vecs, qv, upb, grads, upg,
                 own_sem, vec_sem, rest_sem, x_sem, y_sem, z_sem, fx_sem, fy_sem, fz_sem, frest_sem, core_sem,
                 load_sem, save_sem, stage_sem, comm):
    tick, tick_count, peers = reduction(chunk_rows, chunk_count, bit_count, g_hbm, sum_hbm, *comm)
    ratio = chunk_rows // 64

    def beat(i):
        if ratio == 1:
            tick(i)
        else:
            @pl.when(lax.rem(i, ratio) == ratio - 1)
            def _():
                tick(i // ratio)

    dp, f = lax.axis_index("dp"), lax.axis_index("fsdp")
    core, across = lax.rem(f, 2), f // 2
    yb, zb = lax.rem(dp, 2), lax.rem(dp // 2, 2)
    core_f, x_f, diag_f = f + 1 - 2 * core, f + 2 - 4 * across, 3 - f
    core_peer, x_peer, diag_peer = (dp, core_f), (dp, x_f), (dp, diag_f)
    y_peer, z_peer = (dp + 1 - 2 * yb, f), (dp + 2 - 4 * zb, f)
    part_x = yb + (1 - yb) * 2 * zb
    part_y = (1 - yb) + yb * 2 * zb
    part_z = 2 - 2 * zb
    shards, full = (sqkv, so, su, sd), (wqkv, wo, wu, wd)

    def order(i):
        return 2 * lax.rem(across + i // 2, 2) + lax.rem(core + i, 2)

    def remote(src, dst, sems, slot, peer):
        return pltpu.make_async_remote_copy(src, dst, sems.at[0, slot], sems.at[1, slot], device_id=peer,
                                            device_id_type=MESH)

    def part(k, index):
        return pl.ds(pl.multiple_of(index * PART_ROWS + (k % PIECES) * PIECE_ROWS, 16), PIECE_ROWS)

    rest = pl.ds(REST, D - REST)

    def x_copy(k):
        w, at = k // PIECES, part(k, part_x)
        return remote(shards[w].at[at, :], full[w].at[f, at, :], x_sem, k, x_peer)

    def hop(k, index, sems, peer):
        w, at = k // PIECES, part(k, index)
        return remote(full[w].at[x_f, at, :], full[w].at[x_f, at, :], sems, k, peer)

    y_copy = lambda k: hop(k, part_x, y_sem, y_peer)
    z_copy = lambda k: hop(k, 2 * zb, z_sem, z_peer)
    fx_copy = lambda k: hop(k, part_x, fx_sem, core_peer)
    fy_copy = lambda k: hop(k, part_y, fy_sem, core_peer)
    fz_copy = lambda k: hop(k, part_z, fz_sem, core_peer)

    def rest_copy(w):
        return remote(shards[w].at[rest, :], full[w].at[f, rest, :], rest_sem, w, x_peer)

    def frest_copy(w):
        return remote(full[w].at[x_f, rest, :], full[w].at[x_f, rest, :], frest_sem, w, core_peer)

    def core_copy(w):
        return remote(shards[w], full[w].at[f], core_sem, w, core_peer)

    def own_copy(w):
        return pltpu.make_async_copy(shards[w], full[w].at[f], own_sem.at[w])

    def service(k):
        i = k - Y_LAG - Z_LAG
        if 0 <= i < COUNT:
            z_copy(i).wait_recv()
            fz_copy(i).start()
        i = k - Y_LAG
        if 0 <= i < COUNT:
            y_copy(i).wait_recv()
            fy_copy(i).start()

            @pl.when(yb == 1)
            def _():
                z_copy(i).start()
        if k < COUNT:
            x_copy(k).wait_recv()
            y_copy(k).start()

            @pl.when(yb == 0)
            def _():
                z_copy(k).start()

            fx_copy(k).start()
            if k + WINDOW < COUNT:
                x_copy(k + WINDOW).start()
            if k % PIECES == 0:
                w = k // PIECES
                rest_copy(w).wait_recv()
                frest_copy(w).start()

    def services(index, plan):
        for i, k in plan:
            @pl.when(index == i)
            def _(k=k):
                service(k)

    def arrived(w):
        frest_copy(w).wait_recv()
        for k in range(w * PIECES, (w + 1) * PIECES):
            fx_copy(k).wait_recv()
            fy_copy(k).wait_recv()
            fz_copy(k).wait_recv()

    loads = [pltpu.make_async_copy(src, dst, load_sem.at[i]) for i, (src, dst) in enumerate(
        [(gain_hbm, smalls[0]), (shift_hbm, smalls[1]), (qvb_hbm, smalls[2]), (outb_hbm, smalls[3]), (upb_hbm, smalls[4]),
         (tok_hbm, x), (cot_hbm, dy)])]
    for copy in loads:
        copy.start()
    for w in range(4):
        own_copy(w).start()
    greet(peers + [diag_peer])
    for k in range(WINDOW):
        x_copy(k).start()
    core_copy(0).start()
    for w in range(4):
        rest_copy(w).start()
    for copy in loads[:5]:
        copy.wait()
    pack[...] = jnp.zeros_like(pack)
    for i in range(4):
        pack[2 * i : 2 * i + 2, :] = smalls[i][...].astype(F32)
    pack[8:12, :] = smalls[4][...].astype(F32)
    vec[f] = pack[...].astype(BF16)
    vec_copies = [remote(vec.at[f], vec.at[f], vec_sem, i, peer)
                  for i, peer in enumerate((core_peer, x_peer, diag_peer))]
    for copy in vec_copies:
        copy.start()
    for w in range(1, 4):
        core_copy(w).start()

    first = group_ref[0] == 0
    length = jnp.where(first, LEN0, LEN1)
    inverse = jnp.where(first, 1.0 / LEN0, 1.0 / LEN1).astype(F32)
    limit = (images_ref[0, 0] * length).astype(F32)
    mine = jnp.where(first, counts_ref[0], counts_ref[1])
    fraction = jnp.full((1, 128), mine, jnp.int32).astype(F32) / jnp.full(
        (1, 128), counts_ref[0] + counts_ref[1], jnp.int32).astype(F32)
    factor = fraction[0:1, 0:1] * share
    fill_bias(bias, inverse, limit, rows)
    for copy in vec_copies:
        copy.wait()
    qv[...] = jnp.zeros_like(qv)
    for g in range(4):
        wide = vec[g].astype(F32)
        for i in range(8):
            vecs[i, :, 256 * g : 256 * g + 256] = wide[i : i + 1, :]
        for i in range(4):
            upb[4 * g + i] = wide[8 + i : 9 + i, :]
        for i in range(2):
            qv[2 * g + i] = wide[4:5, 128 * i : 128 * i + 128]
            qv[16 + 2 * g + i] = wide[5:6, 128 * i : 128 * i + 128]

    step = 64

    def normalize(value, which):
        center = value - jnp.mean(value, axis=-1, keepdims=True)
        spread = jnp.mean(center * center, axis=-1, keepdims=True)
        return (center * lax.rsqrt(spread + EPSILON) * vecs[which] + vecs[2 + which]).astype(BF16)

    loads[5].wait()

    def norm_in(i, carry):
        at = pl.ds(pl.multiple_of(i * step, step), step)
        h1[at, :] = normalize(x[at, :].astype(F32), 0)
        return carry

    lax.fori_loop(0, rows // step, norm_in, 0)

    def project(i):
        product = dot_nn(h1[...], wqkv[order(i)])
        for b in range(6):
            block = 6 * order(i) + b
            scale = jnp.where(block < 8, HDIM ** (-0.5), 1.0).astype(F32)
            qkv[block] = ((product[:, 128 * b : 128 * b + 128] + qv[block]) * scale).astype(BF16)

    own_copy(0).wait()
    project(0)
    service(0)
    core_copy(0).wait_recv()
    service(1)
    project(1)
    for k in range(2, PIECES + Y_LAG + Z_LAG):
        service(k)
    loads[6].wait()
    live = lax.broadcasted_iota(jnp.int32, (rows, D), 0).astype(F32) < limit
    dy[...] = jnp.where(live, dy[...].astype(F32), 0.0).astype(BF16)
    arrived(0)
    project(2)
    for k in range(11, 15):
        service(k)
    project(3)
    for k in range(15, 18):
        service(k)

    def heads(p, carry):
        services(p, ((0, 18), (2, 19), (3, 20), (5, 21), (6, 22)))
        q_pair, k_pair, v_turned = qkv[p], qkv[8 + p], qkv[16 + p].T
        total = jnp.zeros((128, rows), F32)
        for half in range(2):
            q_half = jnp.where(half_mask((rows, 128), 1, half), q_pair, jnp.zeros_like(q_pair))
            v_half = jnp.where(half_mask((128, rows), 0, half), v_turned, jnp.zeros_like(v_turned))
            scores = dot_nt(k_pair, q_half) + bias[...]
            highest = jnp.max(scores, axis=0, keepdims=True)
            weights = jnp.exp(scores - highest)
            sums = jnp.sum(weights, axis=0, keepdims=True)
            total += dot_nn(v_half, (weights * (1.0 / sums)).astype(BF16))
            lse[p, half] = highest + jnp.log(sums)
        o[:, lanes(p, 128)] = total.T.astype(BF16)
        return carry

    lax.fori_loop(0, 8, heads, 0)
    for w in range(1, 4):
        own_copy(w).wait()
        core_copy(w).wait_recv()
    arrived(1)
    for g in range(4):
        at = slice(256 * g, 256 * g + 256)
        x1[:, at] = x[:, at].astype(F32) + dot_nn(o[...], wo[g]) + vecs[6, :, at]
    service(23)

    def norm_mid(i, carry):
        at = pl.ds(pl.multiple_of(i * step, step), step)
        value = x1[at, :]
        h2[at, :] = normalize(value, 1)
        y[at, :] = value + vecs[7]
        return carry

    lax.fori_loop(0, rows // step, norm_mid, 0)
    service(24)

    def hidden(i, carry):
        services(i, ((2, 25), (4, 26), (6, 27)))

        @pl.when(i == 8)
        def _():
            arrived(2)

        q, g = lax.rem(i, 4), order(i // 4)
        n = 4 * q + g
        u = dot_nn(h2[...], wu[g, :, lanes(q, 256)]) + upb[4 * g + q]
        bell = 0.5 + 0.5 * erf(u * (0.5 ** 0.5))
        z[n] = (u * bell).astype(BF16)
        slope[n] = (bell + u * (jnp.exp(-0.5 * u * u) * 0.3989422804014327)).astype(BF16)
        return carry

    lax.fori_loop(0, 16, hidden, 0)

    def stage_copy(which, n):
        s, q, g = lax.rem(n, 2), n // 4, lax.rem(n, 4)
        at = pl.ds(pl.multiple_of(which * D + q * 256, 256), 256)
        return pltpu.make_async_copy(stage.at[s], g_hbm.at[lax.rem(g, 2), g // 2, at, :], stage_sem.at[s])

    def flush(which, n):
        @pl.when(n >= 1)
        def _():
            stage_copy(which, n - 1).wait()

    def down_grad(n, carry):
        services(n, ((1, 28), (4, 29), (8, 30), (12, 31)))
        flush(0, n)
        stage[lax.rem(n, 2)] = (dot_nn(z[n].T, dy[...]) * factor).astype(BF16)
        stage_copy(0, n).start()
        for i in range(4):
            @pl.when(n == 4 + 3 * i)
            def _(i=i):
                beat(i)
        return carry

    lax.fori_loop(0, 16, down_grad, 0)
    stage_copy(0, 15).wait()
    arrived(3)
    dh[...] = jnp.zeros_like(dh)

    def ffn_back(n, carry):
        q, g = n // 4, lax.rem(n, 4)
        flush(1, n)
        beat(4 + n)
        du = dot_nt(dy[...], wd[g, lanes(q, 256), :]) * slope[n].astype(F32)
        low = du.astype(BF16)
        upg[n] = jnp.sum(low.astype(F32), axis=0, keepdims=True)
        stage[lax.rem(n, 2)] = (dot_nn(low.T, h2[...]) * factor).astype(BF16)
        stage_copy(1, n).start()
        dh[...] += dot_nt(low, wu[g, :, lanes(q, 256)])
        y[...] += dot_nn(z[n], wd[g, lanes(q, 256), :])
        return carry

    lax.fori_loop(0, 16, ffn_back, 0)
    stage_copy(1, 15).wait()
    out_copies = []
    for c in range(4):
        slope[c] = y[:, 256 * c : 256 * c + 256].astype(BF16)
        out_copies.append(pltpu.make_async_copy(slope.at[c], out_hbm.at[:, pl.ds(256 * c, 256)], save_sem.at[c]))
        out_copies[-1].start()
    beat(20)
    grads[...] = jnp.zeros_like(grads)

    def norm_back(base_ref, which, first_beat, finish):
        def body(i, carry):
            at = pl.ds(pl.multiple_of(i * step, step), step)
            v = base_ref[at, :].astype(F32)
            center = v - jnp.mean(v, axis=-1, keepdims=True)
            rstd = lax.rsqrt(jnp.mean(center * center, axis=-1, keepdims=True) + EPSILON)
            hat = center * rstd
            grad = dh[at, :]
            grads[which] += jnp.sum(grad * hat, axis=0, keepdims=True)
            grads[2 + which] += jnp.sum(grad, axis=0, keepdims=True)
            scaled = grad * vecs[which]
            finish(at, rstd * (scaled - jnp.mean(scaled, axis=-1, keepdims=True)
                               - hat * jnp.mean(scaled * hat, axis=-1, keepdims=True)))

            @pl.when(i == 4)
            def _():
                beat(first_beat)

            return carry

        lax.fori_loop(0, rows // step, body, 0)

    dx1 = y

    def finish_mlp(at, dx):
        dy_part = dy[at, :].astype(F32)
        total = dy_part + dx
        low = total.astype(BF16)
        dx1[at, :] = total
        da[at, :] = low
        grads[6] += jnp.sum(low.astype(F32), axis=0, keepdims=True)
        grads[7] += jnp.sum(dy_part, axis=0, keepdims=True)

    norm_back(x1, 1, 21, finish_mlp)
    for c in range(4):
        total = jnp.zeros((rows, 256), F32)
        for g in range(4):
            total += dot_nt(da[:, 256 * g : 256 * g + 256], wo[g, 256 * c : 256 * c + 256, :])
        slope[4 + c] = total.astype(BF16)
    beat(22)

    def heads_back(p, carry):
        beat(23 + p)
        at = lanes(lax.rem(p, 2), 128)
        q_pair, k_pair, v_pair, do_pair = qkv[p], qkv[8 + p], qkv[16 + p], slope[4 + p // 2, :, at]
        k_turned = k_pair.T
        dk = jnp.zeros((rows, 128), F32)
        dv = jnp.zeros((rows, 128), F32)
        dq = jnp.zeros((128, rows), F32)
        for half in range(2):
            mask = half_mask((rows, 128), 1, half)
            q_half = jnp.where(mask, q_pair, jnp.zeros_like(q_pair))
            do_half = jnp.where(mask, do_pair, jnp.zeros_like(do_pair))
            k_half = jnp.where(half_mask((128, rows), 0, half), k_turned, jnp.zeros_like(k_turned))
            scores = dot_nt(k_pair, q_half) + bias[...]
            weights = jnp.exp(scores - lse[p, half])
            grad = dot_nt(v_pair, do_half)
            inner = jnp.sum(weights * grad, axis=0, keepdims=True)
            low = weights.astype(BF16)
            ds = (weights * (grad - inner)).astype(BF16)
            dv += dot_nn(low, do_half)
            dk += dot_nn(ds, q_half)
            dq += dot_nn(k_half, ds)
        for i, value in ((0, dq.T * HDIM ** (-0.5)), (1, dk), (2, dv)):
            low = value.astype(BF16)
            z[4 * i + p // 2, :, at] = low
            if i != 1:
                grads[4 + i // 2, :, lanes(p, 128)] = jnp.sum(low.astype(F32), axis=0, keepdims=True)
        return carry

    lax.fori_loop(0, 8, heads_back, 0)

    def proj_grad(n, carry):
        s, q, g = lax.rem(n, 2), n // 4, lax.rem(n, 4)
        flush(2, n)
        left = h1[:, lanes(q, 256)].T
        for b in range(3):
            stage[s, :, 256 * b : 256 * b + 256] = (dot_nn(left, z[3 * g + b]) * factor).astype(BF16)
        stage[s, :, 768:1024] = (dot_nn(o[:, lanes(q, 256)].T, da[:, lanes(g, 256)]) * factor).astype(BF16)
        stage_copy(2, n).start()
        for i in range(5):
            @pl.when(n == (1, 5, 8, 11, 14)[i])
            def _(i=i):
                beat(31 + i)
        return carry

    lax.fori_loop(0, 16, proj_grad, 0)
    stage_copy(2, 15).wait()
    for c in range(4):
        total = jnp.zeros((rows, 256), F32)
        for g in range(4):
            for b in range(3):
                total += dot_nt(z[3 * g + b], wqkv[g, 256 * c : 256 * c + 256, 256 * b : 256 * b + 256])
        dh[:, 256 * c : 256 * c + 256] = total
        if c % 2 == 1:
            beat(36 + c // 2)

    def finish_attn(at, dx):
        x[at, :] = (dx1[at, :] + dx).astype(BF16)

    norm_back(x, 0, 38, finish_attn)
    out_copies.append(pltpu.make_async_copy(x, gtok_hbm, save_sem.at[4]))
    out_copies[-1].start()
    beat(39)
    tail_copies = []
    for g in range(4):
        tail = stage.at[g // 2, pl.ds(128 * (g % 2), chunk_rows), :]
        tail[...] = jnp.zeros((chunk_rows, WIDE), BF16)
        for i in range(8):
            tail[2 * i : 2 * i + 1, 0:256] = (grads[i, :, 256 * g : 256 * g + 256] * factor).astype(BF16)
        for q in range(4):
            tail[16:17, 256 * q : 256 * q + 256] = (upg[4 * q + g] * factor).astype(BF16)
        tail_copies.append(pltpu.make_async_copy(tail, g_hbm.at[g % 2, g // 2, pl.ds(3072, chunk_rows), :],
                                                 save_sem.at[5 + g]))
        tail_copies[-1].start()
    for copy in tail_copies:
        copy.wait()

    def remaining(t, carry):
        tick(t)
        return carry

    lax.fori_loop(40 // ratio, tick_count, remaining, 0)
    for copy in out_copies:
        copy.wait()
    for k in range(COUNT):
        for copy in (x_copy(k), y_copy(k), z_copy(k), fx_copy(k), fy_copy(k), fz_copy(k)):
            copy.wait_send()
    for w in range(4):
        for copy in (rest_copy(w), frest_copy(w), core_copy(w)):
            copy.wait_send()


def layer(dp_size, fsdp_size, group, images, counts, tokens, cotangent, small_params, weights):
    rows = tokens.shape[0]
    chunk_rows = 64 if dp_size <= 32 else 128
    chunk_count = 3072 // chunk_rows + 1
    bit_count = dp_size.bit_length() - 1
    g_rows = 3072 + chunk_rows
    any_space, smem = pl.BlockSpec(memory_space=pl.ANY), pl.BlockSpec(memory_space=pltpu.SMEM)
    sems = lambda *dims: pltpu.SemaphoreType.DMA(dims)
    shape = jax.ShapeDtypeStruct
    return pl.pallas_call(
        functools.partial(layer_kernel, rows, chunk_rows, chunk_count, bit_count, 2.0 / (dp_size * fsdp_size)),
        out_shape=(
            shape((rows, D), BF16), shape((rows, D), BF16), shape((g_rows, WIDE), BF16),
            shape((2, 2, g_rows, WIDE), BF16),
        ),
        in_specs=[smem] * 3 + [any_space] * 11,
        out_specs=(any_space,) * 4,
        scratch_shapes=[pltpu.VMEM((4,) + a.shape, BF16) for a in weights] + [
            pltpu.VMEM((rows, D), BF16),
            pltpu.VMEM((rows, D), BF16),
            pltpu.VMEM((24, rows, 128), BF16),
            pltpu.VMEM((rows, D), BF16),
            pltpu.VMEM((rows, D), F32),
            pltpu.VMEM((rows, D), BF16),
            pltpu.VMEM((16, rows, 256), BF16),
            pltpu.VMEM((16, rows, 256), BF16),
            pltpu.VMEM((rows, D), F32),
            pltpu.VMEM((rows, rows), F32),
            pltpu.VMEM((8, 2, 1, rows), F32),
            pltpu.VMEM((rows, D), BF16),
            pltpu.VMEM((rows, D), F32),
            pltpu.VMEM((rows, D), BF16),
            pltpu.VMEM((2, 256, WIDE), BF16),
            [pltpu.VMEM(a.shape, BF16) for a in small_params],
            pltpu.VMEM((16, 256), F32),
            pltpu.VMEM((4, 16, 256), BF16),
            pltpu.VMEM((8, 1, D), F32),
            pltpu.VMEM((24, 1, 128), F32),
            pltpu.VMEM((16, 1, 256), F32),
            pltpu.VMEM((8, 1, D), F32),
            pltpu.VMEM((16, 1, 256), F32),
            sems(4), sems(2, 3), sems(2, 4),
            sems(2, COUNT), sems(2, COUNT), sems(2, COUNT), sems(2, COUNT), sems(2, COUNT), sems(2, COUNT),
            sems(2, 4), sems(2, 4), sems(7), sems(9), sems(2),
            reduce_scratch(chunk_rows, bit_count),
        ],
        compiler_params=pltpu.CompilerParams(collective_id=1, has_side_effects=True, vmem_limit_bytes=VMEM_BYTES),
        name="layer",
    )(group, images, counts, tokens, cotangent, *small_params, *weights)


def widen_kernel(down_ref, up_ref, proj_ref, small_ref, gain_ref, shift_ref, qkv_ref, qvb_ref, wo_ref, outb_ref, wu_ref,
                 upb_ref, wd_ref):
    wd_ref[...] = down_ref[...].astype(F32)
    wu_ref[...] = up_ref[...].T.astype(F32)
    proj = proj_ref[...].astype(F32)
    qkv_ref[...] = proj[:, :768]
    wo_ref[...] = proj[:, 768:]
    small = small_ref[...].astype(F32)
    for i, ref in enumerate((gain_ref, shift_ref, qvb_ref, outb_ref)):
        for j in range(2):
            ref[j : j + 1, :] = small[4 * i + 2 * j : 4 * i + 2 * j + 1, 0:256]
    upb_ref[...] = small[16:17, :]


def widen(total):
    steps = 4
    block = D // steps
    shape = jax.ShapeDtypeStruct
    fixed = lambda *dims: pl.BlockSpec(dims, lambda i: (0, 0))
    return pl.pallas_call(
        widen_kernel,
        grid=(steps,),
        out_shape=(
            shape((2, 256), F32), shape((2, 256), F32), shape((D, 768), F32), shape((2, 256), F32), shape((D, 256), F32),
            shape((2, 256), F32), shape((D, D), F32), shape((1, D), F32), shape((D, D), F32),
        ),
        in_specs=[
            pl.BlockSpec((block, WIDE), lambda i: (i, 0)),
            pl.BlockSpec((block, WIDE), lambda i: (steps + i, 0)),
            pl.BlockSpec((block, WIDE), lambda i: (2 * steps + i, 0)),
            pl.BlockSpec((32, WIDE), lambda i: (3072 // 32, 0)),
        ],
        out_specs=(
            fixed(2, 256), fixed(2, 256), pl.BlockSpec((block, 768), lambda i: (i, 0)), fixed(2, 256),
            pl.BlockSpec((block, 256), lambda i: (i, 0)), fixed(2, 256), pl.BlockSpec((D, block), lambda i: (0, i)),
            fixed(1, D), pl.BlockSpec((block, D), lambda i: (i, 0)),
        ),
        compiler_params=pltpu.CompilerParams(vmem_limit_bytes=32 * 2**20),
        name="widen",
    )(total, total, total, total)


def local(
    tokens,
    cotangent,
    group,
    images,
    counts,
    ln_gain,
    ln_bias,
    w_qkv,
    qv_bias,
    w_out,
    out_bias,
    w_up,
    up_bias,
    w_down,
):
    output, grad_tokens, total, _ = layer(
        lax.axis_size("dp"), lax.axis_size("fsdp"), group, images, counts, tokens, cotangent,
        (ln_gain, ln_bias, qv_bias, out_bias, up_bias.reshape(4, 256)), (w_qkv, w_out, w_up, w_down))
    grads = list(widen(total))
    grads[7] = grads[7].reshape(D)
    return (output, grad_tokens, *grads)


def solution(mesh):
    return jax.shard_map(
        local,
        mesh=mesh,
        in_specs=(
            P(("dp", "fsdp"), None),
            P(("dp", "fsdp"), None),
            P("dp"),
            P("dp", "fsdp"),
            P(),
            P(None, "fsdp"),
            P(None, "fsdp"),
            P(None, "fsdp"),
            P(None, "fsdp"),
            P(None, "fsdp"),
            P(None, "fsdp"),
            P(None, "fsdp"),
            P("fsdp"),
            P("fsdp", None),
        ),
        out_specs=(
            P(("dp", "fsdp"), None),
            P(("dp", "fsdp"), None),
            P(None, "fsdp"),
            P(None, "fsdp"),
            P(None, "fsdp"),
            P(None, "fsdp"),
            P(None, "fsdp"),
            P(None, "fsdp"),
            P(None, "fsdp"),
            P("fsdp"),
            P("fsdp", None),
        ),
        check_vma=False,
    )
```

```python
import functools

import jax
import jax.numpy as jnp
from jax import lax
from jax.experimental import pallas as pl
from jax.experimental.pallas import tpu as pltpu
from jax.sharding import PartitionSpec as P

D = 1024
HDIM = 64
LEN0 = 50
LEN1 = 145
EPSILON = 1e-06
WIDE = 1024
F32 = jnp.float32
BF16 = jnp.bfloat16
MESH = pl.DeviceIdType.MESH
VMEM_BYTES = 62 * 2**20


def split_plan(chunk_rows, bit_count):
    rows, cols, plan = chunk_rows, WIDE, []
    for _ in range(bit_count):
        if rows >= 32:
            rows //= 2
            plan.append(("rows", rows, cols))
        else:
            cols //= 2
            plan.append(("cols", rows, cols))
    return plan


def pipeline_plan(bit_count):
    lag = 2 if bit_count <= 3 else 1
    order = ["core", "x"] + [("bit", b) for b in range(bit_count)] + [("ag", b) for b in reversed(range(bit_count))]
    skews = {stage: 1 if stage == "core" else lag for stage in order}
    when, now = {}, 0
    for stage in order:
        now += skews[stage]
        when[stage] = now
    return skews, when, now


def reduce_scratch(chunk_rows, bit_count):
    plan = split_plan(chunk_rows, bit_count)
    skews, when, _ = pipeline_plan(bit_count)
    slots = {stage: 2 * skew for stage, skew in skews.items()}
    held = when["ag", bit_count - 1] - when["core"] + 1
    return [
        pltpu.VMEM((slots["core"], 2, chunk_rows, WIDE), BF16),
        pltpu.VMEM((slots["core"], 2, chunk_rows, WIDE), BF16),
        pltpu.VMEM((slots["x"], chunk_rows, WIDE), BF16),
        pltpu.VMEM((slots["x"], chunk_rows, WIDE), BF16),
        pltpu.VMEM((held, chunk_rows, WIDE), BF16),
        [pltpu.VMEM((slots["bit", b], r, c), BF16) for b, (_, r, c) in enumerate(plan)],
        pltpu.SemaphoreType.DMA((2, slots["core"])),
        pltpu.SemaphoreType.DMA((2, slots["core"])),
        pltpu.SemaphoreType.DMA((2, slots["x"])),
        [pltpu.SemaphoreType.DMA((2, slots["bit", b])) for b in range(bit_count)],
        [pltpu.SemaphoreType.DMA((2, slots["ag", b])) for b in range(bit_count)],
    ]


def greet(peers):
    barrier = pltpu.get_barrier_semaphore()
    for peer in peers:
        pl.semaphore_signal(barrier, inc=1, device_id=peer, device_id_type=MESH)
    pl.semaphore_wait(barrier, len(peers))


def reduction(chunk_rows, chunk_count, bit_count, g_ref, out_ref, load, core_in, x_out, x_in, acc, bit_in,
              local_sem, core_sem, x_sem, bit_sem, ag_sem):
    dp, f = lax.axis_index("dp"), lax.axis_index("fsdp")
    core, across = lax.rem(f, 2), f // 2
    plan = split_plan(chunk_rows, bit_count)
    skews, when, depth = pipeline_plan(bit_count)
    slot = lambda stage, j: lax.rem(j, 2 * skews[stage])
    held = lambda j: lax.rem(j, acc.shape[0])
    bits = [lax.rem(dp // (1 << b), 2) for b in range(bit_count)]
    flips = [dp + (1 - 2 * bits[b]) * (1 << b) for b in range(bit_count)]
    core_peer = (dp, f + 1 - 2 * core)
    x_peer = (dp, f + 2 - 4 * across)
    peers = [core_peer, x_peer] + [(p, f) for p in flips]

    def region(level, other):
        row, col, rows, cols = 0, 0, chunk_rows, WIDE
        for b in range(level):
            kind, rows, cols = plan[b]
            bit = 1 - bits[b] if other and b == level - 1 else bits[b]
            if kind == "rows":
                row = row + bit * rows
            else:
                col = col + bit * cols
        return row, rows, col, cols

    def cut(ref, lead, base, level, other):
        row, rows, col, cols = region(level, other)
        row_slice = pl.ds(pl.multiple_of(base + row, 16), rows)
        col_slice = slice(None) if cols == WIDE else pl.ds(pl.multiple_of(col, 128), cols)
        return ref.at[lead + (row_slice, col_slice)]

    def rows_of(j):
        return pl.ds(pl.multiple_of(j * chunk_rows, chunk_rows), chunk_rows)

    def remote(src, dst, sems, slot, peer):
        return pltpu.make_async_remote_copy(src, dst, sems.at[0, slot], sems.at[1, slot], device_id=peer,
                                            device_id_type=MESH)

    def load_copy(j):
        s = slot("core", j)
        return pltpu.make_async_copy(g_ref.at[core, :, rows_of(j), :], load.at[s], local_sem.at[0, s])

    def core_copy(j):
        s = slot("core", j)
        return remote(g_ref.at[1 - core, :, rows_of(j), :], core_in.at[s], core_sem, s, core_peer)

    def x_copy(j):
        s = slot("x", j)
        return remote(x_out.at[s], x_in.at[s], x_sem, s, x_peer)

    def bit_copy(b, j):
        s = slot(("bit", b), j)
        return remote(cut(acc, (held(j),), 0, b + 1, True), bit_in[b].at[s], bit_sem[b], s, (flips[b], f))

    def own_copy(j):
        return pltpu.make_async_copy(cut(acc, (held(j),), 0, bit_count, False),
                                     cut(out_ref, (), j * chunk_rows, bit_count, False),
                                     local_sem.at[1, slot("core", j)])

    def ag_copy(b, j):
        mine = cut(out_ref, (), j * chunk_rows, b + 1, False)
        src = cut(acc, (held(j),), 0, bit_count, False) if b == bit_count - 1 else mine
        return remote(src, mine, ag_sem[b], slot(("ag", b), j), (flips[b], f))

    def guarded(t, delay, action):
        j = t - delay

        @pl.when(jnp.logical_and(j >= 0, j < chunk_count))
        def _():
            action(j)

    def on_ag(b):
        def action(j):
            if b == bit_count - 1:
                own_copy(j).wait()
            ag_copy(b, j).wait()
            if b > 0:
                ag_copy(b - 1, j).start()
        return action

    def on_bit(b):
        def action(j):
            bit_copy(b, j).wait()
            mine = cut(acc, (held(j),), 0, b + 1, False)
            mine[...] = (mine[...].astype(F32) + bit_in[b][slot(("bit", b), j)].astype(F32)).astype(BF16)
            if b + 1 < bit_count:
                bit_copy(b + 1, j).start()
            else:
                ag_copy(b, j).start()
                own_copy(j).start()
        return action

    def on_x(j):
        x_copy(j).wait()
        s = held(j)
        acc[s] = (acc[s].astype(F32) + x_in[slot("x", j)].astype(F32)).astype(BF16)
        bit_copy(0, j).start()

    def on_core(j):
        load_copy(j).wait()
        core_copy(j).wait()
        s = slot("core", j)
        for piece, target in ((1 - across, x_out.at[slot("x", j)]), (across, acc.at[held(j)])):
            target[...] = (load[s, piece].astype(F32) + core_in[s, piece].astype(F32)).astype(BF16)
        x_copy(j).start()

    def on_start(j):
        load_copy(j).start()
        core_copy(j).start()

    def tick(t):
        for b in range(bit_count):
            guarded(t, when["ag", b], on_ag(b))
        for b in reversed(range(bit_count)):
            guarded(t, when["bit", b], on_bit(b))
        guarded(t, when["x"], on_x)
        guarded(t, when["core"], on_core)
        guarded(t, 0, on_start)

    return tick, chunk_count + depth, peers


def dot_nn(a, b):
    return lax.dot_general(a, b, (((1,), (0,)), ((), ())), preferred_element_type=F32)


def dot_nt(a, b):
    return lax.dot_general(a, b, (((1,), (1,)), ((), ())), preferred_element_type=F32)


def lanes(index, width):
    return pl.ds(pl.multiple_of(index * width, width), width)


def half_mask(shape, dim, half):
    spot = lax.broadcasted_iota(jnp.int32, shape, dim)
    return spot < HDIM if half == 0 else spot >= HDIM


def fill_bias(bias, inverse, limit, rows):
    step = 128

    def segments(dim, shape, start):
        place = (lax.broadcasted_iota(jnp.int32, shape, dim) + start).astype(F32)
        return jnp.where(place < limit, jnp.floor((place + 0.5) * inverse), float(rows))

    for i in range(rows // step):
        same = segments(0, (step, rows), i * step) == segments(1, (step, rows), 0)
        bias[i * step : (i + 1) * step, :] = jnp.where(same, 0.0, -1e30)


ERF_TERMS = (1.061405429, -1.453152027, 1.421413741, -0.284496736, 0.254829592)


def normal_share(u):
    fall = jnp.exp(u * u * -0.5)
    t = 1.0 / (1.0 + jnp.abs(u) * (0.3275911 * 0.5 ** 0.5))
    series = ERF_TERMS[0] * t
    for c in ERF_TERMS[1:-1]:
        series = (series + c) * t
    tail = 0.5 * (series + ERF_TERMS[-1]) * t * fall
    return jnp.where(u < 0.0, tail, 1.0 - tail), fall


PARTS = 3
PART_ROWS = 336
PIECE_ROWS = 48
PIECES = PART_ROWS // PIECE_ROWS
COUNT = 4 * PIECES
REST = PARTS * PART_ROWS
WINDOWS = (2, 4)
Y_LAG = Z_LAG = 2


def layer_kernel(rows, chunk_rows, chunk_count, bit_count, share, group_ref, images_ref, counts_ref, tok_hbm, cot_hbm,
                 gain_hbm, shift_hbm, qvb_hbm, outb_hbm, upb_hbm, sqkv, so, su, sd,
                 out_hbm, gtok_hbm, sum_hbm, g_hbm,
                 wqkv, wo, wu, wd, x, h1, qkv, o, x1, h2, z, slope, y, bias, lse, dy, dh, da, stage,
                 smalls, pack, vec, vecs, qv, upb, grads, upg,
                 own_sem, vec_sem, rest_sem, x_sem, y_sem, z_sem, fx_sem, fy_sem, fz_sem, frest_sem, core_sem,
                 load_sem, save_sem, stage_sem, comm):
    tick, tick_count, peers = reduction(chunk_rows, chunk_count, bit_count, g_hbm, sum_hbm, *comm)
    ratio = chunk_rows // 64

    def beat(i):
        if ratio == 1:
            tick(i)
        else:
            @pl.when(lax.rem(i, ratio) == ratio - 1)
            def _():
                tick(i // ratio)

    dp, f = lax.axis_index("dp"), lax.axis_index("fsdp")
    core, across = lax.rem(f, 2), f // 2
    yb, zb = lax.rem(dp, 2), lax.rem(dp // 2, 2)
    core_f, x_f, diag_f = f + 1 - 2 * core, f + 2 - 4 * across, 3 - f
    core_peer, x_peer, diag_peer = (dp, core_f), (dp, x_f), (dp, diag_f)
    y_peer, z_peer = (dp + 1 - 2 * yb, f), (dp + 2 - 4 * zb, f)
    part_x = yb + (1 - yb) * 2 * zb
    part_y = (1 - yb) + yb * 2 * zb
    part_z = 2 - 2 * zb
    shards, full = (sqkv, so, su, sd), (wqkv, wo, wu, wd)

    def order(i):
        return 2 * lax.rem(across + i // 2, 2) + lax.rem(core + i, 2)

    def remote(src, dst, sems, slot, peer):
        return pltpu.make_async_remote_copy(src, dst, sems.at[0, slot], sems.at[1, slot], device_id=peer,
                                            device_id_type=MESH)

    def part(k, index):
        return pl.ds(pl.multiple_of(index * PART_ROWS + (k % PIECES) * PIECE_ROWS, 16), PIECE_ROWS)

    rest = pl.ds(REST, D - REST)

    def x_copy(k):
        w, at = k // PIECES, part(k, part_x)
        return remote(shards[w].at[at, :], full[w].at[f, at, :], x_sem, k, x_peer)

    def hop(k, index, sems, peer):
        w, at = k // PIECES, part(k, index)
        return remote(full[w].at[x_f, at, :], full[w].at[x_f, at, :], sems, k, peer)

    y_copy = lambda k: hop(k, part_x, y_sem, y_peer)
    z_copy = lambda k: hop(k, 2 * zb, z_sem, z_peer)
    fx_copy = lambda k: hop(k, part_x, fx_sem, core_peer)
    fy_copy = lambda k: hop(k, part_y, fy_sem, core_peer)
    fz_copy = lambda k: hop(k, part_z, fz_sem, core_peer)

    def rest_copy(w):
        return remote(shards[w].at[rest, :], full[w].at[f, rest, :], rest_sem, w, x_peer)

    def frest_copy(w):
        return remote(full[w].at[x_f, rest, :], full[w].at[x_f, rest, :], frest_sem, w, core_peer)

    def core_copy(w):
        return remote(shards[w], full[w].at[f], core_sem, w, core_peer)

    def own_copy(w):
        return pltpu.make_async_copy(shards[w], full[w].at[f], own_sem.at[w])

    sent = []

    def feed(until):
        while len(sent) < min(until, COUNT):
            x_copy(len(sent)).start()
            sent.append(True)

    def service(k):
        i = k - Y_LAG - Z_LAG
        if 0 <= i < COUNT:
            z_copy(i).wait_recv()
            fz_copy(i).start()
        i = k - Y_LAG
        if 0 <= i < COUNT:
            y_copy(i).wait_recv()
            fy_copy(i).start()

            @pl.when(yb == 1)
            def _():
                z_copy(i).start()
        if k < COUNT:
            x_copy(k).wait_recv()
            y_copy(k).start()

            @pl.when(yb == 0)
            def _():
                z_copy(k).start()

            fx_copy(k).start()
            feed(k + 1 + WINDOWS[k >= PIECES - 2])
            if k % PIECES == 0:
                w = k // PIECES
                rest_copy(w).wait_recv()
                frest_copy(w).start()

    def services(index, plan):
        for i, k in plan:
            @pl.when(index == i)
            def _(k=k):
                service(k)

    def arrived(w):
        frest_copy(w).wait_recv()
        for k in range(w * PIECES, (w + 1) * PIECES):
            fx_copy(k).wait_recv()
            fy_copy(k).wait_recv()
            fz_copy(k).wait_recv()

    loads = [pltpu.make_async_copy(src, dst, load_sem.at[i]) for i, (src, dst) in enumerate(
        [(gain_hbm, smalls[0]), (shift_hbm, smalls[1]), (qvb_hbm, smalls[2]), (outb_hbm, smalls[3]), (upb_hbm, smalls[4]),
         (tok_hbm, x), (cot_hbm, dy)])]
    for copy in loads:
        copy.start()
    own_copy(0).start()
    greet(peers + [diag_peer])
    for copy in loads[:5]:
        copy.wait()
    pack[...] = jnp.zeros_like(pack)
    for i in range(4):
        pack[2 * i : 2 * i + 2, :] = smalls[i][...].astype(F32)
    pack[8:12, :] = smalls[4][...].astype(F32)
    vec[f] = pack[...].astype(BF16)
    vec_copies = [remote(vec.at[f], vec.at[f], vec_sem, i, peer)
                  for i, peer in enumerate((core_peer, x_peer, diag_peer))]
    for copy in vec_copies:
        copy.start()
    feed(WINDOWS[0])
    core_copy(0).start()
    for w in range(4):
        rest_copy(w).start()
    for w in range(1, 4):
        own_copy(w).start()

    first = group_ref[0] == 0
    length = jnp.where(first, LEN0, LEN1)
    inverse = jnp.where(first, 1.0 / LEN0, 1.0 / LEN1).astype(F32)
    limit = (images_ref[0, 0] * length).astype(F32)
    mine = jnp.where(first, counts_ref[0], counts_ref[1])
    fraction = jnp.full((1, 128), mine, jnp.int32).astype(F32) / jnp.full(
        (1, 128), counts_ref[0] + counts_ref[1], jnp.int32).astype(F32)
    factor = fraction[0:1, 0:1] * share
    fill_bias(bias, inverse, limit, rows)
    for copy in vec_copies:
        copy.wait()
    service(0)
    qv[...] = jnp.zeros_like(qv)
    for g in range(4):
        wide = vec[g].astype(F32)
        for i in range(8):
            vecs[i, :, 256 * g : 256 * g + 256] = wide[i : i + 1, :]
        for i in range(4):
            upb[4 * g + i] = wide[8 + i : 9 + i, :]
        for i in range(2):
            qv[2 * g + i] = wide[4:5, 128 * i : 128 * i + 128]
            qv[16 + 2 * g + i] = wide[5:6, 128 * i : 128 * i + 128]

    step = 64

    def normalize(value, which):
        center = value - jnp.mean(value, axis=-1, keepdims=True)
        spread = jnp.mean(center * center, axis=-1, keepdims=True)
        return (center * lax.rsqrt(spread + EPSILON) * vecs[which] + vecs[2 + which]).astype(BF16)

    loads[5].wait()

    def norm_in(i, carry):
        at = pl.ds(pl.multiple_of(i * step, step), step)
        h1[at, :] = normalize(x[at, :].astype(F32), 0)
        return carry

    lax.fori_loop(0, rows // step, norm_in, 0)
    service(1)

    def project(i):
        product = dot_nn(h1[...], wqkv[order(i)])
        for b in range(6):
            block = 6 * order(i) + b
            scale = jnp.where(block < 8, HDIM ** (-0.5), 1.0).astype(F32)
            qkv[block] = ((product[:, 128 * b : 128 * b + 128] + qv[block]) * scale).astype(BF16)

    own_copy(0).wait()
    project(0)
    service(2)
    core_copy(0).wait_recv()
    project(1)
    for k in range(3, PIECES + Y_LAG + Z_LAG):
        service(k)
    for w in range(1, 4):
        core_copy(w).start()
    loads[6].wait()
    live = lax.broadcasted_iota(jnp.int32, (rows, D), 0).astype(F32) < limit
    dy[...] = jnp.where(live, dy[...].astype(F32), 0.0).astype(BF16)
    arrived(0)
    project(2)
    project(3)
    service(11)
    service(12)
    service(13)

    def heads(p, carry):
        services(p, ((0, 14), (2, 15), (3, 16), (5, 17), (6, 18), (7, 19)))
        q_pair, k_pair, v_turned = qkv[p], qkv[8 + p], qkv[16 + p].T
        total = jnp.zeros((128, rows), F32)
        for half in range(2):
            q_half = jnp.where(half_mask((rows, 128), 1, half), q_pair, jnp.zeros_like(q_pair))
            v_half = jnp.where(half_mask((128, rows), 0, half), v_turned, jnp.zeros_like(v_turned))
            scores = dot_nt(k_pair, q_half) + bias[...]
            highest = jnp.max(scores, axis=0, keepdims=True)
            weights = jnp.exp(scores - highest)
            sums = jnp.sum(weights, axis=0, keepdims=True)
            total += dot_nn(v_half, weights.astype(BF16)) * (1.0 / sums)
            lse[p, half] = highest + jnp.log(sums)
        o[:, lanes(p, 128)] = total.T.astype(BF16)
        return carry

    lax.fori_loop(0, 8, heads, 0)
    for w in range(1, 4):
        own_copy(w).wait()
        core_copy(w).wait_recv()
    arrived(1)
    for g in range(4):
        at = slice(256 * g, 256 * g + 256)
        x1[:, at] = x[:, at].astype(F32) + dot_nn(o[...], wo[g]) + vecs[6, :, at]
    service(20)

    def norm_mid(i, carry):
        at = pl.ds(pl.multiple_of(i * step, step), step)
        value = x1[at, :]
        h2[at, :] = normalize(value, 1)
        y[at, :] = value + vecs[7]
        return carry

    lax.fori_loop(0, rows // step, norm_mid, 0)
    service(21)

    def hidden(i, carry):
        services(i, ((2, 22), (4, 23), (6, 24), (9, 25), (11, 26), (13, 27), (15, 28)))

        @pl.when(i == 8)
        def _():
            arrived(2)

        q, g = lax.rem(i, 4), order(i // 4)
        n = 4 * q + g
        u = dot_nn(h2[...], wu[g, :, lanes(q, 256)]) + upb[4 * g + q]
        bell, fall = normal_share(u)
        z[n] = (u * bell).astype(BF16)
        slope[n] = (bell + u * (fall * 0.3989422804014327)).astype(BF16)
        return carry

    lax.fori_loop(0, 16, hidden, 0)

    def stage_copy(which, n):
        s, q, g = lax.rem(n, 2), n // 4, lax.rem(n, 4)
        at = pl.ds(pl.multiple_of(which * D + q * 256, 256), 256)
        return pltpu.make_async_copy(stage.at[s], g_hbm.at[lax.rem(g, 2), g // 2, at, :], stage_sem.at[s])

    def flush(which, n):
        @pl.when(n >= 2)
        def _():
            stage_copy(which, n - 2).wait()

    def down_grad(n, carry):
        services(n, ((1, 29), (3, 30), (4, 31)))
        flush(0, n)
        stage[lax.rem(n, 2)] = (dot_nn(z[n].T, dy[...]) * factor).astype(BF16)
        stage_copy(0, n).start()
        for i in range(4):
            @pl.when(n == 5 + 3 * i)
            def _(i=i):
                beat(i)
        return carry

    lax.fori_loop(0, 16, down_grad, 0)
    stage_copy(0, 14).wait()
    stage_copy(0, 15).wait()
    arrived(3)
    dh[...] = jnp.zeros_like(dh)

    def ffn_back(n, carry):
        q, g = n // 4, lax.rem(n, 4)
        flush(1, n)
        beat(4 + n)
        du = dot_nt(dy[...], wd[g, lanes(q, 256), :]) * slope[n].astype(F32)
        low = du.astype(BF16)
        upg[n] = jnp.sum(low.astype(F32), axis=0, keepdims=True)
        stage[lax.rem(n, 2)] = (dot_nn(low.T, h2[...]) * factor).astype(BF16)
        stage_copy(1, n).start()
        dh[...] += dot_nt(low, wu[g, :, lanes(q, 256)])
        y[...] += dot_nn(z[n], wd[g, lanes(q, 256), :])
        return carry

    lax.fori_loop(0, 16, ffn_back, 0)
    stage_copy(1, 14).wait()
    stage_copy(1, 15).wait()
    out_copies = []
    for c in range(4):
        slope[c] = y[:, 256 * c : 256 * c + 256].astype(BF16)
        out_copies.append(pltpu.make_async_copy(slope.at[c], out_hbm.at[:, pl.ds(256 * c, 256)], save_sem.at[c]))
        out_copies[-1].start()
    beat(20)
    grads[...] = jnp.zeros_like(grads)

    def norm_back(base_ref, which, first_beat, finish):
        def body(i, carry):
            at = pl.ds(pl.multiple_of(i * step, step), step)
            v = base_ref[at, :].astype(F32)
            center = v - jnp.mean(v, axis=-1, keepdims=True)
            rstd = lax.rsqrt(jnp.mean(center * center, axis=-1, keepdims=True) + EPSILON)
            hat = center * rstd
            grad = dh[at, :]
            grads[which] += jnp.sum(grad * hat, axis=0, keepdims=True)
            grads[2 + which] += jnp.sum(grad, axis=0, keepdims=True)
            scaled = grad * vecs[which]
            finish(at, rstd * (scaled - jnp.mean(scaled, axis=-1, keepdims=True)
                               - hat * jnp.mean(scaled * hat, axis=-1, keepdims=True)))

            @pl.when(i == 4)
            def _():
                beat(first_beat)

            return carry

        lax.fori_loop(0, rows // step, body, 0)

    dx1 = y

    def finish_mlp(at, dx):
        dy_part = dy[at, :].astype(F32)
        total = dy_part + dx
        low = total.astype(BF16)
        dx1[at, :] = total
        da[at, :] = low
        grads[6] += jnp.sum(low.astype(F32), axis=0, keepdims=True)
        grads[7] += jnp.sum(dy_part, axis=0, keepdims=True)

    norm_back(x1, 1, 21, finish_mlp)
    for c in range(4):
        total = jnp.zeros((rows, 256), F32)
        for g in range(4):
            total += dot_nt(da[:, 256 * g : 256 * g + 256], wo[g, 256 * c : 256 * c + 256, :])
        slope[4 + c] = total.astype(BF16)
    beat(22)

    def heads_back(p, carry):
        beat(23 + p)
        at = lanes(lax.rem(p, 2), 128)
        q_pair, k_pair, v_pair, do_pair = qkv[p], qkv[8 + p], qkv[16 + p], slope[4 + p // 2, :, at]
        k_turned = k_pair.T
        dk = jnp.zeros((rows, 128), F32)
        dv = jnp.zeros((rows, 128), F32)
        dq = jnp.zeros((128, rows), F32)
        for half in range(2):
            mask = half_mask((rows, 128), 1, half)
            q_half = jnp.where(mask, q_pair, jnp.zeros_like(q_pair))
            do_half = jnp.where(mask, do_pair, jnp.zeros_like(do_pair))
            k_half = jnp.where(half_mask((128, rows), 0, half), k_turned, jnp.zeros_like(k_turned))
            scores = dot_nt(k_pair, q_half) + bias[...]
            weights = jnp.exp(scores - lse[p, half])
            grad = dot_nt(v_pair, do_half)
            inner = jnp.sum(weights * grad, axis=0, keepdims=True)
            low = weights.astype(BF16)
            ds = (weights * (grad - inner)).astype(BF16)
            dv += dot_nn(low, do_half)
            dk += dot_nn(ds, q_half)
            dq += dot_nn(k_half, ds)
        for i, value in ((0, dq.T * HDIM ** (-0.5)), (1, dk), (2, dv)):
            low = value.astype(BF16)
            z[4 * i + p // 2, :, at] = low
            if i != 1:
                grads[4 + i // 2, :, lanes(p, 128)] = jnp.sum(low.astype(F32), axis=0, keepdims=True)
        return carry

    lax.fori_loop(0, 8, heads_back, 0)

    def proj_grad(q, carry):
        left, right = h1[:, lanes(q, 256)].T, o[:, lanes(q, 256)].T
        for g in range(4):
            n = 4 * q + g
            flush(2, n)
            for b in range(3):
                stage[g % 2, :, 256 * b : 256 * b + 256] = (dot_nn(left, z[3 * g + b]) * factor).astype(BF16)
            stage[g % 2, :, 768:1024] = (dot_nn(right, da[:, 256 * g : 256 * g + 256]) * factor).astype(BF16)
            stage_copy(2, n).start()
            if g == 1:
                beat(31 + q)
        return carry

    lax.fori_loop(0, 4, proj_grad, 0)
    stage_copy(2, 14).wait()
    stage_copy(2, 15).wait()
    beat(35)
    for c in range(4):
        total = jnp.zeros((rows, 256), F32)
        for g in range(4):
            for b in range(3):
                total += dot_nt(z[3 * g + b], wqkv[g, 256 * c : 256 * c + 256, 256 * b : 256 * b + 256])
        dh[:, 256 * c : 256 * c + 256] = total
        if c % 2 == 1:
            beat(36 + c // 2)

    def finish_attn(at, dx):
        x[at, :] = (dx1[at, :] + dx).astype(BF16)

    norm_back(x, 0, 38, finish_attn)
    out_copies.append(pltpu.make_async_copy(x, gtok_hbm, save_sem.at[4]))
    out_copies[-1].start()
    beat(39)
    tail_copies = []
    for g in range(4):
        tail = stage.at[g // 2, pl.ds(128 * (g % 2), chunk_rows), :]
        tail[...] = jnp.zeros((chunk_rows, WIDE), BF16)
        for i in range(8):
            tail[2 * i : 2 * i + 1, 0:256] = (grads[i, :, 256 * g : 256 * g + 256] * factor).astype(BF16)
        for q in range(4):
            tail[16:17, 256 * q : 256 * q + 256] = (upg[4 * q + g] * factor).astype(BF16)
        tail_copies.append(pltpu.make_async_copy(tail, g_hbm.at[g % 2, g // 2, pl.ds(3072, chunk_rows), :],
                                                 save_sem.at[5 + g]))
        tail_copies[-1].start()
    for copy in tail_copies:
        copy.wait()

    def remaining(t, carry):
        tick(t)
        return carry

    lax.fori_loop(40 // ratio, tick_count, remaining, 0)
    for copy in out_copies:
        copy.wait()
    for k in range(COUNT):
        for copy in (x_copy(k), y_copy(k), z_copy(k), fx_copy(k), fy_copy(k), fz_copy(k)):
            copy.wait_send()
    for w in range(4):
        for copy in (rest_copy(w), frest_copy(w), core_copy(w)):
            copy.wait_send()


def layer(dp_size, fsdp_size, group, images, counts, tokens, cotangent, small_params, weights):
    rows = tokens.shape[0]
    chunk_rows = 64 if dp_size <= 32 else 128
    chunk_count = 3072 // chunk_rows + 1
    bit_count = dp_size.bit_length() - 1
    g_rows = 3072 + chunk_rows
    any_space, smem = pl.BlockSpec(memory_space=pl.ANY), pl.BlockSpec(memory_space=pltpu.SMEM)
    sems = lambda *dims: pltpu.SemaphoreType.DMA(dims)
    shape = jax.ShapeDtypeStruct
    return pl.pallas_call(
        functools.partial(layer_kernel, rows, chunk_rows, chunk_count, bit_count, 2.0 / (dp_size * fsdp_size)),
        out_shape=(
            shape((rows, D), BF16), shape((rows, D), BF16), shape((g_rows, WIDE), BF16),
            shape((2, 2, g_rows, WIDE), BF16),
        ),
        in_specs=[smem] * 3 + [any_space] * 11,
        out_specs=(any_space,) * 4,
        scratch_shapes=[pltpu.VMEM((4,) + a.shape, BF16) for a in weights] + [
            pltpu.VMEM((rows, D), BF16),
            pltpu.VMEM((rows, D), BF16),
            pltpu.VMEM((24, rows, 128), BF16),
            pltpu.VMEM((rows, D), BF16),
            pltpu.VMEM((rows, D), F32),
            pltpu.VMEM((rows, D), BF16),
            pltpu.VMEM((16, rows, 256), BF16),
            pltpu.VMEM((16, rows, 256), BF16),
            pltpu.VMEM((rows, D), F32),
            pltpu.VMEM((rows, rows), F32),
            pltpu.VMEM((8, 2, 1, rows), F32),
            pltpu.VMEM((rows, D), BF16),
            pltpu.VMEM((rows, D), F32),
            pltpu.VMEM((rows, D), BF16),
            pltpu.VMEM((2, 256, WIDE), BF16),
            [pltpu.VMEM(a.shape, BF16) for a in small_params],
            pltpu.VMEM((16, 256), F32),
            pltpu.VMEM((4, 16, 256), BF16),
            pltpu.VMEM((8, 1, D), F32),
            pltpu.VMEM((24, 1, 128), F32),
            pltpu.VMEM((16, 1, 256), F32),
            pltpu.VMEM((8, 1, D), F32),
            pltpu.VMEM((16, 1, 256), F32),
            sems(4), sems(2, 3), sems(2, 4),
            sems(2, COUNT), sems(2, COUNT), sems(2, COUNT), sems(2, COUNT), sems(2, COUNT), sems(2, COUNT),
            sems(2, 4), sems(2, 4), sems(7), sems(9), sems(2),
            reduce_scratch(chunk_rows, bit_count),
        ],
        compiler_params=pltpu.CompilerParams(collective_id=1, has_side_effects=True, vmem_limit_bytes=VMEM_BYTES),
        name="layer",
    )(group, images, counts, tokens, cotangent, *small_params, *weights)


def widen_kernel(down_ref, up_ref, proj_ref, small_ref, gain_ref, shift_ref, qkv_ref, qvb_ref, wo_ref, outb_ref, wu_ref,
                 upb_ref, wd_ref):
    wd_ref[...] = down_ref[...].astype(F32)
    wu_ref[...] = up_ref[...].T.astype(F32)
    proj = proj_ref[...].astype(F32)
    qkv_ref[...] = proj[:, :768]
    wo_ref[...] = proj[:, 768:]
    small = small_ref[...].astype(F32)
    for i, ref in enumerate((gain_ref, shift_ref, qvb_ref, outb_ref)):
        for j in range(2):
            ref[j : j + 1, :] = small[4 * i + 2 * j : 4 * i + 2 * j + 1, 0:256]
    upb_ref[...] = small[16:17, :]


def widen(total):
    steps = 4
    block = D // steps
    shape = jax.ShapeDtypeStruct
    fixed = lambda *dims: pl.BlockSpec(dims, lambda i: (0, 0))
    return pl.pallas_call(
        widen_kernel,
        grid=(steps,),
        out_shape=(
            shape((2, 256), F32), shape((2, 256), F32), shape((D, 768), F32), shape((2, 256), F32), shape((D, 256), F32),
            shape((2, 256), F32), shape((D, D), F32), shape((1, D), F32), shape((D, D), F32),
        ),
        in_specs=[
            pl.BlockSpec((block, WIDE), lambda i: (i, 0)),
            pl.BlockSpec((block, WIDE), lambda i: (steps + i, 0)),
            pl.BlockSpec((block, WIDE), lambda i: (2 * steps + i, 0)),
            pl.BlockSpec((32, WIDE), lambda i: (3072 // 32, 0)),
        ],
        out_specs=(
            fixed(2, 256), fixed(2, 256), pl.BlockSpec((block, 768), lambda i: (i, 0)), fixed(2, 256),
            pl.BlockSpec((block, 256), lambda i: (i, 0)), fixed(2, 256), pl.BlockSpec((D, block), lambda i: (0, i)),
            fixed(1, D), pl.BlockSpec((block, D), lambda i: (i, 0)),
        ),
        compiler_params=pltpu.CompilerParams(vmem_limit_bytes=32 * 2**20),
        name="widen",
    )(total, total, total, total)


def local(
    tokens,
    cotangent,
    group,
    images,
    counts,
    ln_gain,
    ln_bias,
    w_qkv,
    qv_bias,
    w_out,
    out_bias,
    w_up,
    up_bias,
    w_down,
):
    output, grad_tokens, total, _ = layer(
        lax.axis_size("dp"), lax.axis_size("fsdp"), group, images, counts, tokens, cotangent,
        (ln_gain, ln_bias, qv_bias, out_bias, up_bias.reshape(4, 256)), (w_qkv, w_out, w_up, w_down))
    grads = list(widen(total))
    grads[7] = grads[7].reshape(D)
    return (output, grad_tokens, *grads)


def solution(mesh):
    return jax.shard_map(
        local,
        mesh=mesh,
        in_specs=(
            P(("dp", "fsdp"), None),
            P(("dp", "fsdp"), None),
            P("dp"),
            P("dp", "fsdp"),
            P(),
            P(None, "fsdp"),
            P(None, "fsdp"),
            P(None, "fsdp"),
            P(None, "fsdp"),
            P(None, "fsdp"),
            P(None, "fsdp"),
            P(None, "fsdp"),
            P("fsdp"),
            P("fsdp", None),
        ),
        out_specs=(
            P(("dp", "fsdp"), None),
            P(("dp", "fsdp"), None),
            P(None, "fsdp"),
            P(None, "fsdp"),
            P(None, "fsdp"),
            P(None, "fsdp"),
            P(None, "fsdp"),
            P(None, "fsdp"),
            P(None, "fsdp"),
            P("fsdp"),
            P("fsdp", None),
        ),
        check_vma=False,
    )
```

```python
import functools

import jax
import jax.numpy as jnp
from jax import lax
from jax.experimental import pallas as pl
from jax.experimental.pallas import tpu as pltpu
from jax.sharding import PartitionSpec as P

D = 1024
HDIM = 64
LEN0 = 50
LEN1 = 145
EPSILON = 1e-06
WIDE = 1024
F32 = jnp.float32
BF16 = jnp.bfloat16
MESH = pl.DeviceIdType.MESH
VMEM_BYTES = 64 * 2**20
STAGE_LAGS = (1, 3, 3, 3, 3, 3, 3, 3)
PAIR_EVERY = 8


def split_plan(chunk_rows, bit_count):
    rows, cols, plan = chunk_rows, WIDE, []
    for _ in range(bit_count):
        if rows >= 32:
            rows //= 2
            plan.append(("rows", rows, cols))
        else:
            cols //= 2
            plan.append(("cols", rows, cols))
    return plan


def pipeline_plan(bit_count):
    lags = list(STAGE_LAGS) if bit_count == 3 else [1] * (2 * bit_count + 2)
    return lags[1:], [sum(lags[: i + 1]) for i in range(len(lags))]


def power_of_two(n):
    return 1 << (n - 1).bit_length()


def reduce_scratch(chunk_rows, bit_count):
    plan = split_plan(chunk_rows, bit_count)
    lags, when = pipeline_plan(bit_count)
    held = power_of_two(when[bit_count + 2] - when[0] + 1)
    slots = [power_of_two(2 * lag) for lag in lags]
    half = plan[0][1]
    stages = 2 * bit_count + 1
    return [
        pltpu.VMEM((2, 2, chunk_rows, WIDE), BF16),
        pltpu.VMEM((2, 2, chunk_rows, WIDE), BF16),
        pltpu.VMEM((slots[0], chunk_rows, WIDE), BF16),
        pltpu.VMEM((slots[0], chunk_rows, WIDE), BF16),
        pltpu.VMEM((held, chunk_rows, WIDE), BF16),
        [pltpu.VMEM((slots[1 + b], r, c), BF16) for b, (_, r, c) in enumerate(plan)],
        pltpu.VMEM((2, 2, chunk_rows, WIDE), BF16),
        pltpu.VMEM((2, 2, half, WIDE), BF16),
        pltpu.VMEM((2, half, WIDE), BF16),
        [pltpu.VMEM((2, r, c), BF16) for _, r, c in plan[1:]],
        pltpu.SemaphoreType.DMA((2,)),
        pltpu.SemaphoreType.DMA((2, 2)),
        [pltpu.SemaphoreType.DMA((2, slots[i])) for i in range(stages)],
        [pltpu.SemaphoreType.DMA((2, 2)) for _ in range(stages)],
        pltpu.SemaphoreType.DMA((4,)),
        pltpu.SemaphoreType.DMA((2,)),
    ]


def greet(peers):
    barrier = pltpu.get_barrier_semaphore()
    for peer in peers:
        pl.semaphore_signal(barrier, inc=1, device_id=peer, device_id_type=MESH)
    pl.semaphore_wait(barrier, len(peers))


def reduction(chunk_rows, chunk_count, bit_count, g_ref, out_ref, load, core_in, x_out, x_in, acc, bit_in,
              pair, pair_in, pair_x_in, pair_bit_in, load_sem, core_sem, main_sems, pair_sems, main_own_sem, pair_own_sem):
    dp, f = lax.axis_index("dp"), lax.axis_index("fsdp")
    core, across = lax.rem(f, 2), f // 2
    plan = split_plan(chunk_rows, bit_count)
    lags, when = pipeline_plan(bit_count)
    slot = lambda stage, j: lax.rem(j, power_of_two(2 * lags[stage]))
    held = lambda j: lax.rem(j, acc.shape[0])
    pair_slot = lambda j: lax.rem(j // PAIR_EVERY, 2)
    bits = [lax.rem(dp // (1 << b), 2) for b in range(bit_count)]
    flips = [dp + (1 - 2 * bits[b]) * (1 << b) for b in range(bit_count)]
    core_peer = (dp, f + 1 - 2 * core)
    x_peer = (dp, f + 2 - 4 * across)
    peers = [core_peer, x_peer] + [(p, f) for p in flips]
    main_order = list(range(bit_count))
    pair_order = [1, 0] + main_order[2:]

    def region(level, other, order):
        row, col, rows, cols = 0, 0, chunk_rows, WIDE
        for i in range(level):
            kind, rows, cols = plan[i]
            bit = bits[order[i]]
            if other and i == level - 1:
                bit = 1 - bit
            if kind == "rows":
                row = row + bit * rows
            else:
                col = col + bit * cols
        return row, rows, col, cols

    def cut(ref, lead, base, level, other, order):
        row, rows, col, cols = region(level, other, order)
        row_slice = pl.ds(pl.multiple_of(base + row, 16), rows)
        col_slice = slice(None) if cols == WIDE else pl.ds(pl.multiple_of(col, 128), cols)
        return ref.at[lead + (row_slice, col_slice)]

    def rows_of(j):
        return pl.ds(pl.multiple_of(j * chunk_rows, chunk_rows), chunk_rows)

    def remote(src, dst, sems, s, peer):
        return pltpu.make_async_remote_copy(src, dst, sems.at[0, s], sems.at[1, s], device_id=peer,
                                            device_id_type=MESH)

    def load_copy(j):
        s = lax.rem(j, 2)
        return pltpu.make_async_copy(g_ref.at[core, :, rows_of(j), :], load.at[s], load_sem.at[s])

    def core_copy(j):
        s = lax.rem(j, 2)
        return remote(g_ref.at[1 - core, :, rows_of(j), :], core_in.at[s], core_sem, s, core_peer)

    def spread_copy(j, i, source, order, sems, s):
        mine = cut(out_ref, (), j * chunk_rows, i + 1, False, order)
        return remote(source if i == bit_count - 1 else mine, mine, sems, s, (flips[order[i]], f))

    def main_part(j, level, other):
        return cut(acc, (held(j),), 0, level, other, main_order)

    def main_own(j):
        return pltpu.make_async_copy(main_part(j, bit_count, False),
                                     cut(out_ref, (), j * chunk_rows, bit_count, False, main_order),
                                     main_own_sem.at[lax.rem(j, 4)])

    def main_copy(stage, j):
        s, sems = slot(stage, j), main_sems[stage]
        if stage == 0:
            return remote(x_out.at[s], x_in.at[s], sems, s, x_peer)
        if stage <= bit_count:
            b = stage - 1
            return remote(main_part(j, b + 1, True), bit_in[b].at[s], sems, s, (flips[b], f))
        return spread_copy(j, 2 * bit_count - stage, main_part(j, bit_count, False), main_order, sems, s)

    def main_core(j):
        s = lax.rem(j, 2)
        for piece, target in ((1 - across, x_out.at[slot(0, j)]), (across, acc.at[held(j)])):
            target[...] = load[s, piece] + core_in[s, piece]
        main_copy(0, j).start()

    def main_take(stage, j):
        main_copy(stage, j).wait()
        if stage == 0:
            acc[held(j)] = acc[held(j)] + x_in[slot(0, j)]
        elif stage <= bit_count:
            part = main_part(j, stage, False)
            part[...] = part[...] + bit_in[stage - 1][slot(stage, j)]
        elif stage == bit_count + 1:
            main_own(j).wait()
        if stage == bit_count:
            main_own(j).start()
        if stage < 2 * bit_count:
            main_copy(stage + 1, j).start()

    def pair_part(j, level, other):
        return cut(pair, (pair_slot(j), across), 0, level, other, pair_order)

    def pair_own(j):
        return pltpu.make_async_copy(pair_part(j, bit_count, False),
                                     cut(out_ref, (), j * chunk_rows, bit_count, False, pair_order),
                                     pair_own_sem.at[pair_slot(j)])

    def pair_copy(stage, j):
        s, sems = pair_slot(j), pair_sems[stage]
        if stage == 0:
            return remote(cut(pair, (s, slice(None)), 0, 1, True, pair_order), pair_in.at[s], sems, s, (flips[1], f))
        if stage == 1:
            return remote(cut(pair, (s, 1 - across), 0, 1, False, pair_order), pair_x_in.at[s], sems, s, x_peer)
        if stage <= bit_count:
            return remote(pair_part(j, stage, True), pair_bit_in[stage - 2].at[s], sems, s,
                          (flips[pair_order[stage - 1]], f))
        return spread_copy(j, 2 * bit_count - stage, pair_part(j, bit_count, False), pair_order, sems, s)

    def pair_core(j):
        s = lax.rem(j, 2)
        pair[pair_slot(j)] = load[s] + core_in[s]
        pair_copy(0, j).start()

    def pair_take(stage, j):
        s = pair_slot(j)
        pair_copy(stage, j).wait()
        if stage == 0:
            part = cut(pair, (s, slice(None)), 0, 1, False, pair_order)
            part[...] = part[...] + pair_in[s]
        elif stage == 1:
            part = pair_part(j, 1, False)
            part[...] = part[...] + pair_x_in[s]
        elif stage <= bit_count:
            part = pair_part(j, stage, False)
            part[...] = part[...] + pair_bit_in[stage - 2][s]
        elif stage == bit_count + 1:
            pair_own(j).wait()
        if stage == bit_count:
            pair_own(j).start()
        if stage < 2 * bit_count:
            pair_copy(stage + 1, j).start()

    def guarded(t, delay, *actions):
        j = t - delay
        inside = jnp.logical_and(j >= 0, j < chunk_count)
        chosen = lax.rem(j, PAIR_EVERY) == 3
        for action, choice in zip(actions, (jnp.logical_not(chosen), chosen)):
            @pl.when(jnp.logical_and(inside, choice) if len(actions) > 1 else inside)
            def _(action=action):
                action(j)

    def on_core(take):
        def action(j):
            load_copy(j).wait()
            core_copy(j).wait()
            take(j)
        return action

    def on_start(j):
        load_copy(j).start()
        core_copy(j).start()

    def tick(t):
        for stage in reversed(range(2 * bit_count + 1)):
            guarded(t, when[stage + 1], functools.partial(main_take, stage), functools.partial(pair_take, stage))
        guarded(t, when[0], on_core(main_core), on_core(pair_core))
        guarded(t, 0, on_start)

    return tick, chunk_count + when[-1], peers


def dot_nn(a, b):
    return lax.dot_general(a, b, (((1,), (0,)), ((), ())), preferred_element_type=F32)


def dot_nt(a, b):
    return lax.dot_general(a, b, (((1,), (1,)), ((), ())), preferred_element_type=F32)


def lanes(index, width):
    return pl.ds(pl.multiple_of(index * width, width), width)


def half_mask(shape, dim, half):
    spot = lax.broadcasted_iota(jnp.int32, shape, dim)
    return spot < HDIM if half == 0 else spot >= HDIM


def fill_bias(bias, inverse, limit, rows):
    step = 128

    def segments(dim, shape, start):
        place = (lax.broadcasted_iota(jnp.int32, shape, dim) + start).astype(F32)
        return jnp.where(place < limit, jnp.floor((place + 0.5) * inverse), float(rows))

    for i in range(rows // step):
        same = segments(0, (step, rows), i * step) == segments(1, (step, rows), 0)
        bias[i * step : (i + 1) * step, :] = jnp.where(same, 0.0, -1e30)


ERF_TERMS = (1.061405429, -1.453152027, 1.421413741, -0.284496736, 0.254829592)


def normal_share(u):
    fall = jnp.exp(u * u * -0.5)
    t = 1.0 / (1.0 + jnp.abs(u) * (0.3275911 * 0.5 ** 0.5))
    series = ERF_TERMS[0] * t
    for c in ERF_TERMS[1:-1]:
        series = (series + c) * t
    tail = 0.5 * (series + ERF_TERMS[-1]) * t * fall
    return jnp.where(u < 0.0, tail, 1.0 - tail), fall


PARTS = 3
PART_ROWS = 336
PIECE_ROWS = 48
PIECES = PART_ROWS // PIECE_ROWS
COUNT = 4 * PIECES
REST = PARTS * PART_ROWS
WINDOWS = (2, 4)
Y_LAG = Z_LAG = 2


def layer_kernel(rows, chunk_rows, chunk_count, bit_count, share, group_ref, images_ref, counts_ref, tok_hbm, cot_hbm,
                 gain_hbm, shift_hbm, qvb_hbm, outb_hbm, upb_hbm, sqkv, so, su, sd,
                 out_hbm, gtok_hbm, sum_hbm, g_hbm,
                 wqkv, wo, wu, wd, x, h1, qkv, o, x1, h2, z, slope, y, bias, lse, dy, dh, da, stage,
                 smalls, pack, vec, vecs, qv, upb, grads, upg,
                 own_sem, vec_sem, rest_sem, x_sem, y_sem, z_sem, x_sent, y_sent, z_sent, far_sent, far_sem, core_sem,
                 load_sem, save_sem, stage_sem, comm):
    tick, tick_count, peers = reduction(chunk_rows, chunk_count, bit_count, g_hbm, sum_hbm, *comm)
    ratio = chunk_rows // 64

    def beat(i):
        if ratio == 1:
            tick(i)
        else:
            @pl.when(lax.rem(i, ratio) == ratio - 1)
            def _():
                tick(i // ratio)

    dp, f = lax.axis_index("dp"), lax.axis_index("fsdp")
    core, across = lax.rem(f, 2), f // 2
    yb, zb = lax.rem(dp, 2), lax.rem(dp // 2, 2)
    core_f, x_f, diag_f = f + 1 - 2 * core, f + 2 - 4 * across, 3 - f
    core_peer, x_peer, diag_peer = (dp, core_f), (dp, x_f), (dp, diag_f)
    y_peer, z_peer = (dp + 1 - 2 * yb, f), (dp + 2 - 4 * zb, f)
    part_x = yb + (1 - yb) * 2 * zb
    part_y = (1 - yb) + yb * 2 * zb
    part_z = 2 - 2 * zb
    shards, full = (sqkv, so, su, sd), (wqkv, wo, wu, wd)

    def order(i):
        return 2 * lax.rem(across + i // 2, 2) + lax.rem(core + i, 2)

    def remote(src, dst, sems, slot, peer):
        return pltpu.make_async_remote_copy(src, dst, sems.at[0, slot], sems.at[1, slot], device_id=peer,
                                            device_id_type=MESH)

    def part(k, index):
        return pl.ds(pl.multiple_of(index * PART_ROWS + (k % PIECES) * PIECE_ROWS, 16), PIECE_ROWS)

    rest = pl.ds(REST, D - REST)

    def piece_copy(src, dst, send, receive, peer):
        return pltpu.make_async_remote_copy(src, dst, send, receive, device_id=peer, device_id_type=MESH)

    def x_copy(k):
        w, at = k // PIECES, part(k, part_x)
        return piece_copy(shards[w].at[at, :], full[w].at[f, at, :], x_sent.at[w], x_sem.at[k], x_peer)

    def hop(k, index, send, receive, peer):
        place = full[k // PIECES].at[x_f, part(k, index), :]
        return piece_copy(place, place, send.at[k // PIECES], receive, peer)

    y_copy = lambda k: hop(k, part_x, y_sent, y_sem.at[k], y_peer)
    z_copy = lambda k: hop(k, 2 * zb, z_sent, z_sem.at[k], z_peer)
    fx_copy = lambda k: hop(k, part_x, far_sent, far_sem.at[k // PIECES], core_peer)
    fy_copy = lambda k: hop(k, part_y, far_sent, far_sem.at[k // PIECES], core_peer)
    fz_copy = lambda k: hop(k, part_z, far_sent, far_sem.at[k // PIECES], core_peer)

    def rest_copy(w):
        return remote(shards[w].at[rest, :], full[w].at[f, rest, :], rest_sem, w, x_peer)

    def frest_copy(w):
        place = full[w].at[x_f, rest, :]
        return piece_copy(place, place, far_sent.at[w], far_sem.at[w], core_peer)

    def far_copy(w):
        return piece_copy(full[w].at[x_f], full[w].at[x_f], far_sent.at[w], far_sem.at[w], core_peer)

    def part_sent(w, sent, peer):
        place = full[w].at[x_f, pl.ds(0, PART_ROWS), :]
        return piece_copy(place, place, sent.at[w], x_sem.at[0], peer)

    def core_copy(w):
        return remote(shards[w], full[w].at[f], core_sem, w, core_peer)

    def own_copy(w):
        return pltpu.make_async_copy(shards[w], full[w].at[f], own_sem.at[w])

    sent = []

    def feed(until):
        while len(sent) < min(until, COUNT):
            x_copy(len(sent)).start()
            sent.append(True)

    def service(k):
        i = k - Y_LAG - Z_LAG
        if 0 <= i < COUNT:
            z_copy(i).wait_recv()
            fz_copy(i).start()
        i = k - Y_LAG
        if 0 <= i < COUNT:
            y_copy(i).wait_recv()
            fy_copy(i).start()

            @pl.when(yb == 1)
            def _():
                z_copy(i).start()
        if k < COUNT:
            x_copy(k).wait_recv()
            y_copy(k).start()

            @pl.when(yb == 0)
            def _():
                z_copy(k).start()

            fx_copy(k).start()
            feed(k + 1 + WINDOWS[k >= PIECES - 2])
            if k % PIECES == 0:
                w = k // PIECES
                rest_copy(w).wait_recv()
                frest_copy(w).start()

    def services(index, plan):
        for i, k in plan:
            @pl.when(index == i)
            def _(k=k):
                service(k)

    def arrived(w):
        far_copy(w).wait_recv()

    loads = [pltpu.make_async_copy(src, dst, load_sem.at[i]) for i, (src, dst) in enumerate(
        [(gain_hbm, smalls[0]), (shift_hbm, smalls[1]), (qvb_hbm, smalls[2]), (outb_hbm, smalls[3]), (upb_hbm, smalls[4]),
         (tok_hbm, x), (cot_hbm, dy)])]
    for copy in loads:
        copy.start()
    own_copy(0).start()
    greet(peers + [diag_peer])
    for copy in loads[:5]:
        copy.wait()
    pack[...] = jnp.zeros_like(pack)
    for i in range(4):
        pack[2 * i : 2 * i + 2, :] = smalls[i][...].astype(F32)
    pack[8:12, :] = smalls[4][...].astype(F32)
    vec[f] = pack[...].astype(BF16)
    vec_copies = [remote(vec.at[f], vec.at[f], vec_sem, i, peer)
                  for i, peer in enumerate((core_peer, x_peer, diag_peer))]
    for copy in vec_copies:
        copy.start()
    feed(WINDOWS[0])
    core_copy(0).start()
    for w in range(4):
        rest_copy(w).start()
    for w in range(1, 4):
        own_copy(w).start()

    first = group_ref[0] == 0
    length = jnp.where(first, LEN0, LEN1)
    inverse = jnp.where(first, 1.0 / LEN0, 1.0 / LEN1).astype(F32)
    limit = (images_ref[0, 0] * length).astype(F32)
    mine = jnp.where(first, counts_ref[0], counts_ref[1])
    fraction = jnp.full((1, 128), mine, jnp.int32).astype(F32) / jnp.full(
        (1, 128), counts_ref[0] + counts_ref[1], jnp.int32).astype(F32)
    factor = fraction[0:1, 0:1] * share
    fill_bias(bias, inverse, limit, rows)
    for copy in vec_copies:
        copy.wait()
    service(0)
    qv[...] = jnp.zeros_like(qv)
    for g in range(4):
        wide = vec[g].astype(F32)
        for i in range(8):
            vecs[i, :, 256 * g : 256 * g + 256] = wide[i : i + 1, :]
        for i in range(4):
            upb[4 * g + i] = wide[8 + i : 9 + i, :]
        for i in range(2):
            qv[2 * g + i] = wide[4:5, 128 * i : 128 * i + 128]
            qv[16 + 2 * g + i] = wide[5:6, 128 * i : 128 * i + 128]

    step = 64

    def normalize(value, which):
        center = value - jnp.mean(value, axis=-1, keepdims=True)
        spread = jnp.mean(center * center, axis=-1, keepdims=True)
        return (center * lax.rsqrt(spread + EPSILON) * vecs[which] + vecs[2 + which]).astype(BF16)

    loads[5].wait()

    def norm_in(i, carry):
        at = pl.ds(pl.multiple_of(i * step, step), step)
        h1[at, :] = normalize(x[at, :].astype(F32), 0)
        return carry

    lax.fori_loop(0, rows // step, norm_in, 0)
    service(1)

    def project(i):
        product = dot_nn(h1[...], wqkv[order(i)])
        for b in range(6):
            block = 6 * order(i) + b
            scale = jnp.where(block < 8, HDIM ** (-0.5), 1.0).astype(F32)
            qkv[block] = ((product[:, 128 * b : 128 * b + 128] + qv[block]) * scale).astype(BF16)

    own_copy(0).wait()
    project(0)
    service(2)
    core_copy(0).wait_recv()
    project(1)
    for k in range(3, PIECES + Y_LAG + Z_LAG + 1):
        service(k)
    for w in range(1, 4):
        core_copy(w).start()
    loads[6].wait()
    live = lax.broadcasted_iota(jnp.int32, (rows, D), 0).astype(F32) < limit
    dy[...] = jnp.where(live, dy[...].astype(F32), 0.0).astype(BF16)
    arrived(0)
    project(2)
    service(12)
    project(3)
    service(13)

    def heads(p, carry):
        services(p, ((0, 14), (2, 15), (3, 16), (5, 17), (6, 18), (7, 19)))
        q_pair, k_pair, v_turned = qkv[p], qkv[8 + p], qkv[16 + p].T
        total = jnp.zeros((128, rows), F32)
        for half in range(2):
            q_half = jnp.where(half_mask((rows, 128), 1, half), q_pair, jnp.zeros_like(q_pair))
            v_half = jnp.where(half_mask((128, rows), 0, half), v_turned, jnp.zeros_like(v_turned))
            scores = dot_nt(k_pair, q_half) + bias[...]
            highest = jnp.max(scores, axis=0, keepdims=True)
            weights = jnp.exp(scores - highest)
            sums = jnp.sum(weights, axis=0, keepdims=True)
            total += dot_nn(v_half, weights.astype(BF16)) * (1.0 / sums)
            lse[p, half] = highest + jnp.log(sums)
        o[:, lanes(p, 128)] = total.T.astype(BF16)
        return carry

    lax.fori_loop(0, 8, heads, 0)
    for w in range(1, 4):
        own_copy(w).wait()
        core_copy(w).wait_recv()
    arrived(1)
    for g in range(4):
        at = slice(256 * g, 256 * g + 256)
        x1[:, at] = x[:, at].astype(F32) + dot_nn(o[...], wo[g]) + vecs[6, :, at]
    service(20)

    def norm_mid(i, carry):
        at = pl.ds(pl.multiple_of(i * step, step), step)
        value = x1[at, :]
        h2[at, :] = normalize(value, 1)
        y[at, :] = value + vecs[7]
        return carry

    lax.fori_loop(0, rows // step, norm_mid, 0)
    service(21)

    def hidden(q, i):
        g = order(i)
        n = 4 * q + g
        u = dot_nn(h2[...], wu[g, :, lanes(q, 256)]) + upb[4 * g + q]
        bell, fall = normal_share(u)
        z[n] = (u * bell).astype(BF16)
        slope[n] = (bell + u * (fall * 0.3989422804014327)).astype(BF16)

    def hidden_near(i, carry):
        services(i, ((0, 22), (1, 23), (3, 24)))
        hidden(i // 2, lax.rem(i, 2))
        return carry

    lax.fori_loop(0, 4, hidden_near, 0)
    arrived(2)

    def hidden_far(i, carry):
        hidden(0, 2 + i)
        return carry

    lax.fori_loop(0, 2, hidden_far, 0)
    service(25)

    def stage_copy(which, n):
        s, q, g = lax.rem(n, 2), n // 4, lax.rem(n, 4)
        at = pl.ds(pl.multiple_of(which * D + q * 256, 256), 256)
        return pltpu.make_async_copy(stage.at[s], g_hbm.at[lax.rem(g, 2), g // 2, at, :], stage_sem.at[s])

    def flush(which, n, start=0):
        @pl.when(n >= start + 2)
        def _():
            stage_copy(which, n - 2).wait()

    def down_grad(n, start):
        flush(0, n, start)
        stage[lax.rem(n, 2)] = (dot_nn(z[n].T, dy[...]) * factor).astype(BF16)
        stage_copy(0, n).start()

    def down_first(n, carry):
        services(n, ((1, 26), (3, 27)))
        down_grad(n, 0)
        return carry

    lax.fori_loop(0, 4, down_first, 0)
    stage_copy(0, 2).wait()
    stage_copy(0, 3).wait()
    beat(0)

    def down_block(q, carry):
        def units(i, inner):
            services(4 * q + i, ((6, 28), (7, 29)))

            @pl.when(4 * q + i >= 6)
            def _():
                hidden(q, i)

            for spot, t in ((7, 1), (14, 6)):
                @pl.when(4 * q + i == spot)
                def _(t=t):
                    beat(t)
            return inner

        def grads_of(g, inner):
            n = 4 * q + g
            services(n, ((5, 30), (6, 31)))
            down_grad(n, 4)
            for spot, t in ((5, 2), (7, 3), (9, 4), (11, 5), (13, 7), (15, 8)):
                @pl.when(n == spot)
                def _(t=t):
                    beat(t)
            return inner

        lax.fori_loop(0, 4, units, 0)
        lax.fori_loop(0, 4, grads_of, 0)
        return carry

    lax.fori_loop(1, 4, down_block, 0)
    stage_copy(0, 14).wait()
    stage_copy(0, 15).wait()
    arrived(3)
    dh[...] = jnp.zeros_like(dh)

    def ffn_back(n, carry):
        q, g = n // 4, lax.rem(n, 4)
        flush(1, n)

        @pl.when(jnp.logical_or(n == 0, lax.rem(n, 5) != 0))
        def _():
            beat(9 + n - n // 5)

        du = dot_nt(dy[...], wd[g, lanes(q, 256), :]) * slope[n].astype(F32)
        low = du.astype(BF16)
        upg[n] = jnp.sum(low.astype(F32), axis=0, keepdims=True)
        stage[lax.rem(n, 2)] = (dot_nn(low.T, h2[...]) * factor).astype(BF16)
        stage_copy(1, n).start()
        dh[...] += dot_nt(low, wu[g, :, lanes(q, 256)])
        y[...] += dot_nn(z[n], wd[g, lanes(q, 256), :])
        return carry

    lax.fori_loop(0, 16, ffn_back, 0)
    stage_copy(1, 14).wait()
    stage_copy(1, 15).wait()
    out_copies = []
    for c in range(4):
        slope[c] = y[:, 256 * c : 256 * c + 256].astype(BF16)
        out_copies.append(pltpu.make_async_copy(slope.at[c], out_hbm.at[:, pl.ds(256 * c, 256)], save_sem.at[c]))
        out_copies[-1].start()
    beat(22)
    grads[...] = jnp.zeros_like(grads)

    def norm_back(base_ref, which, first_beat, finish):
        def body(i, carry):
            at = pl.ds(pl.multiple_of(i * step, step), step)
            v = base_ref[at, :].astype(F32)
            center = v - jnp.mean(v, axis=-1, keepdims=True)
            rstd = lax.rsqrt(jnp.mean(center * center, axis=-1, keepdims=True) + EPSILON)
            hat = center * rstd
            grad = dh[at, :]
            grads[which] += jnp.sum(grad * hat, axis=0, keepdims=True)
            grads[2 + which] += jnp.sum(grad, axis=0, keepdims=True)
            scaled = grad * vecs[which]
            finish(at, rstd * (scaled - jnp.mean(scaled, axis=-1, keepdims=True)
                               - hat * jnp.mean(scaled * hat, axis=-1, keepdims=True)))

            @pl.when(i == 4)
            def _():
                beat(first_beat)

            return carry

        lax.fori_loop(0, rows // step, body, 0)

    dx1 = y

    def finish_mlp(at, dx):
        dy_part = dy[at, :].astype(F32)
        total = dy_part + dx
        low = total.astype(BF16)
        dx1[at, :] = total
        da[at, :] = low
        grads[6] += jnp.sum(low.astype(F32), axis=0, keepdims=True)
        grads[7] += jnp.sum(dy_part, axis=0, keepdims=True)

    norm_back(x1, 1, 23, finish_mlp)
    for c in range(4):
        total = jnp.zeros((rows, 256), F32)
        for g in range(4):
            total += dot_nt(da[:, 256 * g : 256 * g + 256], wo[g, 256 * c : 256 * c + 256, :])
        slope[4 + c] = total.astype(BF16)
    beat(24)

    def heads_back(p, carry):
        @pl.when(lax.rem(p, 4) != 3)
        def _():
            beat(25 + p - p // 4)

        at = lanes(lax.rem(p, 2), 128)
        q_pair, k_pair, v_pair, do_pair = qkv[p], qkv[8 + p], qkv[16 + p], slope[4 + p // 2, :, at]
        k_turned = k_pair.T
        dk = jnp.zeros((rows, 128), F32)
        dv = jnp.zeros((rows, 128), F32)
        dq = jnp.zeros((128, rows), F32)
        for half in range(2):
            mask = half_mask((rows, 128), 1, half)
            q_half = jnp.where(mask, q_pair, jnp.zeros_like(q_pair))
            do_half = jnp.where(mask, do_pair, jnp.zeros_like(do_pair))
            k_half = jnp.where(half_mask((128, rows), 0, half), k_turned, jnp.zeros_like(k_turned))
            scores = dot_nt(k_pair, q_half) + bias[...]
            weights = jnp.exp(scores - lse[p, half])
            grad = dot_nt(v_pair, do_half)
            inner = jnp.sum(weights * grad, axis=0, keepdims=True)
            low = weights.astype(BF16)
            ds = (weights * (grad - inner)).astype(BF16)
            dv += dot_nn(low, do_half)
            dk += dot_nn(ds, q_half)
            dq += dot_nn(k_half, ds)
        for i, value in ((0, dq.T * HDIM ** (-0.5)), (1, dk), (2, dv)):
            low = value.astype(BF16)
            z[4 * i + p // 2, :, at] = low
            if i != 1:
                grads[4 + i // 2, :, lanes(p, 128)] = jnp.sum(low.astype(F32), axis=0, keepdims=True)
        return carry

    lax.fori_loop(0, 8, heads_back, 0)

    def proj_grad(q, carry):
        left, right = h1[:, lanes(q, 256)].T, o[:, lanes(q, 256)].T
        for g in range(4):
            n = 4 * q + g
            flush(2, n)
            for b in range(3):
                stage[g % 2, :, 256 * b : 256 * b + 256] = (dot_nn(left, z[3 * g + b]) * factor).astype(BF16)
            stage[g % 2, :, 768:1024] = (dot_nn(right, da[:, 256 * g : 256 * g + 256]) * factor).astype(BF16)
            stage_copy(2, n).start()
            if g == 1:
                beat(31 + q)
        return carry

    lax.fori_loop(0, 4, proj_grad, 0)
    stage_copy(2, 14).wait()
    stage_copy(2, 15).wait()
    beat(35)
    for c in range(4):
        total = jnp.zeros((rows, 256), F32)
        for g in range(4):
            for b in range(3):
                total += dot_nt(z[3 * g + b], wqkv[g, 256 * c : 256 * c + 256, 256 * b : 256 * b + 256])
        dh[:, 256 * c : 256 * c + 256] = total
        if c % 2 == 1:
            beat(36 + c // 2)

    def finish_attn(at, dx):
        x[at, :] = (dx1[at, :] + dx).astype(BF16)

    norm_back(x, 0, 38, finish_attn)
    out_copies.append(pltpu.make_async_copy(x, gtok_hbm, save_sem.at[4]))
    out_copies[-1].start()
    beat(39)
    tail_copies = []
    for g in range(4):
        tail = stage.at[g // 2, pl.ds(128 * (g % 2), chunk_rows), :]
        tail[...] = jnp.zeros((chunk_rows, WIDE), BF16)
        for i in range(8):
            tail[2 * i : 2 * i + 1, 0:256] = (grads[i, :, 256 * g : 256 * g + 256] * factor).astype(BF16)
        for q in range(4):
            tail[16:17, 256 * q : 256 * q + 256] = (upg[4 * q + g] * factor).astype(BF16)
        tail_copies.append(pltpu.make_async_copy(tail, g_hbm.at[g % 2, g // 2, pl.ds(3072, chunk_rows), :],
                                                 save_sem.at[5 + g]))
        tail_copies[-1].start()
    for copy in tail_copies:
        copy.wait()

    def remaining(t, carry):
        tick(t)
        return carry

    lax.fori_loop(40 // ratio, tick_count, remaining, 0)
    for copy in out_copies:
        copy.wait()
    for w in range(4):
        for copy in (part_sent(w, x_sent, x_peer), part_sent(w, y_sent, y_peer), part_sent(w, z_sent, z_peer),
                     rest_copy(w), far_copy(w), core_copy(w)):
            copy.wait_send()


def layer(dp_size, fsdp_size, group, images, counts, tokens, cotangent, small_params, weights):
    rows = tokens.shape[0]
    chunk_rows = 64 if dp_size <= 32 else 128
    chunk_count = 3072 // chunk_rows + 1
    bit_count = dp_size.bit_length() - 1
    g_rows = 3072 + chunk_rows
    any_space, smem = pl.BlockSpec(memory_space=pl.ANY), pl.BlockSpec(memory_space=pltpu.SMEM)
    sems = lambda *dims: pltpu.SemaphoreType.DMA(dims)
    shape = jax.ShapeDtypeStruct
    return pl.pallas_call(
        functools.partial(layer_kernel, rows, chunk_rows, chunk_count, bit_count, 2.0 / (dp_size * fsdp_size)),
        out_shape=(
            shape((rows, D), BF16), shape((rows, D), BF16), shape((g_rows, WIDE), BF16),
            shape((2, 2, g_rows, WIDE), BF16),
        ),
        in_specs=[smem] * 3 + [any_space] * 11,
        out_specs=(any_space,) * 4,
        scratch_shapes=[pltpu.VMEM((4,) + a.shape, BF16) for a in weights] + [
            pltpu.VMEM((rows, D), BF16),
            pltpu.VMEM((rows, D), BF16),
            pltpu.VMEM((24, rows, 128), BF16),
            pltpu.VMEM((rows, D), BF16),
            pltpu.VMEM((rows, D), F32),
            pltpu.VMEM((rows, D), BF16),
            pltpu.VMEM((16, rows, 256), BF16),
            pltpu.VMEM((16, rows, 256), BF16),
            pltpu.VMEM((rows, D), F32),
            pltpu.VMEM((rows, rows), F32),
            pltpu.VMEM((8, 2, 1, rows), F32),
            pltpu.VMEM((rows, D), BF16),
            pltpu.VMEM((rows, D), F32),
            pltpu.VMEM((rows, D), BF16),
            pltpu.VMEM((2, 256, WIDE), BF16),
            [pltpu.VMEM(a.shape, BF16) for a in small_params],
            pltpu.VMEM((16, 256), F32),
            pltpu.VMEM((4, 16, 256), BF16),
            pltpu.VMEM((8, 1, D), F32),
            pltpu.VMEM((24, 1, 128), F32),
            pltpu.VMEM((16, 1, 256), F32),
            pltpu.VMEM((8, 1, D), F32),
            pltpu.VMEM((16, 1, 256), F32),
            sems(4), sems(2, 3), sems(2, 4),
            sems(COUNT), sems(COUNT), sems(COUNT), sems(4), sems(4), sems(4), sems(4), sems(4),
            sems(2, 4), sems(7), sems(9), sems(2),
            reduce_scratch(chunk_rows, bit_count),
        ],
        compiler_params=pltpu.CompilerParams(collective_id=1, has_side_effects=True, vmem_limit_bytes=VMEM_BYTES),
        name="layer",
    )(group, images, counts, tokens, cotangent, *small_params, *weights)


def widen_kernel(down_ref, up_ref, proj_ref, small_ref, gain_ref, shift_ref, qkv_ref, qvb_ref, wo_ref, outb_ref, wu_ref,
                 upb_ref, wd_ref):
    wd_ref[...] = down_ref[...].astype(F32)
    wu_ref[...] = up_ref[...].T.astype(F32)
    proj = proj_ref[...].astype(F32)
    qkv_ref[...] = proj[:, :768]
    wo_ref[...] = proj[:, 768:]
    small = small_ref[...].astype(F32)
    for i, ref in enumerate((gain_ref, shift_ref, qvb_ref, outb_ref)):
        for j in range(2):
            ref[j : j + 1, :] = small[4 * i + 2 * j : 4 * i + 2 * j + 1, 0:256]
    upb_ref[...] = small[16:17, :]


def widen(total):
    steps = 4
    block = D // steps
    shape = jax.ShapeDtypeStruct
    fixed = lambda *dims: pl.BlockSpec(dims, lambda i: (0, 0))
    return pl.pallas_call(
        widen_kernel,
        grid=(steps,),
        out_shape=(
            shape((2, 256), F32), shape((2, 256), F32), shape((D, 768), F32), shape((2, 256), F32), shape((D, 256), F32),
            shape((2, 256), F32), shape((D, D), F32), shape((1, D), F32), shape((D, D), F32),
        ),
        in_specs=[
            pl.BlockSpec((block, WIDE), lambda i: (i, 0)),
            pl.BlockSpec((block, WIDE), lambda i: (steps + i, 0)),
            pl.BlockSpec((block, WIDE), lambda i: (2 * steps + i, 0)),
            pl.BlockSpec((32, WIDE), lambda i: (3072 // 32, 0)),
        ],
        out_specs=(
            fixed(2, 256), fixed(2, 256), pl.BlockSpec((block, 768), lambda i: (i, 0)), fixed(2, 256),
            pl.BlockSpec((block, 256), lambda i: (i, 0)), fixed(2, 256), pl.BlockSpec((D, block), lambda i: (0, i)),
            fixed(1, D), pl.BlockSpec((block, D), lambda i: (i, 0)),
        ),
        compiler_params=pltpu.CompilerParams(vmem_limit_bytes=32 * 2**20),
        name="widen",
    )(total, total, total, total)


def local(
    tokens,
    cotangent,
    group,
    images,
    counts,
    ln_gain,
    ln_bias,
    w_qkv,
    qv_bias,
    w_out,
    out_bias,
    w_up,
    up_bias,
    w_down,
):
    output, grad_tokens, total, _ = layer(
        lax.axis_size("dp"), lax.axis_size("fsdp"), group, images, counts, tokens, cotangent,
        (ln_gain, ln_bias, qv_bias, out_bias, up_bias.reshape(4, 256)), (w_qkv, w_out, w_up, w_down))
    grads = list(widen(total))
    grads[7] = grads[7].reshape(D)
    return (output, grad_tokens, *grads)


def solution(mesh):
    return jax.shard_map(
        local,
        mesh=mesh,
        in_specs=(
            P(("dp", "fsdp"), None),
            P(("dp", "fsdp"), None),
            P("dp"),
            P("dp", "fsdp"),
            P(),
            P(None, "fsdp"),
            P(None, "fsdp"),
            P(None, "fsdp"),
            P(None, "fsdp"),
            P(None, "fsdp"),
            P(None, "fsdp"),
            P(None, "fsdp"),
            P("fsdp"),
            P("fsdp", None),
        ),
        out_specs=(
            P(("dp", "fsdp"), None),
            P(("dp", "fsdp"), None),
            P(None, "fsdp"),
            P(None, "fsdp"),
            P(None, "fsdp"),
            P(None, "fsdp"),
            P(None, "fsdp"),
            P(None, "fsdp"),
            P(None, "fsdp"),
            P("fsdp"),
            P("fsdp", None),
        ),
        check_vma=False,
    )
```

```python
import functools

import jax
import jax.numpy as jnp
from jax import lax
from jax.experimental import pallas as pl
from jax.experimental.pallas import tpu as pltpu
from jax.sharding import PartitionSpec as P

D = 1024
HDIM = 64
LEN0 = 50
LEN1 = 145
EPSILON = 1e-06
WIDE = 1024
F32 = jnp.float32
BF16 = jnp.bfloat16
MESH = pl.DeviceIdType.MESH
VMEM_BYTES = 64 * 2**20
STAGE_LAGS = (1, 3, 3, 3, 3, 3, 3, 3)
PAIR_EVERY = 8


def split_plan(chunk_rows, bit_count):
    rows, cols, plan = chunk_rows, WIDE, []
    for _ in range(bit_count):
        if rows >= 32:
            rows //= 2
            plan.append(("rows", rows, cols))
        else:
            cols //= 2
            plan.append(("cols", rows, cols))
    return plan


def pipeline_plan(bit_count):
    lags = list(STAGE_LAGS) if bit_count == 3 else [1] * (2 * bit_count + 2)
    return lags[1:], [sum(lags[: i + 1]) for i in range(len(lags))]


def power_of_two(n):
    return 1 << (n - 1).bit_length()


def reduce_scratch(chunk_rows, bit_count):
    plan = split_plan(chunk_rows, bit_count)
    lags, when = pipeline_plan(bit_count)
    held = power_of_two(when[bit_count + 2] - when[0] + 1)
    slots = [power_of_two(2 * lag) for lag in lags]
    half = plan[0][1]
    stages = 2 * bit_count + 1
    return [
        pltpu.VMEM((2, 2, chunk_rows, WIDE), BF16),
        pltpu.VMEM((2, 2, chunk_rows, WIDE), BF16),
        pltpu.VMEM((slots[0], chunk_rows, WIDE), BF16),
        pltpu.VMEM((slots[0], chunk_rows, WIDE), BF16),
        pltpu.VMEM((held, chunk_rows, WIDE), BF16),
        [pltpu.VMEM((slots[1 + b], r, c), BF16) for b, (_, r, c) in enumerate(plan)],
        pltpu.VMEM((2, 2, chunk_rows, WIDE), BF16),
        pltpu.VMEM((2, 2, half, WIDE), BF16),
        pltpu.VMEM((2, half, WIDE), BF16),
        [pltpu.VMEM((2, r, c), BF16) for _, r, c in plan[1:]],
        pltpu.SemaphoreType.DMA((2,)),
        pltpu.SemaphoreType.DMA((2, 2)),
        [pltpu.SemaphoreType.DMA((2, slots[i])) for i in range(stages)],
        [pltpu.SemaphoreType.DMA((2, 2)) for _ in range(stages)],
        pltpu.SemaphoreType.DMA((4,)),
        pltpu.SemaphoreType.DMA((2,)),
    ]


def greet(peers):
    barrier = pltpu.get_barrier_semaphore()
    for peer in peers:
        pl.semaphore_signal(barrier, inc=1, device_id=peer, device_id_type=MESH)
    pl.semaphore_wait(barrier, len(peers))


def reduction(chunk_rows, chunk_count, bit_count, g_ref, out_ref, load, core_in, x_out, x_in, acc, bit_in,
              pair, pair_in, pair_x_in, pair_bit_in, load_sem, core_sem, main_sems, pair_sems, main_own_sem, pair_own_sem):
    dp, f = lax.axis_index("dp"), lax.axis_index("fsdp")
    core, across = lax.rem(f, 2), f // 2
    plan = split_plan(chunk_rows, bit_count)
    lags, when = pipeline_plan(bit_count)
    slot = lambda stage, j: lax.rem(j, power_of_two(2 * lags[stage]))
    held = lambda j: lax.rem(j, acc.shape[0])
    pair_slot = lambda j: lax.rem(j // PAIR_EVERY, 2)
    bits = [lax.rem(dp // (1 << b), 2) for b in range(bit_count)]
    flips = [dp + (1 - 2 * bits[b]) * (1 << b) for b in range(bit_count)]
    core_peer = (dp, f + 1 - 2 * core)
    x_peer = (dp, f + 2 - 4 * across)
    peers = [core_peer, x_peer] + [(p, f) for p in flips]
    main_order = list(range(bit_count))
    pair_order = [1, 0] + main_order[2:]

    def region(level, other, order):
        row, col, rows, cols = 0, 0, chunk_rows, WIDE
        for i in range(level):
            kind, rows, cols = plan[i]
            bit = bits[order[i]]
            if other and i == level - 1:
                bit = 1 - bit
            if kind == "rows":
                row = row + bit * rows
            else:
                col = col + bit * cols
        return row, rows, col, cols

    def cut(ref, lead, base, level, other, order):
        row, rows, col, cols = region(level, other, order)
        row_slice = pl.ds(pl.multiple_of(base + row, 16), rows)
        col_slice = slice(None) if cols == WIDE else pl.ds(pl.multiple_of(col, 128), cols)
        return ref.at[lead + (row_slice, col_slice)]

    def rows_of(j):
        return pl.ds(pl.multiple_of(j * chunk_rows, chunk_rows), chunk_rows)

    def remote(src, dst, sems, s, peer):
        return pltpu.make_async_remote_copy(src, dst, sems.at[0, s], sems.at[1, s], device_id=peer,
                                            device_id_type=MESH)

    def load_copy(j):
        s = lax.rem(j, 2)
        return pltpu.make_async_copy(g_ref.at[core, :, rows_of(j), :], load.at[s], load_sem.at[s])

    def core_copy(j):
        s = lax.rem(j, 2)
        return remote(g_ref.at[1 - core, :, rows_of(j), :], core_in.at[s], core_sem, s, core_peer)

    def spread_copy(j, i, source, order, sems, s):
        mine = cut(out_ref, (), j * chunk_rows, i + 1, False, order)
        return remote(source if i == bit_count - 1 else mine, mine, sems, s, (flips[order[i]], f))

    def main_part(j, level, other):
        return cut(acc, (held(j),), 0, level, other, main_order)

    def main_own(j):
        return pltpu.make_async_copy(main_part(j, bit_count, False),
                                     cut(out_ref, (), j * chunk_rows, bit_count, False, main_order),
                                     main_own_sem.at[lax.rem(j, 4)])

    def main_copy(stage, j):
        s, sems = slot(stage, j), main_sems[stage]
        if stage == 0:
            return remote(x_out.at[s], x_in.at[s], sems, s, x_peer)
        if stage <= bit_count:
            b = stage - 1
            return remote(main_part(j, b + 1, True), bit_in[b].at[s], sems, s, (flips[b], f))
        return spread_copy(j, 2 * bit_count - stage, main_part(j, bit_count, False), main_order, sems, s)

    def main_core(j):
        s = lax.rem(j, 2)
        for piece, target in ((1 - across, x_out.at[slot(0, j)]), (across, acc.at[held(j)])):
            target[...] = load[s, piece] + core_in[s, piece]
        main_copy(0, j).start()

    def main_take(stage, j):
        main_copy(stage, j).wait()
        if stage == 0:
            acc[held(j)] = acc[held(j)] + x_in[slot(0, j)]
        elif stage <= bit_count:
            part = main_part(j, stage, False)
            part[...] = part[...] + bit_in[stage - 1][slot(stage, j)]
        elif stage == bit_count + 1:
            main_own(j).wait()
        if stage == bit_count:
            main_own(j).start()
        if stage < 2 * bit_count:
            main_copy(stage + 1, j).start()

    def pair_part(j, level, other):
        return cut(pair, (pair_slot(j), across), 0, level, other, pair_order)

    def pair_own(j):
        return pltpu.make_async_copy(pair_part(j, bit_count, False),
                                     cut(out_ref, (), j * chunk_rows, bit_count, False, pair_order),
                                     pair_own_sem.at[pair_slot(j)])

    def pair_copy(stage, j):
        s, sems = pair_slot(j), pair_sems[stage]
        if stage == 0:
            return remote(cut(pair, (s, slice(None)), 0, 1, True, pair_order), pair_in.at[s], sems, s, (flips[1], f))
        if stage == 1:
            return remote(cut(pair, (s, 1 - across), 0, 1, False, pair_order), pair_x_in.at[s], sems, s, x_peer)
        if stage <= bit_count:
            return remote(pair_part(j, stage, True), pair_bit_in[stage - 2].at[s], sems, s,
                          (flips[pair_order[stage - 1]], f))
        return spread_copy(j, 2 * bit_count - stage, pair_part(j, bit_count, False), pair_order, sems, s)

    def pair_core(j):
        s = lax.rem(j, 2)
        pair[pair_slot(j)] = load[s] + core_in[s]
        pair_copy(0, j).start()

    def pair_take(stage, j):
        s = pair_slot(j)
        pair_copy(stage, j).wait()
        if stage == 0:
            part = cut(pair, (s, slice(None)), 0, 1, False, pair_order)
            part[...] = part[...] + pair_in[s]
        elif stage == 1:
            part = pair_part(j, 1, False)
            part[...] = part[...] + pair_x_in[s]
        elif stage <= bit_count:
            part = pair_part(j, stage, False)
            part[...] = part[...] + pair_bit_in[stage - 2][s]
        elif stage == bit_count + 1:
            pair_own(j).wait()
        if stage == bit_count:
            pair_own(j).start()
        if stage < 2 * bit_count:
            pair_copy(stage + 1, j).start()

    def guarded(t, delay, *actions):
        j = t - delay
        inside = jnp.logical_and(j >= 0, j < chunk_count)
        chosen = lax.rem(j, PAIR_EVERY) == 3
        for action, choice in zip(actions, (jnp.logical_not(chosen), chosen)):
            @pl.when(jnp.logical_and(inside, choice) if len(actions) > 1 else inside)
            def _(action=action):
                action(j)

    def on_core(take):
        def action(j):
            load_copy(j).wait()
            core_copy(j).wait()
            take(j)
        return action

    def on_start(j):
        load_copy(j).start()
        core_copy(j).start()

    def tick(t):
        for stage in reversed(range(2 * bit_count + 1)):
            guarded(t, when[stage + 1], functools.partial(main_take, stage), functools.partial(pair_take, stage))
        guarded(t, when[0], on_core(main_core), on_core(pair_core))
        guarded(t, 0, on_start)

    return tick, chunk_count + when[-1], peers


def dot_nn(a, b):
    return lax.dot_general(a, b, (((1,), (0,)), ((), ())), preferred_element_type=F32)


def dot_nt(a, b):
    return lax.dot_general(a, b, (((1,), (1,)), ((), ())), preferred_element_type=F32)


def lanes(index, width):
    return pl.ds(pl.multiple_of(index * width, width), width)


def half_mask(shape, dim, half):
    spot = lax.broadcasted_iota(jnp.int32, shape, dim)
    return spot < HDIM if half == 0 else spot >= HDIM


def fill_bias(bias, inverse, limit, rows):
    step = 128

    def segments(dim, shape, start):
        place = (lax.broadcasted_iota(jnp.int32, shape, dim) + start).astype(F32)
        return jnp.where(place < limit, jnp.floor((place + 0.5) * inverse), float(rows))

    for i in range(rows // step):
        same = segments(0, (step, rows), i * step) == segments(1, (step, rows), 0)
        bias[i * step : (i + 1) * step, :] = jnp.where(same, 0.0, -1e30)


ERF_TERMS = (1.061405429, -1.453152027, 1.421413741, -0.284496736, 0.254829592)


def normal_share(u):
    fall = jnp.exp(u * u * -0.5)
    t = 1.0 / (1.0 + jnp.abs(u) * (0.3275911 * 0.5 ** 0.5))
    series = ERF_TERMS[0] * t
    for c in ERF_TERMS[1:-1]:
        series = (series + c) * t
    tail = 0.5 * (series + ERF_TERMS[-1]) * t * fall
    return jnp.where(u < 0.0, tail, 1.0 - tail), fall


PARTS = 3
PART_ROWS = 336
PIECE_ROWS = 48
PIECES = PART_ROWS // PIECE_ROWS
COUNT = 4 * PIECES
REST = PARTS * PART_ROWS
WINDOWS = (2, 4)
Y_LAG = Z_LAG = 2


def layer_kernel(rows, chunk_rows, chunk_count, bit_count, share, group_ref, images_ref, counts_ref, tok_hbm, cot_hbm,
                 gain_hbm, shift_hbm, qvb_hbm, outb_hbm, upb_hbm, sqkv, so, su, sd,
                 out_hbm, gtok_hbm, sum_hbm, g_hbm,
                 wqkv, wo, wu, wd, x, h1, qkv, o, x1, h2, z, slope, y, bias, lse, dy, dh, da, stage,
                 smalls, pack, vec, vecs, qv, upb, grads, upg,
                 own_sem, vec_sem, rest_sem, x_sem, y_sem, z_sem, x_sent, y_sent, z_sent, far_sent, far_sem, core_sem,
                 load_sem, save_sem, stage_sem, comm):
    tick, tick_count, peers = reduction(chunk_rows, chunk_count, bit_count, g_hbm, sum_hbm, *comm)
    ratio = chunk_rows // 64

    def beat(i):
        if ratio == 1:
            tick(i)
        else:
            @pl.when(lax.rem(i, ratio) == ratio - 1)
            def _():
                tick(i // ratio)

    dp, f = lax.axis_index("dp"), lax.axis_index("fsdp")
    core, across = lax.rem(f, 2), f // 2
    yb, zb = lax.rem(dp, 2), lax.rem(dp // 2, 2)
    core_f, x_f, diag_f = f + 1 - 2 * core, f + 2 - 4 * across, 3 - f
    core_peer, x_peer, diag_peer = (dp, core_f), (dp, x_f), (dp, diag_f)
    y_peer, z_peer = (dp + 1 - 2 * yb, f), (dp + 2 - 4 * zb, f)
    part_x = yb + (1 - yb) * 2 * zb
    part_y = (1 - yb) + yb * 2 * zb
    part_z = 2 - 2 * zb
    shards, full = (sqkv, so, su, sd), (wqkv, wo, wu, wd)

    def order(i):
        return 2 * lax.rem(across + i // 2, 2) + lax.rem(core + i, 2)

    def remote(src, dst, sems, slot, peer):
        return pltpu.make_async_remote_copy(src, dst, sems.at[0, slot], sems.at[1, slot], device_id=peer,
                                            device_id_type=MESH)

    def part(k, index):
        return pl.ds(pl.multiple_of(index * PART_ROWS + (k % PIECES) * PIECE_ROWS, 16), PIECE_ROWS)

    rest = pl.ds(REST, D - REST)

    def piece_copy(src, dst, send, receive, peer):
        return pltpu.make_async_remote_copy(src, dst, send, receive, device_id=peer, device_id_type=MESH)

    def x_copy(k):
        w, at = k // PIECES, part(k, part_x)
        return piece_copy(shards[w].at[at, :], full[w].at[f, at, :], x_sent.at[w], x_sem.at[k], x_peer)

    def hop(k, index, send, receive, peer):
        place = full[k // PIECES].at[x_f, part(k, index), :]
        return piece_copy(place, place, send.at[k // PIECES], receive, peer)

    y_copy = lambda k: hop(k, part_x, y_sent, y_sem.at[k], y_peer)
    z_copy = lambda k: hop(k, 2 * zb, z_sent, z_sem.at[k], z_peer)
    fx_copy = lambda k: hop(k, part_x, far_sent, far_sem.at[k // PIECES], core_peer)
    fy_copy = lambda k: hop(k, part_y, far_sent, far_sem.at[k // PIECES], core_peer)
    fz_copy = lambda k: hop(k, part_z, far_sent, far_sem.at[k // PIECES], core_peer)

    def rest_copy(w):
        return remote(shards[w].at[rest, :], full[w].at[f, rest, :], rest_sem, w, x_peer)

    def frest_copy(w):
        place = full[w].at[x_f, rest, :]
        return piece_copy(place, place, far_sent.at[w], far_sem.at[w], core_peer)

    def far_copy(w):
        return piece_copy(full[w].at[x_f], full[w].at[x_f], far_sent.at[w], far_sem.at[w], core_peer)

    def part_sent(w, sent, peer):
        place = full[w].at[x_f, pl.ds(0, PART_ROWS), :]
        return piece_copy(place, place, sent.at[w], x_sem.at[0], peer)

    def core_copy(w):
        return remote(shards[w], full[w].at[f], core_sem, w, core_peer)

    def own_copy(w):
        return pltpu.make_async_copy(shards[w], full[w].at[f], own_sem.at[w])

    sent = []

    def feed(until):
        while len(sent) < min(until, COUNT):
            x_copy(len(sent)).start()
            sent.append(True)

    def service(k):
        i = k - Y_LAG - Z_LAG
        if 0 <= i < COUNT:
            z_copy(i).wait_recv()
            fz_copy(i).start()
        i = k - Y_LAG
        if 0 <= i < COUNT:
            y_copy(i).wait_recv()
            fy_copy(i).start()

            @pl.when(yb == 1)
            def _():
                z_copy(i).start()
        if k < COUNT:
            x_copy(k).wait_recv()
            y_copy(k).start()

            @pl.when(yb == 0)
            def _():
                z_copy(k).start()

            fx_copy(k).start()
            feed(k + 1 + WINDOWS[k >= PIECES - 2])
            if k % PIECES == 0:
                w = k // PIECES
                rest_copy(w).wait_recv()
                frest_copy(w).start()

    def services(index, plan):
        for i, k in plan:
            @pl.when(index == i)
            def _(k=k):
                service(k)

    def arrived(w):
        far_copy(w).wait_recv()

    loads = [pltpu.make_async_copy(src, dst, load_sem.at[i]) for i, (src, dst) in enumerate(
        [(gain_hbm, smalls[0]), (shift_hbm, smalls[1]), (qvb_hbm, smalls[2]), (outb_hbm, smalls[3]), (upb_hbm, smalls[4]),
         (tok_hbm, x), (cot_hbm, dy)])]
    for copy in loads:
        copy.start()
    own_copy(0).start()
    greet(peers + [diag_peer])
    for copy in loads[:5]:
        copy.wait()
    pack[...] = jnp.zeros_like(pack)
    for i in range(4):
        pack[2 * i : 2 * i + 2, :] = smalls[i][...].astype(F32)
    pack[8:12, :] = smalls[4][...].astype(F32)
    vec[f] = pack[...].astype(BF16)
    vec_copies = [remote(vec.at[f], vec.at[f], vec_sem, i, peer)
                  for i, peer in enumerate((core_peer, x_peer, diag_peer))]
    for copy in vec_copies:
        copy.start()
    feed(WINDOWS[0])
    core_copy(0).start()
    for w in range(4):
        rest_copy(w).start()
    for w in range(1, 4):
        own_copy(w).start()

    first = group_ref[0] == 0
    length = jnp.where(first, LEN0, LEN1)
    inverse = jnp.where(first, 1.0 / LEN0, 1.0 / LEN1).astype(F32)
    limit = (images_ref[0, 0] * length).astype(F32)
    mine = jnp.where(first, counts_ref[0], counts_ref[1])
    fraction = jnp.full((1, 128), mine, jnp.int32).astype(F32) / jnp.full(
        (1, 128), counts_ref[0] + counts_ref[1], jnp.int32).astype(F32)
    factor = fraction[0:1, 0:1] * share
    fill_bias(bias, inverse, limit, rows)
    for copy in vec_copies:
        copy.wait()
    service(0)
    qv[...] = jnp.zeros_like(qv)
    for g in range(4):
        wide = vec[g].astype(F32)
        for i in range(8):
            vecs[i, :, 256 * g : 256 * g + 256] = wide[i : i + 1, :]
        for i in range(4):
            upb[4 * g + i] = wide[8 + i : 9 + i, :]
        for i in range(2):
            qv[2 * g + i] = wide[4:5, 128 * i : 128 * i + 128]
            qv[16 + 2 * g + i] = wide[5:6, 128 * i : 128 * i + 128]

    step = 64

    def normalize(value, which):
        center = value - jnp.mean(value, axis=-1, keepdims=True)
        spread = jnp.mean(center * center, axis=-1, keepdims=True)
        return (center * lax.rsqrt(spread + EPSILON) * vecs[which] + vecs[2 + which]).astype(BF16)

    loads[5].wait()

    def norm_in(i, carry):
        at = pl.ds(pl.multiple_of(i * step, step), step)
        h1[at, :] = normalize(x[at, :].astype(F32), 0)
        return carry

    lax.fori_loop(0, rows // step, norm_in, 0)
    service(1)

    def project(i):
        product = dot_nn(h1[...], wqkv[order(i)])
        for b in range(6):
            block = 6 * order(i) + b
            scale = jnp.where(block < 8, HDIM ** (-0.5), 1.0).astype(F32)
            qkv[block] = ((product[:, 128 * b : 128 * b + 128] + qv[block]) * scale).astype(BF16)

    own_copy(0).wait()
    project(0)
    service(2)
    core_copy(0).wait_recv()
    project(1)
    for k in range(3, PIECES + Y_LAG + Z_LAG + 1):
        service(k)
    for w in range(1, 4):
        core_copy(w).start()
    loads[6].wait()
    live = lax.broadcasted_iota(jnp.int32, (rows, D), 0).astype(F32) < limit
    dy[...] = jnp.where(live, dy[...].astype(F32), 0.0).astype(BF16)
    arrived(0)
    project(2)
    service(12)
    project(3)
    service(13)

    def heads(p, carry):
        services(p, ((1, 14), (2, 15), (4, 16), (5, 17), (7, 18)))
        q_pair, k_pair, v_turned = qkv[p], qkv[8 + p], qkv[16 + p].T
        total = jnp.zeros((128, rows), F32)
        for half in range(2):
            q_half = jnp.where(half_mask((rows, 128), 1, half), q_pair, jnp.zeros_like(q_pair))
            v_half = jnp.where(half_mask((128, rows), 0, half), v_turned, jnp.zeros_like(v_turned))
            scores = dot_nt(k_pair, q_half) + bias[...]
            highest = jnp.max(scores, axis=0, keepdims=True)
            weights = jnp.exp(scores - highest)
            sums = jnp.sum(weights, axis=0, keepdims=True)
            total += dot_nn(v_half, weights.astype(BF16)) * (1.0 / sums)
            lse[p, half] = highest + jnp.log(sums)
        o[:, lanes(p, 128)] = total.T.astype(BF16)
        return carry

    lax.fori_loop(0, 8, heads, 0)
    for w in range(1, 4):
        own_copy(w).wait()
        core_copy(w).wait_recv()
    service(19)
    arrived(1)
    for g in range(4):
        at = slice(256 * g, 256 * g + 256)
        x1[:, at] = x[:, at].astype(F32) + dot_nn(o[...], wo[g]) + vecs[6, :, at]
    service(20)

    def norm_mid(i, carry):
        at = pl.ds(pl.multiple_of(i * step, step), step)
        value = x1[at, :]
        h2[at, :] = normalize(value, 1)
        y[at, :] = value + vecs[7]
        return carry

    lax.fori_loop(0, rows // step, norm_mid, 0)
    service(21)

    def hidden(q, i):
        g = order(i)
        n = 4 * q + g
        u = dot_nn(h2[...], wu[g, :, lanes(q, 256)]) + upb[4 * g + q]
        bell, fall = normal_share(u)
        z[n] = (u * bell).astype(BF16)
        slope[n] = (bell + u * (fall * 0.3989422804014327)).astype(BF16)

    def hidden_near(i, carry):
        services(i, ((0, 22), (1, 23), (3, 24)))
        hidden(i // 2, lax.rem(i, 2))
        return carry

    lax.fori_loop(0, 4, hidden_near, 0)
    arrived(2)

    def hidden_far(i, carry):
        hidden(0, 2 + i)
        return carry

    lax.fori_loop(0, 2, hidden_far, 0)
    service(25)

    def stage_copy(which, n):
        s, q, g = lax.rem(n, 2), n // 4, lax.rem(n, 4)
        at = pl.ds(pl.multiple_of(which * D + q * 256, 256), 256)
        return pltpu.make_async_copy(stage.at[s], g_hbm.at[lax.rem(g, 2), g // 2, at, :], stage_sem.at[s])

    def flush(which, n, start=0):
        @pl.when(n >= start + 2)
        def _():
            stage_copy(which, n - 2).wait()

    def down_grad(n, start):
        flush(0, n, start)
        stage[lax.rem(n, 2)] = (dot_nn(z[n].T, dy[...]) * factor).astype(BF16)
        stage_copy(0, n).start()

    def down_first(n, carry):
        services(n, ((1, 26), (3, 27)))
        down_grad(n, 0)
        return carry

    lax.fori_loop(0, 4, down_first, 0)
    stage_copy(0, 2).wait()
    stage_copy(0, 3).wait()
    beat(0)

    def down_block(q, carry):
        def units(i, inner):
            services(4 * q + i, ((6, 28), (7, 29)))

            @pl.when(4 * q + i >= 6)
            def _():
                hidden(q, i)

            for spot, t in ((7, 1), (14, 6)):
                @pl.when(4 * q + i == spot)
                def _(t=t):
                    beat(t)
            return inner

        def grads_of(g, inner):
            n = 4 * q + g
            services(n, ((5, 30), (6, 31)))
            down_grad(n, 4)
            for spot, t in ((5, 2), (7, 3), (9, 4), (11, 5), (13, 7), (15, 8)):
                @pl.when(n == spot)
                def _(t=t):
                    beat(t)
            return inner

        lax.fori_loop(0, 4, units, 0)
        lax.fori_loop(0, 4, grads_of, 0)
        return carry

    lax.fori_loop(1, 4, down_block, 0)
    stage_copy(0, 14).wait()
    stage_copy(0, 15).wait()
    arrived(3)
    dh[...] = jnp.zeros_like(dh)

    def ffn_back(n, carry):
        q, g = n // 4, lax.rem(n, 4)
        flush(1, n)

        @pl.when(jnp.logical_or(n == 0, lax.rem(n, 5) != 0))
        def _():
            beat(9 + n - n // 5)

        du = dot_nt(dy[...], wd[g, lanes(q, 256), :]) * slope[n].astype(F32)
        low = du.astype(BF16)
        upg[n] = jnp.sum(low.astype(F32), axis=0, keepdims=True)
        stage[lax.rem(n, 2)] = (dot_nn(low.T, h2[...]) * factor).astype(BF16)
        stage_copy(1, n).start()
        dh[...] += dot_nt(low, wu[g, :, lanes(q, 256)])
        y[...] += dot_nn(z[n], wd[g, lanes(q, 256), :])
        return carry

    lax.fori_loop(0, 16, ffn_back, 0)
    stage_copy(1, 14).wait()
    stage_copy(1, 15).wait()
    out_copies = []
    for c in range(4):
        slope[c] = y[:, 256 * c : 256 * c + 256].astype(BF16)
        out_copies.append(pltpu.make_async_copy(slope.at[c], out_hbm.at[:, pl.ds(256 * c, 256)], save_sem.at[c]))
        out_copies[-1].start()
    beat(22)
    grads[...] = jnp.zeros_like(grads)

    def norm_back(base_ref, which, first_beat, finish):
        def body(i, carry):
            at = pl.ds(pl.multiple_of(i * step, step), step)
            v = base_ref[at, :].astype(F32)
            center = v - jnp.mean(v, axis=-1, keepdims=True)
            rstd = lax.rsqrt(jnp.mean(center * center, axis=-1, keepdims=True) + EPSILON)
            hat = center * rstd
            grad = dh[at, :]
            grads[which] += jnp.sum(grad * hat, axis=0, keepdims=True)
            grads[2 + which] += jnp.sum(grad, axis=0, keepdims=True)
            scaled = grad * vecs[which]
            finish(at, rstd * (scaled - jnp.mean(scaled, axis=-1, keepdims=True)
                               - hat * jnp.mean(scaled * hat, axis=-1, keepdims=True)))

            @pl.when(i == 4)
            def _():
                beat(first_beat)

            return carry

        lax.fori_loop(0, rows // step, body, 0)

    dx1 = y

    def finish_mlp(at, dx):
        dy_part = dy[at, :].astype(F32)
        total = dy_part + dx
        low = total.astype(BF16)
        dx1[at, :] = total
        da[at, :] = low
        grads[6] += jnp.sum(low.astype(F32), axis=0, keepdims=True)
        grads[7] += jnp.sum(dy_part, axis=0, keepdims=True)

    norm_back(x1, 1, 23, finish_mlp)
    for c in range(4):
        total = jnp.zeros((rows, 256), F32)
        for g in range(4):
            total += dot_nt(da[:, 256 * g : 256 * g + 256], wo[g, 256 * c : 256 * c + 256, :])
        slope[4 + c] = total.astype(BF16)
    beat(24)

    def heads_back(p, carry):
        @pl.when(lax.rem(p, 4) != 3)
        def _():
            beat(25 + p - p // 4)

        at = lanes(lax.rem(p, 2), 128)
        q_pair, k_pair, v_pair, do_pair = qkv[p], qkv[8 + p], qkv[16 + p], slope[4 + p // 2, :, at]
        k_turned = k_pair.T
        dk = jnp.zeros((rows, 128), F32)
        dv = jnp.zeros((rows, 128), F32)
        dq = jnp.zeros((128, rows), F32)
        for half in range(2):
            mask = half_mask((rows, 128), 1, half)
            q_half = jnp.where(mask, q_pair, jnp.zeros_like(q_pair))
            do_half = jnp.where(mask, do_pair, jnp.zeros_like(do_pair))
            k_half = jnp.where(half_mask((128, rows), 0, half), k_turned, jnp.zeros_like(k_turned))
            scores = dot_nt(k_pair, q_half) + bias[...]
            weights = jnp.exp(scores - lse[p, half])
            grad = dot_nt(v_pair, do_half)
            inner = jnp.sum(weights * grad, axis=0, keepdims=True)
            low = weights.astype(BF16)
            ds = (weights * (grad - inner)).astype(BF16)
            dv += dot_nn(low, do_half)
            dk += dot_nn(ds, q_half)
            dq += dot_nn(k_half, ds)
        for i, value in ((0, dq.T * HDIM ** (-0.5)), (1, dk), (2, dv)):
            low = value.astype(BF16)
            z[4 * i + p // 2, :, at] = low
            if i != 1:
                grads[4 + i // 2, :, lanes(p, 128)] = jnp.sum(low.astype(F32), axis=0, keepdims=True)
        return carry

    lax.fori_loop(0, 8, heads_back, 0)

    def proj_grad(q, carry):
        left, right = h1[:, lanes(q, 256)].T, o[:, lanes(q, 256)].T
        for g in range(4):
            n = 4 * q + g
            flush(2, n)
            for b in range(3):
                stage[g % 2, :, 256 * b : 256 * b + 256] = (dot_nn(left, z[3 * g + b]) * factor).astype(BF16)
            stage[g % 2, :, 768:1024] = (dot_nn(right, da[:, 256 * g : 256 * g + 256]) * factor).astype(BF16)
            stage_copy(2, n).start()
            if g == 1:
                beat(31 + q)
        return carry

    lax.fori_loop(0, 4, proj_grad, 0)
    stage_copy(2, 14).wait()
    stage_copy(2, 15).wait()
    beat(35)
    for c in range(4):
        total = jnp.zeros((rows, 256), F32)
        for g in range(4):
            for b in range(3):
                total += dot_nt(z[3 * g + b], wqkv[g, 256 * c : 256 * c + 256, 256 * b : 256 * b + 256])
        dh[:, 256 * c : 256 * c + 256] = total
        if c % 2 == 1:
            beat(36 + c // 2)

    def finish_attn(at, dx):
        x[at, :] = (dx1[at, :] + dx).astype(BF16)

    norm_back(x, 0, 38, finish_attn)
    out_copies.append(pltpu.make_async_copy(x, gtok_hbm, save_sem.at[4]))
    out_copies[-1].start()
    beat(39)
    tail_copies = []
    for g in range(4):
        tail = stage.at[g // 2, pl.ds(128 * (g % 2), chunk_rows), :]
        tail[...] = jnp.zeros((chunk_rows, WIDE), BF16)
        for i in range(8):
            tail[2 * i : 2 * i + 1, 0:256] = (grads[i, :, 256 * g : 256 * g + 256] * factor).astype(BF16)
        for q in range(4):
            tail[16:17, 256 * q : 256 * q + 256] = (upg[4 * q + g] * factor).astype(BF16)
        tail_copies.append(pltpu.make_async_copy(tail, g_hbm.at[g % 2, g // 2, pl.ds(3072, chunk_rows), :],
                                                 save_sem.at[5 + g]))
        tail_copies[-1].start()
    for copy in tail_copies:
        copy.wait()

    def remaining(t, carry):
        tick(t)
        return carry

    lax.fori_loop(40 // ratio, tick_count, remaining, 0)
    for copy in out_copies:
        copy.wait()
    for w in range(4):
        for copy in (part_sent(w, x_sent, x_peer), part_sent(w, y_sent, y_peer), part_sent(w, z_sent, z_peer),
                     rest_copy(w), far_copy(w), core_copy(w)):
            copy.wait_send()


def layer(dp_size, fsdp_size, group, images, counts, tokens, cotangent, small_params, weights):
    rows = tokens.shape[0]
    chunk_rows = 64 if dp_size <= 32 else 128
    chunk_count = 3072 // chunk_rows + 1
    bit_count = dp_size.bit_length() - 1
    g_rows = 3072 + chunk_rows
    any_space, smem = pl.BlockSpec(memory_space=pl.ANY), pl.BlockSpec(memory_space=pltpu.SMEM)
    sems = lambda *dims: pltpu.SemaphoreType.DMA(dims)
    shape = jax.ShapeDtypeStruct
    return pl.pallas_call(
        functools.partial(layer_kernel, rows, chunk_rows, chunk_count, bit_count, 2.0 / (dp_size * fsdp_size)),
        out_shape=(
            shape((rows, D), BF16), shape((rows, D), BF16), shape((g_rows, WIDE), BF16),
            shape((2, 2, g_rows, WIDE), BF16),
        ),
        in_specs=[smem] * 3 + [any_space] * 11,
        out_specs=(any_space,) * 4,
        scratch_shapes=[pltpu.VMEM((4,) + a.shape, BF16) for a in weights] + [
            pltpu.VMEM((rows, D), BF16),
            pltpu.VMEM((rows, D), BF16),
            pltpu.VMEM((24, rows, 128), BF16),
            pltpu.VMEM((rows, D), BF16),
            pltpu.VMEM((rows, D), F32),
            pltpu.VMEM((rows, D), BF16),
            pltpu.VMEM((16, rows, 256), BF16),
            pltpu.VMEM((16, rows, 256), BF16),
            pltpu.VMEM((rows, D), F32),
            pltpu.VMEM((rows, rows), F32),
            pltpu.VMEM((8, 2, 1, rows), F32),
            pltpu.VMEM((rows, D), BF16),
            pltpu.VMEM((rows, D), F32),
            pltpu.VMEM((rows, D), BF16),
            pltpu.VMEM((2, 256, WIDE), BF16),
            [pltpu.VMEM(a.shape, BF16) for a in small_params],
            pltpu.VMEM((16, 256), F32),
            pltpu.VMEM((4, 16, 256), BF16),
            pltpu.VMEM((8, 1, D), F32),
            pltpu.VMEM((24, 1, 128), F32),
            pltpu.VMEM((16, 1, 256), F32),
            pltpu.VMEM((8, 1, D), F32),
            pltpu.VMEM((16, 1, 256), F32),
            sems(4), sems(2, 3), sems(2, 4),
            sems(COUNT), sems(COUNT), sems(COUNT), sems(4), sems(4), sems(4), sems(4), sems(4),
            sems(2, 4), sems(7), sems(9), sems(2),
            reduce_scratch(chunk_rows, bit_count),
        ],
        compiler_params=pltpu.CompilerParams(collective_id=1, has_side_effects=True, vmem_limit_bytes=VMEM_BYTES),
        name="layer",
    )(group, images, counts, tokens, cotangent, *small_params, *weights)


def widen_kernel(down_ref, up_ref, proj_ref, small_ref, gain_ref, shift_ref, qkv_ref, qvb_ref, wo_ref, outb_ref, wu_ref,
                 upb_ref, wd_ref):
    wd_ref[...] = down_ref[...].astype(F32)
    wu_ref[...] = up_ref[...].T.astype(F32)
    proj = proj_ref[...].astype(F32)
    qkv_ref[...] = proj[:, :768]
    wo_ref[...] = proj[:, 768:]
    small = small_ref[...].astype(F32)
    for i, ref in enumerate((gain_ref, shift_ref, qvb_ref, outb_ref)):
        for j in range(2):
            ref[j : j + 1, :] = small[4 * i + 2 * j : 4 * i + 2 * j + 1, 0:256]
    upb_ref[...] = small[16:17, :]


def widen(total):
    steps = 4
    block = D // steps
    shape = jax.ShapeDtypeStruct
    fixed = lambda *dims: pl.BlockSpec(dims, lambda i: (0, 0))
    return pl.pallas_call(
        widen_kernel,
        grid=(steps,),
        out_shape=(
            shape((2, 256), F32), shape((2, 256), F32), shape((D, 768), F32), shape((2, 256), F32), shape((D, 256), F32),
            shape((2, 256), F32), shape((D, D), F32), shape((1, D), F32), shape((D, D), F32),
        ),
        in_specs=[
            pl.BlockSpec((block, WIDE), lambda i: (i, 0)),
            pl.BlockSpec((block, WIDE), lambda i: (steps + i, 0)),
            pl.BlockSpec((block, WIDE), lambda i: (2 * steps + i, 0)),
            pl.BlockSpec((32, WIDE), lambda i: (3072 // 32, 0)),
        ],
        out_specs=(
            fixed(2, 256), fixed(2, 256), pl.BlockSpec((block, 768), lambda i: (i, 0)), fixed(2, 256),
            pl.BlockSpec((block, 256), lambda i: (i, 0)), fixed(2, 256), pl.BlockSpec((D, block), lambda i: (0, i)),
            fixed(1, D), pl.BlockSpec((block, D), lambda i: (i, 0)),
        ),
        compiler_params=pltpu.CompilerParams(vmem_limit_bytes=32 * 2**20),
        name="widen",
    )(total, total, total, total)


def local(
    tokens,
    cotangent,
    group,
    images,
    counts,
    ln_gain,
    ln_bias,
    w_qkv,
    qv_bias,
    w_out,
    out_bias,
    w_up,
    up_bias,
    w_down,
):
    output, grad_tokens, total, _ = layer(
        lax.axis_size("dp"), lax.axis_size("fsdp"), group, images, counts, tokens, cotangent,
        (ln_gain, ln_bias, qv_bias, out_bias, up_bias.reshape(4, 256)), (w_qkv, w_out, w_up, w_down))
    grads = list(widen(total))
    grads[7] = grads[7].reshape(D)
    return (output, grad_tokens, *grads)


def solution(mesh):
    return jax.shard_map(
        local,
        mesh=mesh,
        in_specs=(
            P(("dp", "fsdp"), None),
            P(("dp", "fsdp"), None),
            P("dp"),
            P("dp", "fsdp"),
            P(),
            P(None, "fsdp"),
            P(None, "fsdp"),
            P(None, "fsdp"),
            P(None, "fsdp"),
            P(None, "fsdp"),
            P(None, "fsdp"),
            P(None, "fsdp"),
            P("fsdp"),
            P("fsdp", None),
        ),
        out_specs=(
            P(("dp", "fsdp"), None),
            P(("dp", "fsdp"), None),
            P(None, "fsdp"),
            P(None, "fsdp"),
            P(None, "fsdp"),
            P(None, "fsdp"),
            P(None, "fsdp"),
            P(None, "fsdp"),
            P(None, "fsdp"),
            P("fsdp"),
            P("fsdp", None),
        ),
        check_vma=False,
    )
```
